32 devices in a mesh: tp: 2 (over x), ep: 16 (over z, y, core).
Axes of the slice: x: 2, y: 2, z: 4, core: 2. Of those that a mesh axis runs over, the one named last changes fastest.
Arguments:
- hidden_in: bfloat16 [256, 4096], P(('ep', 'tp')), may hold values from -6 to 6
- norm_gain: bfloat16 [4096], replicated, may hold values from 0.099609375 to 1.8984375
- expert_ids: int32 [256, 8], P('ep'), may hold values from 0 to 63, all different within a row; in each aligned block of 16 rows (0 to 15, 16 to 31, ...) at most 4 rows name the same one
- gate_weights: float32 [256, 8], P('ep'), may hold values from 0.05 to 0.35
- w_gate: bfloat16 [64, 4096, 1024], P('ep', None, 'tp'), may hold values from -0.09375 to 0.09375
- w_up: bfloat16 [64, 4096, 1024], P('ep', None, 'tp'), may hold values from -0.09375 to 0.09375
- w_down: bfloat16 [64, 1024, 4096], P('ep', None, 'tp'), may hold values from -0.1875 to 0.1875
Outputs:
- mixed: bfloat16 [256, 4096], P('ep', 'tp')
The draws below stay inside these ranges and needn't reach their ends.
Inputs may be any that keep to these rules, and one draw needn't show every extreme that they name: `expert_ids`: each row names 8 different experts. Tokens form groups of 16 consecutive rows; within one group no expert is named by more than 4 rows, and in every draw some expert is named by exactly 4 rows of some group.
All inputs are finite; a program needn't handle non-finite values.
Results may differ from the reference program's by a relative error of at most 0.0043.
Values may be sent and summed in bfloat16 or wider, within the bound.
No kernel may reach another device: no remote copies, remote signals or barrier semaphores. Data moves between devices by JAX's collectives and lax.ppermute only.
A program may use at most 128 MiB of HBM per device.

```python
import math
import jax
import jax.numpy as jnp
import numpy as np
from jax import lax

D = 4096
HID = 1024
EXPERTS = 64
TOP = 8
GROUP = 16
CAP = 4
TOKENS = 256
N_EP = 16


def level_of(rng, dims, shards, smallest, high):
    def one(axis_at, blocks):
        heights = jax.random.uniform(jax.random.fold_in(jax.random.fold_in(rng, 6), axis_at), (blocks,), jnp.float32, smallest / len(shards), high / len(shards))
        return jnp.repeat(jnp.exp(heights), dims[axis_at] // blocks).reshape((-1,) + (1,) * (len(dims) - axis_at - 1))

    loudness = one(*shards[0])
    for cut in shards[1:]:
        loudness = loudness * one(*cut)
    return loudness


def shared_out(own_key, own, number, rows, number_of, top, bound, slope):
    sequence = jax.random.permutation(own_key, number_of)
    crowded, ordinary = portions_of(number_of, rows * top, bound, slope, True), portions_of(number_of, rows * top, bound, slope, False)
    places = jnp.arange(number_of)

    def named(lengths, offset_by):
        used = int((lengths > 0).sum())
        fixed = max(1, used // 4)
        moved = fixed + (places - fixed + offset_by * (used - fixed)) % max(1, number_of - fixed)
        return jnp.zeros((number_of,), jnp.int32).at[sequence[jnp.where(places < fixed, places, moved)]].set(jnp.asarray(lengths, jnp.int32))

    lengths = jnp.where(number % 4 == 0, named(crowded, number // 4), named(ordinary, number - number // 4 - 1))
    mixed = jax.random.permutation(jax.random.fold_in(own, 3), number_of)
    source_of, sink = mixed[0:number_of // 2 * 2:2], mixed[1:number_of // 2 * 2:2]
    slack = jnp.minimum(lengths[source_of] - 1, bound - lengths[sink]) // 2
    slack = jnp.where((source_of == sequence[0]) | (sink == sequence[0]) | (lengths[sink] == 0), 0, jnp.maximum(slack, 0))
    moved = jax.random.randint(jax.random.fold_in(own, 4), (number_of // 2,), 0, 1 << 20) % (slack + 1)
    lengths = lengths.at[source_of].add(-moved).at[sink].add(moved)
    labels = jnp.searchsorted(jnp.cumsum(lengths), jnp.arange(rows * top), side="right").astype(jnp.int32)
    table = labels.reshape(top, rows).T
    table = table[jax.random.permutation(jax.random.fold_in(own, 1), rows)]
    offset_by = jax.random.randint(jax.random.fold_in(own, 2), (rows, 1), 0, top)
    return jnp.take_along_axis(table, (jnp.arange(top)[None, :] + offset_by) % top, axis=1)


def portions_of(number_of, total, bound, slope, full):
    loads = [(1 << 20) // math.isqrt(grade ** slope) + 1 for grade in range(1, number_of + 1)]
    largest = bound if full else min(bound, max(-(-total // number_of), total * loads[0] // sum(loads)))
    least = 1 if total - largest >= number_of - 1 else 0
    counts, rest = [largest] + [least] * (number_of - 1), total - largest - least * (number_of - 1)
    while rest > 0:
        free = [i for i in range(1, number_of) if counts[i] < largest] or [i for i in range(1, number_of) if counts[i] < bound]
        mass, remaining = sum([loads[i] for i in free]), rest
        for i in free:
            extra = min(bound - counts[i], max(1, remaining * loads[i] // mass), rest)
            counts[i] = counts[i] + extra
            rest = rest - extra
    return np.array(counts)


def scatter_about(rng, shape, spread, most, cuts=(), kind=jnp.bfloat16):
    gain = level_of(rng, shape, cuts, -0.22, 0.18) if cuts else 1.0
    result = jax.random.normal(rng, shape, jnp.float32) * spread * gain
    return jnp.minimum(jnp.maximum(result, -most), most).astype(kind)


def setup_inputs(seed: int = 0) -> dict:
    streams_of = jax.random.split(jax.random.key(seed), 8)
    hidden_in = scatter_about(streams_of[0], (TOKENS, D), 1.0, 6.0, ((0, 32),))
    norm_gain = jnp.clip(1.0 + 0.18 * jax.random.normal(streams_of[1], (D,), jnp.float32), 0.099609375, 1.8984375).astype(jnp.bfloat16)
    expert_ids_keys = jax.random.split(jax.random.fold_in(streams_of[2], 1), TOKENS // GROUP)
    expert_ids_turns = jax.random.permutation(jax.random.fold_in(streams_of[2], 3), TOKENS // GROUP)
    expert_ids = jax.vmap(lambda own, number: shared_out(jax.random.fold_in(streams_of[2], 2), own, number, GROUP, EXPERTS, TOP, CAP, 2))(expert_ids_keys, expert_ids_turns).reshape((TOKENS, TOP))
    gate_weights = jnp.clip(0.05 + 0.29999999 * jax.random.uniform(streams_of[3], (TOKENS, TOP), jnp.float32) ** level_of(streams_of[3], (TOKENS, TOP), ((0, 16),), -0.2, 0.2), 0.05, 0.35)
    w_gate = scatter_about(streams_of[4], (EXPERTS, D, HID), D ** -0.5, 0.09375, ((0, 16), (2, 2)))
    w_up = scatter_about(streams_of[5], (EXPERTS, D, HID), D ** -0.5, 0.09375, ((0, 16), (2, 2)))
    w_down = scatter_about(streams_of[6], (EXPERTS, HID, D), HID ** -0.5, 0.1875, ((0, 16), (2, 2)))
    return dict(hidden_in=hidden_in, norm_gain=norm_gain, expert_ids=expert_ids, gate_weights=gate_weights, w_gate=w_gate, w_up=w_up, w_down=w_down)


def reference(hidden_in, norm_gain, expert_ids, gate_weights, w_gate, w_up, w_down):
    values = hidden_in.astype(jnp.float32)
    scale = lax.rsqrt(lax.optimization_barrier(jnp.mean(values * values, axis=1, keepdims=True)) + 1e-06)
    normed = (values * scale * norm_gain.astype(jnp.float32)).astype(jnp.bfloat16)
    flat_ids = expert_ids.reshape(-1)
    flat_gates = gate_weights.reshape(-1)
    window = N_EP * CAP

    def one_expert(total, expert):
        live = flat_ids == expert
        picks = jnp.nonzero(live, size=window, fill_value=0)[0].astype(jnp.int32)
        valid = jnp.arange(window, dtype=jnp.int32) < jnp.sum(live.astype(jnp.int32))
        weights = jnp.where(valid, flat_gates[picks], jnp.zeros((), flat_gates.dtype))
        token_rows = (picks // TOP).astype(jnp.int32)
        rows = normed[token_rows]
        gate_act = jnp.dot(rows, w_gate[expert], preferred_element_type=jnp.float32)
        up_act = jnp.dot(rows, w_up[expert], preferred_element_type=jnp.float32)
        hidden = (jax.nn.silu(gate_act) * up_act).astype(jnp.bfloat16)
        expert_out = jnp.dot(hidden, w_down[expert], preferred_element_type=jnp.float32).astype(jnp.bfloat16)
        term = weights[:, None] * expert_out.astype(total.dtype)
        return (total.at[token_rows].add(term), None)
    start = jnp.zeros((TOKENS, D), jnp.float32)
    total, _ = lax.scan(one_expert, start, jnp.arange(EXPERTS, dtype=jnp.int32))
    return (values + total).astype(jnp.bfloat16)
```

```python
import jax
import jax.numpy as jnp
from jax import lax
from jax.sharding import PartitionSpec as P


def shards(hidden_in, norm_gain, expert_ids, gate_weights, w_gate, w_up, w_down):
    n_ep = lax.axis_size("ep")
    ep_pos = lax.axis_index("ep")
    tp_pos = lax.axis_index("tp")
    tok_dev, width = hidden_in.shape
    group, top = expert_ids.shape
    exp_loc, _, hid_part = w_gate.shape
    col_part = w_down.shape[2]
    experts = exp_loc * n_ep
    cap = max(2, 2 * top * group // experts)
    rows = cap * n_ep
    tokens = group * n_ep

    whole = lax.all_gather(hidden_in, ("ep", "tp"), axis=0, tiled=True)
    routing = jnp.concatenate([expert_ids.astype(jnp.float32), gate_weights], axis=1)
    routing = lax.all_gather(routing, "ep", axis=0, tiled=True)
    ids = routing[:, :top].astype(jnp.int32)
    weights = routing[:, top:]
    local = ep_pos * exp_loc + lax.broadcasted_iota(jnp.int32, (tokens, top, exp_loc), 2)
    match = ids[:, :, None] == local
    weight_of = jnp.sum(jnp.where(match, weights[:, :, None], 0.0), axis=1)
    hit = jnp.any(match, axis=1).astype(jnp.int32)
    position = jnp.cumsum(hit, axis=0) - hit
    place = jnp.where(hit > 0, position, -1).T
    pick = (place[:, None, :] == lax.broadcasted_iota(jnp.int32, (exp_loc, rows, tokens), 1))
    select = pick.astype(jnp.bfloat16)
    picked = jnp.einsum("ert,td->erd", select, whole, preferred_element_type=jnp.float32)
    scale = lax.rsqrt(jnp.mean(picked * picked, axis=2, keepdims=True) + 1e-06)
    normed = (picked * scale * norm_gain.astype(jnp.float32)).astype(jnp.bfloat16)
    gate_act = jnp.einsum("erd,edh->erh", normed, w_gate, preferred_element_type=jnp.float32)
    up_act = jnp.einsum("erd,edh->erh", normed, w_up, preferred_element_type=jnp.float32)
    hidden = (jax.nn.silu(gate_act) * up_act).astype(jnp.bfloat16)
    hidden = lax.all_gather(hidden, "tp", axis=2, tiled=True)
    outputs = jnp.einsum("erh,ehf->erf", hidden, w_down, preferred_element_type=jnp.float32)
    outputs = outputs.astype(jnp.bfloat16)
    spread = jnp.where(pick, weight_of.T[:, None, :], 0.0)
    high = spread.astype(jnp.bfloat16)
    rest = spread - high.astype(jnp.float32)
    low = rest.astype(jnp.bfloat16)
    partial = jnp.einsum("ert,erf->tf", high, outputs, preferred_element_type=jnp.float32)
    partial = partial + jnp.einsum("ert,erf->tf", low, outputs, preferred_element_type=jnp.float32)
    combined = lax.psum_scatter(partial.astype(jnp.bfloat16), "ep", scatter_dimension=0, tiled=True)
    residual = lax.dynamic_slice(whole, (ep_pos * group, tp_pos * col_part), (group, col_part))
    return (residual.astype(jnp.float32) + combined.astype(jnp.float32)).astype(jnp.bfloat16)


def solution(mesh):
    in_specs = (
        P(("ep", "tp"), None),
        P(),
        P("ep", None),
        P("ep", None),
        P("ep", None, "tp"),
        P("ep", None, "tp"),
        P("ep", None, "tp"),
    )
    out_specs = P("ep", "tp")
    return jax.shard_map(shards, mesh=mesh, in_specs=in_specs, out_specs=out_specs, check_vma=False)
```

```python
import jax
import jax.numpy as jnp
from jax import lax
from jax.sharding import PartitionSpec as P

LANES = 128


def factors_of(n):
    digits, stride = [], 1
    for _ in range(2):
        if n % 2 == 0 and n > 1:
            digits.append((stride, 2))
            stride, n = stride * 2, n // 2
    while n > 1:
        radix = next(r for r in (4, 3, 2, n) if n % r == 0)
        digits.append((stride, radix))
        stride, n = stride * radix, n // radix
    return digits


def shifted(x, axis, size, stride, radix, by):
    pairs = []
    for i in range(size):
        digit = i // stride % radix
        pairs.append((i, i + ((digit + by) % radix - digit) * stride))
    return lax.ppermute(x, axis, pairs)


def gathered(x, axis, size, stride, radix):
    return jnp.stack([x] + [shifted(x, axis, size, stride, radix, s) for s in range(1, radix)])


def scattered(x, axis, size, stride, radix):
    total = x[0].astype(jnp.float32)
    for s in range(1, radix):
        total = total + shifted(x[s], axis, size, stride, radix, radix - s).astype(jnp.float32)
    return total.astype(x.dtype)


def by_slots(hidden_in, norm_gain, expert_ids, gate_weights, w_gate, w_up, w_down):
    n_ep = lax.axis_size("ep")
    tp_pos = lax.axis_index("tp")
    tok_dev, width = hidden_in.shape
    group, top = expert_ids.shape
    exp_loc, _, hid_part = w_gate.shape
    col_part = w_down.shape[2]
    experts = exp_loc * n_ep
    cap = max(2, 2 * top * group // experts)
    values = hidden_in.astype(jnp.float32)
    scale = lax.rsqrt(jnp.mean(values * values, axis=1, keepdims=True) + 1e-06)
    normed = (values * scale * norm_gain.astype(jnp.float32)).astype(jnp.bfloat16)
    flat_ids = expert_ids.reshape(-1)
    pairs = flat_ids.shape[0]
    hits = (flat_ids[:, None] == lax.broadcasted_iota(jnp.int32, (pairs, experts), 1)).astype(
        jnp.int32
    )
    before = jnp.cumsum(hits, axis=0) - hits
    position = jnp.sum(before * hits, axis=1)
    slot_index = flat_ids * cap + position
    places = lax.broadcasted_iota(jnp.int32, (experts * cap, group, top), 0)
    dispatch_map = jnp.any(places == slot_index.reshape(group, top)[None], axis=2).astype(
        jnp.bfloat16
    )
    whole_norm, whole_input = (
        lax.all_gather(normed, "tp", axis=0, tiled=True),
        lax.all_gather(hidden_in, "tp", axis=0, tiled=True),
    )
    residual = lax.dynamic_slice_in_dim(whole_input, tp_pos * col_part, col_part, 1)
    packed = jnp.dot(dispatch_map, whole_norm, preferred_element_type=jnp.float32).astype(
        jnp.bfloat16
    )
    packed = packed.reshape(n_ep, exp_loc, cap, width)
    arrived = lax.all_to_all(packed, "ep", split_axis=0, concat_axis=0, tiled=True)
    gate_act = jnp.einsum("secd,edh->sech", arrived, w_gate, preferred_element_type=jnp.float32)
    up_act = jnp.einsum("secd,edh->sech", arrived, w_up, preferred_element_type=jnp.float32)
    hidden = (jax.nn.silu(gate_act) * up_act).astype(jnp.bfloat16)
    outputs = jnp.einsum(
        "sech,ehf->secf",
        lax.all_gather(hidden, "tp", axis=3, tiled=True),
        w_down,
        preferred_element_type=jnp.float32,
    )
    returned = lax.all_to_all(
        outputs.astype(jnp.bfloat16), "ep", split_axis=0, concat_axis=0, tiled=True
    )
    flat_back = returned.reshape(experts * cap, col_part)
    picked = flat_back[slot_index].reshape(group, top, col_part).astype(jnp.float32)
    combined = jnp.sum(picked * gate_weights[:, :, None], axis=1)
    return (residual.astype(jnp.float32) + combined).astype(jnp.bfloat16)


def by_tokens(hidden_in, norm_gain, expert_ids, gate_weights, w_gate, w_up, w_down):
    n_ep = lax.axis_size("ep")
    n_tp = lax.axis_size("tp")
    ep_pos = lax.axis_index("ep")
    tp_pos = lax.axis_index("tp")
    tok_dev, width = hidden_in.shape
    group, top = expert_ids.shape
    exp_loc, _, hid_part = w_gate.shape
    col_part = w_down.shape[2]
    experts = exp_loc * n_ep
    cap = max(2, 2 * top * group // experts)
    rows = cap * n_ep
    tokens = group * n_ep
    digits = factors_of(n_ep)
    fast, mid, slow = digits[0], digits[1:2], digits[2:]
    half = width // 2

    mine = lambda a: lax.dynamic_slice_in_dim(a, tp_pos * tok_dev, tok_dev, 0)
    w_own = mine(gate_weights)
    w_hi = w_own.astype(jnp.bfloat16)
    w_rest = w_own - w_hi.astype(jnp.float32)
    w_mid = w_rest.astype(jnp.bfloat16)
    w_lo = (w_rest - w_mid.astype(jnp.float32)).astype(jnp.bfloat16)
    blank = jnp.zeros((tok_dev, LANES - 4 * top), jnp.bfloat16)
    routing = [mine(expert_ids).astype(jnp.bfloat16), w_hi, w_mid, w_lo, blank]

    first = jnp.concatenate([hidden_in[:, :half]] + routing, axis=1)
    second = hidden_in[:, half:]
    for digit in reversed(slow):
        first = gathered(first, "ep", n_ep, *digit)
        second = gathered(second, "ep", n_ep, *digit)
    lead = [radix for _, radix in reversed(slow)]
    count = len(lead)
    along_tp = lambda a: gathered(a, "tp", n_tp, 1, n_tp)
    for digit in mid:
        first = gathered(first, "ep", n_ep, *digit)
    first = along_tp(first)
    second = along_tp(second)
    for digit in mid:
        second = gathered(second, "ep", n_ep, *digit)
    first = gathered(first, "ep", n_ep, *fast)
    second = gathered(second, "ep", n_ep, *fast)
    mids = [radix for _, radix in mid]
    slow_n = 1
    for r in lead:
        slow_n *= r
    mid_n = mids[0] if mids else 1
    first = first.reshape(fast[1], n_tp, mid_n, slow_n, tok_dev, -1).transpose(0, 2, 3, 1, 4, 5)
    second = second.reshape(fast[1], mid_n, n_tp, slow_n, tok_dev, -1).transpose(0, 1, 3, 2, 4, 5)
    whole = jnp.concatenate(
        [first[..., :half], second], axis=-1
    ).reshape(tokens, width)
    routing = first[..., half:].reshape(tokens, -1).astype(jnp.float32)
    ids = routing[:, :top].astype(jnp.int32)
    weights = routing[:, top : 2 * top] + (routing[:, 2 * top : 3 * top] + routing[:, 3 * top : 4 * top])

    local = ep_pos * exp_loc + lax.broadcasted_iota(jnp.int32, (tokens, top, exp_loc), 2)
    match = ids[:, :, None] == local
    weight_of = jnp.sum(jnp.where(match, weights[:, :, None], 0.0), axis=1)
    hit = jnp.any(match, axis=1)
    number = lax.broadcasted_iota(jnp.int32, (tokens, 1), 0)
    tp_of = (number // tok_dev % n_tp) * -1 + tp_pos + n_tp
    number = number + (tp_of % n_tp - number // tok_dev % n_tp) * tok_dev
    before = (number.reshape(1, tokens) < number).astype(jnp.bfloat16)
    position = jnp.dot(before, hit.astype(jnp.bfloat16), preferred_element_type=jnp.float32)
    place = jnp.where(hit, position.astype(jnp.int32), -1).T
    pick = place[:, None, :] == lax.broadcasted_iota(jnp.int32, (exp_loc, rows, tokens), 1)
    select = pick.astype(jnp.bfloat16)
    picked = jnp.einsum("ert,td->erd", select, whole, preferred_element_type=jnp.float32)
    scale = lax.rsqrt(jnp.mean(picked * picked, axis=2, keepdims=True) + 1e-06)
    normed = (picked * scale * norm_gain.astype(jnp.float32)).astype(jnp.bfloat16)
    parts = []
    for e in range(exp_loc):
        gate_act = jnp.dot(normed[e], w_gate[e], preferred_element_type=jnp.float32)
        up_act = jnp.dot(normed[e], w_up[e], preferred_element_type=jnp.float32)
        hidden = (jax.nn.silu(gate_act) * up_act).astype(jnp.bfloat16)
        around = gathered(hidden, "tp", n_tp, 1, n_tp)
        total = 0.0
        for s in range(n_tp):
            start = (tp_pos - s + n_tp) % n_tp * hid_part
            rows_of = lax.dynamic_slice_in_dim(w_down[e], start, hid_part, 0)
            total = total + jnp.dot(around[s], rows_of, preferred_element_type=jnp.float32)
        parts.append(total.astype(jnp.bfloat16))
    outputs = jnp.stack(parts)
    spread = jnp.where(pick, weight_of.T[:, None, :], 0.0)
    high = spread.astype(jnp.bfloat16)
    low = (spread - high.astype(jnp.float32)).astype(jnp.bfloat16)
    partial = jnp.einsum("ert,erf->tf", high, outputs, preferred_element_type=jnp.float32)
    partial = partial + jnp.einsum("ert,erf->tf", low, outputs, preferred_element_type=jnp.float32)
    total = partial.astype(jnp.bfloat16).reshape([fast[1]] + mids + lead + [group, col_part])
    total = scattered(total, "ep", n_ep, *fast)
    for digit in mid:
        total = scattered(total, "ep", n_ep, *digit)
    for digit in reversed(slow):
        total = scattered(total, "ep", n_ep, *digit)
    combined = total
    mine_rows = whole[:group]
    residual = lax.dynamic_slice_in_dim(mine_rows, tp_pos * col_part, col_part, 1)
    result = (residual.astype(jnp.float32) + combined.astype(jnp.float32)).astype(jnp.bfloat16)
    result = result.reshape(n_tp, tok_dev, col_part)
    order = (tp_pos - jnp.arange(n_tp)) % n_tp
    turned = [result[0]] * n_tp
    for j in range(n_tp):
        piece = result[0]
        for s in range(1, n_tp):
            piece = jnp.where(order[s] == j, result[s], piece)
        turned[j] = piece
    return jnp.concatenate(turned, axis=0)


def shards(hidden_in, norm_gain, expert_ids, gate_weights, w_gate, w_up, w_down):
    group, top = expert_ids.shape
    exp_loc = w_gate.shape[0]
    cap = max(2, 2 * top * group // (exp_loc * lax.axis_size("ep")))
    plan = by_tokens if exp_loc * cap >= group else by_slots
    return plan(hidden_in, norm_gain, expert_ids, gate_weights, w_gate, w_up, w_down)


def solution(mesh):
    in_specs = (
        P(("ep", "tp"), None),
        P(),
        P("ep", None),
        P("ep", None),
        P("ep", None, "tp"),
        P("ep", None, "tp"),
        P("ep", None, "tp"),
    )
    out_specs = P("ep", "tp")
    return jax.shard_map(shards, mesh=mesh, in_specs=in_specs, out_specs=out_specs, check_vma=False)
```

```python
import functools

import jax
import jax.numpy as jnp
from jax import lax
from jax.experimental import pallas as pl
from jax.experimental.pallas import tpu as pltpu
from jax.sharding import PartitionSpec as P

LANES = 128


def factors_of(n):
    digits, stride = [], 1
    for _ in range(2):
        if n % 2 == 0 and n > 1:
            digits.append((stride, 2))
            stride, n = stride * 2, n // 2
    while n > 1:
        radix = next(r for r in (4, 3, 2, n) if n % r == 0)
        digits.append((stride, radix))
        stride, n = stride * radix, n // radix
    return digits


def shifted(x, axis, size, stride, radix, by):
    pairs = []
    for i in range(size):
        digit = i // stride % radix
        pairs.append((i, i + ((digit + by) % radix - digit) * stride))
    return lax.ppermute(x, axis, pairs)


def arrivals(x, axis, size, stride, radix):
    return [x] + [shifted(x, axis, size, stride, radix, s) for s in range(1, radix)]


def gathered(x, axis, size, stride, radix):
    return jnp.stack(arrivals(x, axis, size, stride, radix))


def scattered(x, axis, size, stride, radix):
    total = x[0].astype(jnp.float32)
    for s in range(1, radix):
        total = total + shifted(x[s], axis, size, stride, radix, radix - s).astype(jnp.float32)
    return total.astype(x.dtype)


def up_copies(up_ref, held, sems, start, count):
    copies = [pltpu.make_async_copy(up_ref.at[start + i], held.at[i], sems.at[i]) for i in range(count)]
    for copy in copies:
        copy.start()
    return copies


def swiglu(x_ref, gate_ref, held, hidden_ref, copies, start):
    for i, copy in enumerate(copies):
        x = x_ref[start + i]
        gate_act = jnp.dot(x, gate_ref[start + i], preferred_element_type=jnp.float32)
        copy.wait()
        up_act = jnp.dot(x, held[i], preferred_element_type=jnp.float32)
        hidden_ref[i] = (gate_act / (1.0 + jnp.exp(-gate_act)) * up_act).astype(jnp.bfloat16)


def select_kernel(dims, pos_ref, gain_ref, *refs):
    n_fast, n_mid, n_tp, slow_n, tok_dev, top, exp_loc, rows, half = dims
    first, second = refs[:n_fast], refs[n_fast : 2 * n_fast]
    gate_ref, up_ref, normed_ref, high_ref, low_ref, hidden_ref, held, sems = refs[2 * n_fast :]
    count = hidden_ref.shape[0]
    copies = up_copies(up_ref, held, sems, 0, count)
    tp_pos, base = pos_ref[0], pos_ref[1]
    run = slow_n * tok_dev
    tokens = n_fast * n_mid * n_tp * run
    routing = jnp.concatenate([ref[:, half:] for ref in first], axis=0).astype(jnp.float32)
    ids = routing[:, :top]
    weights = routing[:, top : 2 * top] + (
        routing[:, 2 * top : 3 * top] + routing[:, 3 * top : 4 * top]
    )

    def number(shape, dim):
        at = lax.broadcasted_iota(jnp.int32, shape, dim)
        tp_at = lax.rem(lax.div(at, n_mid * run), n_tp)
        return at + (lax.rem(tp_pos - tp_at + n_tp, n_tp) - tp_at) * (n_mid * run)

    before = number((tokens, tokens), 1) < number((tokens, tokens), 0)
    match = [ids == (base + e).astype(jnp.float32) for e in range(exp_loc)]
    hits = [jnp.sum(m.astype(jnp.float32), axis=1, keepdims=True) for m in match]
    gates = [jnp.sum(jnp.where(m, weights, 0.0), axis=1, keepdims=True) for m in match]
    lane = lax.broadcasted_iota(jnp.int32, (tokens, 128), 1)
    hit = functools.reduce(
        lambda a, e: jnp.where(lane == e, hits[e], a), range(exp_loc), jnp.zeros((tokens, 128), jnp.float32)
    )
    position = jnp.dot(
        before.astype(jnp.float32).astype(jnp.bfloat16),
        hit.astype(jnp.bfloat16),
        preferred_element_type=jnp.float32,
    )
    slot = lax.broadcasted_iota(jnp.int32, (tokens, rows), 1).astype(jnp.float32)
    picks, spreads = [], []
    for e in range(exp_loc):
        place = jnp.where(hits[e] > 0, position[:, e : e + 1], -1.0)
        pick = slot == place
        picks.append(pick.astype(jnp.float32))
        spreads.append(jnp.where(pick, gates[e], 0.0))
    spread = jnp.concatenate(spreads, axis=1)
    blocks = []
    for f in range(n_fast):
        for m in range(n_mid):
            for s in range(slow_n):
                for t in range(n_tp):
                    start = (((f * n_tp + t) * n_mid + m) * slow_n + s) * tok_dev
                    blocks.append(spread[start : start + tok_dev])
    spread = jnp.concatenate(blocks, axis=0)
    high = spread.astype(jnp.bfloat16)
    high_ref[...] = high
    low_ref[...] = (spread - high.astype(jnp.float32)).astype(jnp.bfloat16)

    part = n_mid * n_tp * run
    gain = gain_ref[...].astype(jnp.float32)
    dims_of = (((0,), (0,)), ((), ()))
    for e in range(exp_loc):
        left, right = [], []
        for f in range(n_fast):
            pick = picks[e][f * part : (f + 1) * part]
            turned = jnp.concatenate(
                [
                    pick[(t * n_mid + m) * run : (t * n_mid + m + 1) * run]
                    for m in range(n_mid)
                    for t in range(n_tp)
                ],
                axis=0,
            )
            left.append(
                lax.dot_general(
                    pick.astype(jnp.bfloat16), first[f][:, :half], dims_of, preferred_element_type=jnp.float32
                )
            )
            right.append(
                lax.dot_general(
                    turned.astype(jnp.bfloat16), second[f][...], dims_of, preferred_element_type=jnp.float32
                )
            )
        left, right = sum(left[1:], left[0]), sum(right[1:], right[0])
        squares = jnp.sum(left * left, axis=1, keepdims=True) + jnp.sum(right * right, axis=1, keepdims=True)
        scale = lax.rsqrt(squares / (2 * half) + 1e-06)
        normed_ref[e, :, :half] = (right * scale * gain[:, :half]).astype(jnp.bfloat16)
        normed_ref[e, :, half:] = (left * scale * gain[:, half:]).astype(jnp.bfloat16)
    swiglu(normed_ref, gate_ref, held, hidden_ref, copies, 0)


def up_kernel(start, x_ref, gate_ref, up_ref, hidden_ref, held, sems):
    copies = up_copies(up_ref, held, sems, start, hidden_ref.shape[0])
    swiglu(x_ref, gate_ref, held, hidden_ref, copies, start)


def down_kernel(n_tp, splits, pos_ref, high_ref, low_ref, *refs):
    pieces = refs[: len(splits) * n_tp]
    down_ref, partial_ref, out_ref = refs[len(splits) * n_tp :]
    _, rows, hid_part = pieces[0].shape
    tp_pos = pos_ref[0]
    done = 0
    for g, count in enumerate(splits):
        for i in range(count):
            total = 0.0
            for s in range(n_tp):
                begin = pl.multiple_of(lax.rem(tp_pos - s + n_tp, n_tp) * hid_part, hid_part)
                total = total + jnp.dot(
                    pieces[g * n_tp + s][i],
                    down_ref[done, pl.ds(begin, hid_part), :],
                    preferred_element_type=jnp.float32,
                )
            out_ref[done * rows : (done + 1) * rows] = total.astype(jnp.bfloat16)
            done += 1
    out = out_ref[...]
    partial = jnp.dot(high_ref[...], out, preferred_element_type=jnp.float32)
    partial = partial + jnp.dot(low_ref[...], out, preferred_element_type=jnp.float32)
    partial_ref[...] = partial.astype(jnp.bfloat16)


def load_kernel(src_ref, dst_ref, sems):
    copies = [
        pltpu.make_async_copy(src_ref.at[i], dst_ref.at[i], sems.at[i]) for i in range(src_ref.shape[0])
    ]
    for copy in copies:
        copy.start()
    for copy in copies:
        copy.wait()


def loaded(array):
    return pl.pallas_call(
        load_kernel,
        out_shape=pltpu.VMEM(array.shape, array.dtype),
        in_specs=[pl.BlockSpec(memory_space=pltpu.HBM)],
        out_specs=pl.BlockSpec(memory_space=pltpu.VMEM),
        scratch_shapes=[pltpu.SemaphoreType.DMA((array.shape[0],))],
        compiler_params=pltpu.CompilerParams(vmem_limit_bytes=1 << 20),
        cost_estimate=pl.CostEstimate(
            flops=0, bytes_accessed=2 * array.size, transcendentals=0
        ),
    )(pltpu.with_memory_space_constraint(array, pltpu.HBM))


VMEM = pl.BlockSpec(memory_space=pltpu.VMEM)
SMEM = pl.BlockSpec(memory_space=pltpu.SMEM)


HBM = pl.BlockSpec(memory_space=pltpu.HBM)


def local_call(kernel, shapes, operands, far=(), scratch=(), limit=16 << 20, flops=0, moved=0):
    specs = [HBM if i in far else SMEM if a.dtype == jnp.int32 else VMEM for i, a in enumerate(operands)]
    operands = [
        pltpu.with_memory_space_constraint(a, pltpu.HBM) if i in far else a for i, a in enumerate(operands)
    ]
    return pl.pallas_call(
        kernel,
        out_shape=shapes,
        in_specs=specs,
        out_specs=jax.tree.map(lambda _: VMEM, shapes),
        scratch_shapes=list(scratch),
        compiler_params=pltpu.CompilerParams(vmem_limit_bytes=limit),
        cost_estimate=pl.CostEstimate(flops=flops, bytes_accessed=moved, transcendentals=0),
    )(*operands)


def by_tokens(hidden_in, norm_gain, expert_ids, gate_weights, w_gate, w_up, w_down):
    n_ep = lax.axis_size("ep")
    n_tp = lax.axis_size("tp")
    ep_pos = lax.axis_index("ep")
    tp_pos = lax.axis_index("tp")
    tok_dev, width = hidden_in.shape
    group, top = expert_ids.shape
    exp_loc, _, hid_part = w_gate.shape
    col_part = w_down.shape[2]
    experts = exp_loc * n_ep
    cap = max(2, 2 * top * group // experts)
    rows = cap * n_ep
    tokens = group * n_ep
    digits = factors_of(n_ep)
    fast, mid, slow = digits[0], digits[1:2], digits[2:]
    half = width // 2
    slow_n = n_ep
    for _, radix in [fast] + mid:
        slow_n //= radix
    n_fast, n_mid = fast[1], mid[0][1] if mid else 1

    mine = lambda a: lax.dynamic_slice_in_dim(a, tp_pos * tok_dev, tok_dev, 0)
    w_own = mine(gate_weights)
    w_hi = w_own.astype(jnp.bfloat16)
    w_rest = w_own - w_hi.astype(jnp.float32)
    w_mid = w_rest.astype(jnp.bfloat16)
    w_lo = (w_rest - w_mid.astype(jnp.float32)).astype(jnp.bfloat16)
    blank = jnp.zeros((tok_dev, LANES - 4 * top), jnp.bfloat16)
    routing = [mine(expert_ids).astype(jnp.bfloat16), w_hi, w_mid, w_lo, blank]

    whole = jnp.concatenate([hidden_in] + routing, axis=1)
    for digit in reversed(slow):
        whole = gathered(whole, "ep", n_ep, *digit)
    whole = whole.reshape(slow_n * tok_dev, -1)
    second, first = whole[:, :half], whole[:, half:]
    along_tp = lambda a: gathered(a, "tp", n_tp, 1, n_tp)
    for digit in mid:
        first = gathered(first, "ep", n_ep, *digit)
    second = along_tp(second)
    first = along_tp(first)
    for digit in mid:
        second = gathered(second, "ep", n_ep, *digit)
    first = arrivals(first.reshape(tokens // n_fast, -1), "ep", n_ep, *fast)
    second = arrivals(second.reshape(tokens // n_fast, -1), "ep", n_ep, *fast)

    position = jnp.stack([tp_pos, ep_pos * exp_loc])
    gain = norm_gain.reshape(1, width)
    dims = (n_fast, n_mid, n_tp, slow_n, tok_dev, top, exp_loc, rows, half)
    bf16 = functools.partial(jax.ShapeDtypeStruct, dtype=jnp.bfloat16)
    slots = exp_loc * rows
    splits = [exp_loc - exp_loc // 2, exp_loc // 2] if exp_loc > 1 else [1]
    gate_w = loaded(w_gate)
    held = lambda count: [
        pltpu.VMEM((count,) + w_up.shape[1:], jnp.bfloat16),
        pltpu.SemaphoreType.DMA((count,)),
    ]
    operands = [position, gain] + first + second + [gate_w, w_up]
    normed, high, low, hidden = local_call(
        functools.partial(select_kernel, dims),
        [
            bf16((exp_loc, rows, width)),
            bf16((tokens, slots)),
            bf16((tokens, slots)),
            bf16((splits[0], rows, hid_part)),
        ],
        operands,
        far=[len(operands) - 1],
        scratch=held(splits[0]),
        flops=2 * slots * tokens * width,
        moved=4 * splits[0] * width * hid_part,
    )
    pieces, start = arrivals(hidden, "tp", n_tp, 1, n_tp), splits[0]
    for count in splits[1:]:
        hidden = local_call(
            functools.partial(up_kernel, start),
            bf16((count, rows, hid_part)),
            [normed, gate_w, w_up],
            far=[2],
            scratch=held(count),
            flops=4 * count * rows * width * hid_part,
            moved=4 * count * width * hid_part,
        )
        pieces += arrivals(hidden, "tp", n_tp, 1, n_tp)
        start += count
    partial = local_call(
        functools.partial(down_kernel, n_tp, splits),
        bf16((tokens, col_part)),
        [position, high, low] + pieces + [w_down],
        scratch=[pltpu.VMEM((slots, col_part), jnp.bfloat16)],
        flops=2 * slots * n_tp * hid_part * col_part,
        moved=2 * exp_loc * n_tp * hid_part * col_part,
    )
    total = partial.reshape(n_fast, -1, group, col_part)
    total = scattered(total, "ep", n_ep, *fast)
    for digit in mid:
        total = scattered(total.reshape(digit[1], -1, group, col_part), "ep", n_ep, *digit)
    for digit in reversed(slow):
        total = scattered(total.reshape(digit[1], -1, group, col_part), "ep", n_ep, *digit)
    combined = total.reshape(n_tp, tok_dev, col_part)
    column = lambda a, at: lax.dynamic_slice_in_dim(a, at, col_part, 1)
    near = first[0].reshape(n_tp, -1, first[0].shape[1])[:, :tok_dev]
    far = second[0].reshape(n_mid, n_tp, -1, half)[0, :, :tok_dev]
    own = jnp.concatenate([far, near[:, :, :half]], axis=2)
    residual = lax.dynamic_slice_in_dim(own, tp_pos * col_part, col_part, 2)
    result = (residual.astype(jnp.float32) + combined.astype(jnp.float32)).astype(jnp.bfloat16)
    order = [lax.rem(tp_pos - s + n_tp, n_tp) for s in range(n_tp)]
    turned = []
    for j in range(n_tp):
        piece = result[0]
        for s in range(1, n_tp):
            piece = jnp.where(order[s] == j, result[s], piece)
        turned.append(piece)
    return jnp.concatenate(turned, axis=0)


def by_slots(hidden_in, norm_gain, expert_ids, gate_weights, w_gate, w_up, w_down):
    n_ep = lax.axis_size("ep")
    tp_pos = lax.axis_index("tp")
    tok_dev, width = hidden_in.shape
    group, top = expert_ids.shape
    exp_loc, _, hid_part = w_gate.shape
    col_part = w_down.shape[2]
    experts = exp_loc * n_ep
    cap = max(2, 2 * top * group // experts)
    values = hidden_in.astype(jnp.float32)
    scale = lax.rsqrt(jnp.mean(values * values, axis=1, keepdims=True) + 1e-06)
    normed = (values * scale * norm_gain.astype(jnp.float32)).astype(jnp.bfloat16)
    flat_ids = expert_ids.reshape(-1)
    pairs = flat_ids.shape[0]
    hits = (flat_ids[:, None] == lax.broadcasted_iota(jnp.int32, (pairs, experts), 1)).astype(
        jnp.int32
    )
    before = jnp.cumsum(hits, axis=0) - hits
    position = jnp.sum(before * hits, axis=1)
    slot_index = flat_ids * cap + position
    places = lax.broadcasted_iota(jnp.int32, (experts * cap, group, top), 0)
    dispatch_map = jnp.any(places == slot_index.reshape(group, top)[None], axis=2).astype(
        jnp.bfloat16
    )
    whole_norm, whole_input = (
        lax.all_gather(normed, "tp", axis=0, tiled=True),
        lax.all_gather(hidden_in, "tp", axis=0, tiled=True),
    )
    residual = lax.dynamic_slice_in_dim(whole_input, tp_pos * col_part, col_part, 1)
    packed = jnp.dot(dispatch_map, whole_norm, preferred_element_type=jnp.float32).astype(
        jnp.bfloat16
    )
    packed = packed.reshape(n_ep, exp_loc, cap, width)
    arrived = lax.all_to_all(packed, "ep", split_axis=0, concat_axis=0, tiled=True)
    gate_act = jnp.einsum("secd,edh->sech", arrived, w_gate, preferred_element_type=jnp.float32)
    up_act = jnp.einsum("secd,edh->sech", arrived, w_up, preferred_element_type=jnp.float32)
    hidden = (jax.nn.silu(gate_act) * up_act).astype(jnp.bfloat16)
    outputs = jnp.einsum(
        "sech,ehf->secf",
        lax.all_gather(hidden, "tp", axis=3, tiled=True),
        w_down,
        preferred_element_type=jnp.float32,
    )
    returned = lax.all_to_all(
        outputs.astype(jnp.bfloat16), "ep", split_axis=0, concat_axis=0, tiled=True
    )
    flat_back = returned.reshape(experts * cap, col_part)
    picked = flat_back[slot_index].reshape(group, top, col_part).astype(jnp.float32)
    combined = jnp.sum(picked * gate_weights[:, :, None], axis=1)
    return (residual.astype(jnp.float32) + combined).astype(jnp.bfloat16)


def shards(hidden_in, norm_gain, expert_ids, gate_weights, w_gate, w_up, w_down):
    group, top = expert_ids.shape
    exp_loc = w_gate.shape[0]
    cap = max(2, 2 * top * group // (exp_loc * lax.axis_size("ep")))
    plan = by_tokens if exp_loc * cap >= group else by_slots
    return plan(hidden_in, norm_gain, expert_ids, gate_weights, w_gate, w_up, w_down)


def solution(mesh):
    in_specs = (
        P(("ep", "tp"), None),
        P(),
        P("ep", None),
        P("ep", None),
        P("ep", None, "tp"),
        P("ep", None, "tp"),
        P("ep", None, "tp"),
    )
    out_specs = P("ep", "tp")
    return jax.shard_map(shards, mesh=mesh, in_specs=in_specs, out_specs=out_specs, check_vma=False)
```

```python
import functools

import jax
import jax.numpy as jnp
from jax import lax
from jax.experimental import pallas as pl
from jax.experimental.pallas import tpu as pltpu
from jax.sharding import PartitionSpec as P

LANES = 128


def factors_of(n):
    digits, stride = [], 1
    for _ in range(2):
        if n % 2 == 0 and n > 1:
            digits.append((stride, 2))
            stride, n = stride * 2, n // 2
    while n > 1:
        radix = next(r for r in (4, 3, 2, n) if n % r == 0)
        digits.append((stride, radix))
        stride, n = stride * radix, n // radix
    return digits


def shifted(x, axis, size, stride, radix, by):
    pairs = []
    for i in range(size):
        digit = i // stride % radix
        pairs.append((i, i + ((digit + by) % radix - digit) * stride))
    return lax.ppermute(x, axis, pairs)


def arrivals(x, axis, size, stride, radix):
    return [x] + [shifted(x, axis, size, stride, radix, s) for s in range(1, radix)]


def gathered(x, axis, size, stride, radix):
    return jnp.stack(arrivals(x, axis, size, stride, radix))


def scattered(x, axis, size, stride, radix):
    total = x[0].astype(jnp.float32)
    for s in range(1, radix):
        total = total + shifted(x[s], axis, size, stride, radix, radix - s).astype(jnp.float32)
    return total.astype(x.dtype)


def pack_kernel(top, pos_ref, ids_ref, weights_ref, values_ref, message_ref, ids, weights, sems):
    tok_dev, width = values_ref.shape
    copies = [
        pltpu.make_async_copy(ids_ref, ids, sems.at[0]),
        pltpu.make_async_copy(weights_ref, weights, sems.at[1]),
        pltpu.make_async_copy(values_ref, message_ref.at[:, pl.ds(0, width)], sems.at[2]),
    ]
    for copy in copies:
        copy.start()
    copies[0].wait()
    copies[1].wait()
    group = ids.shape[1]
    high = weights[...].astype(jnp.bfloat16).astype(jnp.float32)
    rest = weights[...] - high
    mid = rest.astype(jnp.bfloat16).astype(jnp.float32)
    terms = [ids[...].astype(jnp.float32), high, mid, rest - mid]
    terms.append(jnp.zeros((LANES - 4 * top, group), jnp.float32))
    table = jnp.concatenate(terms, axis=0).astype(jnp.bfloat16)
    own = lax.broadcasted_iota(jnp.int32, (tok_dev, group), 0) + pos_ref[0] * tok_dev
    own = (own == lax.broadcasted_iota(jnp.int32, (tok_dev, group), 1)).astype(jnp.float32)
    routing = lax.dot_general(
        own.astype(jnp.bfloat16), table, (((1,), (1,)), ((), ())), preferred_element_type=jnp.float32
    )
    message_ref[:, width:] = routing.astype(jnp.bfloat16)
    copies[2].wait()


def split_kernel(half, *refs):
    pieces, (first_ref, second_ref, token_ref) = refs[:-3], refs[-3:]
    pieces = [ref for ref in pieces if ref.shape[1] > 2 * half]
    whole = jnp.concatenate([ref[...].astype(jnp.float32) for ref in pieces], axis=0).astype(jnp.bfloat16)
    second_ref[...] = whole[:, :half]
    first_ref[...] = whole[:, half:]
    token_ref[...] = jnp.zeros_like(token_ref)


def join_kernel(count, *refs):
    out_ref, token_ref = refs[-2:]
    rows = refs[0].shape[0]
    for i, ref in enumerate(refs[:count]):
        out_ref[i * rows : (i + 1) * rows] = ref[...]
    token_ref[...] = jnp.zeros_like(token_ref)


def load_kernel(start, src_ref, *refs):
    dst_ref, token_ref, sems = refs[-3:]
    copies = load_copies(src_ref, dst_ref, sems, start)
    token_ref[...] = jnp.zeros_like(token_ref)
    for copy in copies:
        copy.wait()


def load_copies(src_ref, dst_ref, sems, start):
    copies = [
        pltpu.make_async_copy(src_ref.at[start + i], dst_ref.at[i], sems.at[i]) for i in range(dst_ref.shape[0])
    ]
    for copy in copies:
        copy.start()
    return copies


def swiglu(normed_ref, gate_ref, up_ref, hidden_ref, start):
    for i in range(hidden_ref.shape[0]):
        x = normed_ref[start + i]
        gate_act = jnp.dot(x, gate_ref[i], preferred_element_type=jnp.float32)
        up_act = jnp.dot(x, up_ref[i], preferred_element_type=jnp.float32)
        hidden_ref[i] = (gate_act / (1.0 + jnp.exp(-gate_act)) * up_act).astype(jnp.bfloat16)


def select_kernel(dims, pos_ref, gain_ref, *refs):
    n_fast, n_mid, n_tp, slow_n, tok_dev, top, exp_loc, rows, half = dims
    first, second = refs[:n_fast], refs[n_fast : 2 * n_fast]
    gate_ref, up_ref, far_ref, hidden_ref, near_ref, normed_ref, high_ref, low_ref, sems = refs[2 * n_fast :]
    copies = load_copies(far_ref, near_ref, sems, 0)
    tp_pos, base = pos_ref[0], pos_ref[1]
    run = slow_n * tok_dev
    tokens = n_fast * n_mid * n_tp * run
    routing = jnp.concatenate([ref[:, half:] for ref in first], axis=0).astype(jnp.float32)
    ids = routing[:, :top]
    weights = routing[:, top : 2 * top] + (
        routing[:, 2 * top : 3 * top] + routing[:, 3 * top : 4 * top]
    )

    def number(shape, dim):
        at = lax.broadcasted_iota(jnp.int32, shape, dim)
        tp_at = lax.rem(lax.div(at, n_mid * run), n_tp)
        return at + (lax.rem(tp_pos - tp_at + n_tp, n_tp) - tp_at) * (n_mid * run)

    before = number((tokens, tokens), 1) < number((tokens, tokens), 0)
    match = [ids == (base + e).astype(jnp.float32) for e in range(exp_loc)]
    hits = [jnp.sum(m.astype(jnp.float32), axis=1, keepdims=True) for m in match]
    gates = [jnp.sum(jnp.where(m, weights, 0.0), axis=1, keepdims=True) for m in match]
    lane = lax.broadcasted_iota(jnp.int32, (tokens, LANES), 1)
    hit = functools.reduce(
        lambda a, e: jnp.where(lane == e, hits[e], a),
        range(exp_loc),
        jnp.zeros((tokens, LANES), jnp.float32),
    )
    position = jnp.dot(
        before.astype(jnp.float32).astype(jnp.bfloat16),
        hit.astype(jnp.bfloat16),
        preferred_element_type=jnp.float32,
    )
    slot = lax.broadcasted_iota(jnp.int32, (tokens, rows), 1).astype(jnp.float32)
    picks, spreads = [], []
    for e in range(exp_loc):
        place = jnp.where(hits[e] > 0, position[:, e : e + 1], -1.0)
        pick = slot == place
        picks.append(pick.astype(jnp.float32))
        spreads.append(jnp.where(pick, gates[e], 0.0))
    spread = jnp.concatenate(spreads, axis=1)
    blocks = []
    for f in range(n_fast):
        for m in range(n_mid):
            for s in range(slow_n):
                for t in range(n_tp):
                    start = (((f * n_tp + t) * n_mid + m) * slow_n + s) * tok_dev
                    blocks.append(spread[start : start + tok_dev])
    spread = jnp.concatenate(blocks, axis=0)
    high = spread.astype(jnp.bfloat16)
    high_ref[...] = high
    low_ref[...] = (spread - high.astype(jnp.float32)).astype(jnp.bfloat16)

    part = n_mid * n_tp * run
    gain = gain_ref[...].astype(jnp.float32)
    dims_of = (((0,), (0,)), ((), ()))
    for e in range(exp_loc):
        left, right = [], []
        for f in range(n_fast):
            pick = picks[e][f * part : (f + 1) * part]
            turned = jnp.concatenate(
                [
                    pick[(t * n_mid + m) * run : (t * n_mid + m + 1) * run]
                    for m in range(n_mid)
                    for t in range(n_tp)
                ],
                axis=0,
            )
            left.append(
                lax.dot_general(
                    turned.astype(jnp.bfloat16), second[f][...], dims_of, preferred_element_type=jnp.float32
                )
            )
            right.append(
                lax.dot_general(
                    pick.astype(jnp.bfloat16), first[f][:, :half], dims_of, preferred_element_type=jnp.float32
                )
            )
        left, right = sum(left[1:], left[0]), sum(right[1:], right[0])
        squares = jnp.sum(left * left, axis=1, keepdims=True) + jnp.sum(right * right, axis=1, keepdims=True)
        scale = lax.rsqrt(squares / (2 * half) + 1e-06)
        normed_ref[e, :, :half] = (left * scale * gain[:, :half]).astype(jnp.bfloat16)
        normed_ref[e, :, half:] = (right * scale * gain[:, half:]).astype(jnp.bfloat16)
    swiglu(normed_ref, gate_ref, up_ref, hidden_ref, 0)
    for copy in copies:
        copy.wait()


def up_kernel(start, normed_ref, gate_ref, up_ref, far_ref, hidden_ref, near_ref, sems):
    copies = load_copies(far_ref, near_ref, sems, start)
    swiglu(normed_ref, gate_ref, up_ref, hidden_ref, start)
    for copy in copies:
        copy.wait()


def lower(n_tp, tp_pos, pieces, down_ref, i):
    hid_part = pieces[0].shape[2]
    total = 0.0
    for s in range(n_tp):
        begin = pl.multiple_of(lax.rem(tp_pos - s + n_tp, n_tp) * hid_part, hid_part)
        total = total + jnp.dot(
            pieces[s][i], down_ref[i, pl.ds(begin, hid_part), :], preferred_element_type=jnp.float32
        )
    return total.astype(jnp.bfloat16)


def down_kernel(n_tp, pos_ref, *refs):
    pieces, (down_ref, out_ref) = refs[:n_tp], refs[n_tp:]
    rows = pieces[0].shape[1]
    for i in range(down_ref.shape[0]):
        out_ref[i * rows : (i + 1) * rows] = lower(n_tp, pos_ref[0], pieces, down_ref, i)


def mix_kernel(n_tp, pos_ref, high_ref, low_ref, *refs):
    pieces, down_ref, done, (partial_ref, out_ref) = refs[:n_tp], refs[n_tp], refs[n_tp + 1 : -2], refs[-2:]
    rows, at = pieces[0].shape[1], 0
    for ref in done:
        out_ref[at : at + ref.shape[0]] = ref[...]
        at += ref.shape[0]
    for i in range(down_ref.shape[0]):
        out_ref[at : at + rows] = lower(n_tp, pos_ref[0], pieces, down_ref, i)
        at += rows
    out = out_ref[...]
    partial = jnp.dot(high_ref[...], out, preferred_element_type=jnp.float32)
    partial = partial + jnp.dot(low_ref[...], out, preferred_element_type=jnp.float32)
    partial_ref[...] = partial.astype(jnp.bfloat16)


VMEM = pl.BlockSpec(memory_space=pltpu.VMEM)
SMEM = pl.BlockSpec(memory_space=pltpu.SMEM)
HBM = pl.BlockSpec(memory_space=pltpu.HBM)
KEPT = pltpu.VMEM


def local_call(kernel, shapes, operands, far=(), scratch=(), limit=8 << 20, flops=0, moved=0):
    specs, given = [], []
    for i, a in enumerate(operands):
        if i in far:
            specs.append(HBM)
            given.append(pltpu.with_memory_space_constraint(a, pltpu.HBM))
        else:
            specs.append(SMEM if a.dtype == jnp.int32 else VMEM)
            given.append(a)
    return pl.pallas_call(
        kernel,
        out_shape=shapes,
        in_specs=specs,
        out_specs=[VMEM] * len(shapes),
        scratch_shapes=list(scratch),
        compiler_params=pltpu.CompilerParams(vmem_limit_bytes=limit),
        cost_estimate=pl.CostEstimate(flops=flops, bytes_accessed=moved, transcendentals=0),
    )(*given)


TOKEN = jax.ShapeDtypeStruct((8, LANES), jnp.float32)


def loaded(array, start, count, after):
    size = (count,) + array.shape[1:]
    return local_call(
        functools.partial(load_kernel, start),
        [KEPT(size, array.dtype), TOKEN],
        [array] + after,
        far=[0],
        scratch=[pltpu.SemaphoreType.DMA((count,))],
        limit=1 << 20,
        moved=2 * count * array.size // array.shape[0],
    )


def joined(pieces, after):
    rows, columns = pieces[0].shape
    return local_call(
        functools.partial(join_kernel, len(pieces)),
        [jax.ShapeDtypeStruct((len(pieces) * rows, columns), pieces[0].dtype), TOKEN],
        list(pieces) + after,
        limit=4 << 20,
        moved=4 * len(pieces) * rows * columns,
    )


def by_tokens(hidden_in, norm_gain, expert_ids, gate_weights, w_gate, w_up, w_down):
    n_ep = lax.axis_size("ep")
    n_tp = lax.axis_size("tp")
    ep_pos = lax.axis_index("ep")
    tp_pos = lax.axis_index("tp")
    tok_dev, width = hidden_in.shape
    group, top = expert_ids.shape
    exp_loc, _, hid_part = w_gate.shape
    col_part = w_down.shape[2]
    experts = exp_loc * n_ep
    cap = max(2, 2 * top * group // experts)
    rows = cap * n_ep
    tokens = group * n_ep
    digits = factors_of(n_ep)
    fast, mid, slow = digits[0], digits[1:2], digits[2:]
    half = width // 2
    slow_n = n_ep
    for _, radix in [fast] + mid:
        slow_n //= radix
    n_fast, n_mid = fast[1], mid[0][1] if mid else 1

    bf16 = functools.partial(jax.ShapeDtypeStruct, dtype=jnp.bfloat16)
    slots = exp_loc * rows
    counts = [exp_loc - exp_loc // 2, exp_loc // 2] if exp_loc > 1 else [1]
    lead = counts[0]
    tail = counts[1:]
    gain = norm_gain.reshape(1, width)
    position = jnp.stack([tp_pos, ep_pos * exp_loc])
    (message,) = local_call(
        functools.partial(pack_kernel, top),
        [bf16((tok_dev, width + LANES))],
        [position, expert_ids.T, gate_weights.T, hidden_in],
        far=[1, 2, 3],
        scratch=[
            pltpu.VMEM((top, group), jnp.int32),
            pltpu.VMEM((top, group), jnp.float32),
            pltpu.SemaphoreType.DMA((3,)),
        ],
        limit=4 << 20,
    )
    around = [message]
    for digit in reversed(slow):
        around = [a for piece in around for a in arrivals(piece, "ep", n_ep, *digit)]
    gate_lead, sign = loaded(w_gate, 0, lead, [gain])
    first, second, sign = local_call(
        functools.partial(split_kernel, half),
        [bf16((slow_n * tok_dev, width + LANES - half)), bf16((slow_n * tok_dev, half)), TOKEN],
        around + [sign],
        limit=4 << 20,
    )
    up_lead, up_sign = loaded(w_up, 0, lead, [sign])
    along_tp = lambda a: arrivals(a, "tp", n_tp, 1, n_tp)
    along_mid = lambda a: arrivals(a, "ep", n_ep, *mid[0]) if mid else [a]
    first, second = along_mid(first), along_tp(second)
    first, sign = joined(first, [up_sign])
    second, _ = joined(second, [])
    gate_tail = [loaded(w_gate, lead, count, [sign]) for count in tail]
    first, second = along_tp(first), along_mid(second)
    first, sign = joined(first, [sign for _, sign in gate_tail])
    second, _ = joined(second, [])
    up_tail = [loaded(w_up, lead, count, [sign]) for count in tail]
    first = arrivals(first, "ep", n_ep, *fast)
    second = arrivals(second, "ep", n_ep, *fast)

    dims = (n_fast, n_mid, n_tp, slow_n, tok_dev, top, exp_loc, rows, half)
    down_size = lambda count: KEPT((count,) + w_down.shape[1:], w_down.dtype)
    operands = [position, gain] + first + second + [gate_lead, up_lead, w_down]
    hidden, down_lead, normed, high, low = local_call(
        functools.partial(select_kernel, dims),
        [
            bf16((lead, rows, hid_part)),
            down_size(lead),
            bf16((exp_loc, rows, width)),
            bf16((tokens, slots)),
            bf16((tokens, slots)),
        ],
        operands,
        far=[len(operands) - 1],
        scratch=[pltpu.SemaphoreType.DMA((lead,))],
        flops=2 * slots * tokens * width + 4 * lead * rows * width * hid_part,
        moved=4 * lead * width * hid_part,
    )
    pieces = along_tp(hidden)
    partial_of = lambda pieces, down, done: local_call(
        functools.partial(mix_kernel, n_tp),
        [bf16((tokens, col_part))],
        [position, high, low] + pieces + [down] + done,
        scratch=[pltpu.VMEM((slots, col_part), jnp.bfloat16)],
        flops=2 * slots * n_tp * hid_part * col_part,
        moved=2 * exp_loc * n_tp * hid_part * col_part,
    )[0]
    if not tail:
        partial = partial_of(pieces, down_lead, [])
    else:
        hidden, down_tail = local_call(
            functools.partial(up_kernel, lead),
            [bf16((tail[0], rows, hid_part)), down_size(tail[0])],
            [normed, gate_tail[0][0], up_tail[0][0], w_down],
            far=[3],
            scratch=[pltpu.SemaphoreType.DMA((tail[0],))],
            flops=4 * tail[0] * rows * width * hid_part,
            moved=4 * tail[0] * width * hid_part,
        )
        late = along_tp(hidden)
        (done,) = local_call(
            functools.partial(down_kernel, n_tp),
            [bf16((lead * rows, col_part))],
            [position] + pieces + [down_lead],
            flops=2 * lead * rows * n_tp * hid_part * col_part,
            moved=2 * lead * n_tp * hid_part * col_part,
        )
        partial = partial_of(late, down_tail, [done])
    total = partial.reshape(n_fast, -1, group, col_part)
    total = scattered(total, "ep", n_ep, *fast)
    for digit in mid:
        total = scattered(total.reshape(digit[1], -1, group, col_part), "ep", n_ep, *digit)
    for digit in reversed(slow):
        total = scattered(total.reshape(digit[1], -1, group, col_part), "ep", n_ep, *digit)
    combined = total.reshape(n_tp, tok_dev, col_part)
    column = lambda a, at: lax.dynamic_slice_in_dim(a, at, col_part, 1)
    right = first[0].reshape(n_tp, -1, first[0].shape[1])[:, :tok_dev, :half]
    left = second[0].reshape(n_mid, n_tp, -1, half)[0, :, :tok_dev]
    own = jnp.concatenate([left, right], axis=2)
    residual = lax.dynamic_slice_in_dim(own, tp_pos * col_part, col_part, 2)
    result = (residual.astype(jnp.float32) + combined.astype(jnp.float32)).astype(jnp.bfloat16)
    order = [lax.rem(tp_pos - s + n_tp, n_tp) for s in range(n_tp)]
    turned = []
    for j in range(n_tp):
        piece = result[0]
        for s in range(1, n_tp):
            piece = jnp.where(order[s] == j, result[s], piece)
        turned.append(piece)
    return jnp.concatenate(turned, axis=0)


def by_slots(hidden_in, norm_gain, expert_ids, gate_weights, w_gate, w_up, w_down):
    n_ep = lax.axis_size("ep")
    tp_pos = lax.axis_index("tp")
    tok_dev, width = hidden_in.shape
    group, top = expert_ids.shape
    exp_loc, _, hid_part = w_gate.shape
    col_part = w_down.shape[2]
    experts = exp_loc * n_ep
    cap = max(2, 2 * top * group // experts)
    values = hidden_in.astype(jnp.float32)
    scale = lax.rsqrt(jnp.mean(values * values, axis=1, keepdims=True) + 1e-06)
    normed = (values * scale * norm_gain.astype(jnp.float32)).astype(jnp.bfloat16)
    flat_ids = expert_ids.reshape(-1)
    pairs = flat_ids.shape[0]
    hits = (flat_ids[:, None] == lax.broadcasted_iota(jnp.int32, (pairs, experts), 1)).astype(
        jnp.int32
    )
    before = jnp.cumsum(hits, axis=0) - hits
    position = jnp.sum(before * hits, axis=1)
    slot_index = flat_ids * cap + position
    places = lax.broadcasted_iota(jnp.int32, (experts * cap, group, top), 0)
    dispatch_map = jnp.any(places == slot_index.reshape(group, top)[None], axis=2).astype(
        jnp.bfloat16
    )
    whole_norm, whole_input = (
        lax.all_gather(normed, "tp", axis=0, tiled=True),
        lax.all_gather(hidden_in, "tp", axis=0, tiled=True),
    )
    residual = lax.dynamic_slice_in_dim(whole_input, tp_pos * col_part, col_part, 1)
    packed = jnp.dot(dispatch_map, whole_norm, preferred_element_type=jnp.float32).astype(
        jnp.bfloat16
    )
    packed = packed.reshape(n_ep, exp_loc, cap, width)
    arrived = lax.all_to_all(packed, "ep", split_axis=0, concat_axis=0, tiled=True)
    gate_act = jnp.einsum("secd,edh->sech", arrived, w_gate, preferred_element_type=jnp.float32)
    up_act = jnp.einsum("secd,edh->sech", arrived, w_up, preferred_element_type=jnp.float32)
    hidden = (jax.nn.silu(gate_act) * up_act).astype(jnp.bfloat16)
    outputs = jnp.einsum(
        "sech,ehf->secf",
        lax.all_gather(hidden, "tp", axis=3, tiled=True),
        w_down,
        preferred_element_type=jnp.float32,
    )
    returned = lax.all_to_all(
        outputs.astype(jnp.bfloat16), "ep", split_axis=0, concat_axis=0, tiled=True
    )
    flat_back = returned.reshape(experts * cap, col_part)
    picked = flat_back[slot_index].reshape(group, top, col_part).astype(jnp.float32)
    combined = jnp.sum(picked * gate_weights[:, :, None], axis=1)
    return (residual.astype(jnp.float32) + combined).astype(jnp.bfloat16)


def shards(hidden_in, norm_gain, expert_ids, gate_weights, w_gate, w_up, w_down):
    group, top = expert_ids.shape
    exp_loc = w_gate.shape[0]
    cap = max(2, 2 * top * group // (exp_loc * lax.axis_size("ep")))
    plan = by_tokens if exp_loc * cap >= group else by_slots
    return plan(hidden_in, norm_gain, expert_ids, gate_weights, w_gate, w_up, w_down)


def solution(mesh):
    in_specs = (
        P(("ep", "tp"), None),
        P(),
        P("ep", None),
        P("ep", None),
        P("ep", None, "tp"),
        P("ep", None, "tp"),
        P("ep", None, "tp"),
    )
    out_specs = P("ep", "tp")
    return jax.shard_map(shards, mesh=mesh, in_specs=in_specs, out_specs=out_specs, check_vma=False)
```

```python
import functools

import jax
import jax.numpy as jnp
from jax import lax
from jax.experimental import pallas as pl
from jax.experimental.pallas import tpu as pltpu
from jax.sharding import PartitionSpec as P

LANES = 128


def factors_of(n):
    digits, stride = [], 1
    for _ in range(2):
        if n % 2 == 0 and n > 1:
            digits.append((stride, 2))
            stride, n = stride * 2, n // 2
    while n > 1:
        radix = next(r for r in (4, 3, 2, n) if n % r == 0)
        digits.append((stride, radix))
        stride, n = stride * radix, n // radix
    return digits


def shifted(x, axis, size, stride, radix, by):
    pairs = []
    for i in range(size):
        digit = i // stride % radix
        pairs.append((i, i + ((digit + by) % radix - digit) * stride))
    return lax.ppermute(x, axis, pairs)


def arrivals(x, axis, size, stride, radix):
    return [x] + [shifted(x, axis, size, stride, radix, s) for s in range(1, radix)]


def gathered(x, axis, size, stride, radix):
    return jnp.stack(arrivals(x, axis, size, stride, radix))


def scattered(x, axis, size, stride, radix):
    total = x[0].astype(jnp.float32)
    for s in range(1, radix):
        total = total + shifted(x[s], axis, size, stride, radix, radix - s).astype(jnp.float32)
    return total.astype(x.dtype)


def pack_kernel(top, pos_ref, ids_ref, weights_ref, values_ref, message_ref, ids, weights, sems):
    tok_dev, width = values_ref.shape
    copies = [
        pltpu.make_async_copy(ids_ref, ids, sems.at[0]),
        pltpu.make_async_copy(weights_ref, weights, sems.at[1]),
        pltpu.make_async_copy(values_ref, message_ref.at[:, pl.ds(0, width)], sems.at[2]),
    ]
    for copy in copies:
        copy.start()
    copies[0].wait()
    copies[1].wait()
    group = ids.shape[1]
    high = weights[...].astype(jnp.bfloat16).astype(jnp.float32)
    rest = weights[...] - high
    mid = rest.astype(jnp.bfloat16).astype(jnp.float32)
    terms = [ids[...].astype(jnp.float32), high, mid, rest - mid]
    terms.append(jnp.zeros((LANES - 4 * top, group), jnp.float32))
    table = jnp.concatenate(terms, axis=0).astype(jnp.bfloat16)
    own = lax.broadcasted_iota(jnp.int32, (tok_dev, group), 0) + pos_ref[0] * tok_dev
    own = (own == lax.broadcasted_iota(jnp.int32, (tok_dev, group), 1)).astype(jnp.float32)
    routing = lax.dot_general(
        own.astype(jnp.bfloat16), table, (((1,), (1,)), ((), ())), preferred_element_type=jnp.float32
    )
    message_ref[:, width:] = routing.astype(jnp.bfloat16)
    copies[2].wait()


def split_kernel(half, *refs):
    pieces, (first_ref, second_ref, token_ref) = refs[:-3], refs[-3:]
    pieces = [ref for ref in pieces if ref.shape[1] > 2 * half]
    whole = jnp.concatenate([ref[...].astype(jnp.float32) for ref in pieces], axis=0).astype(jnp.bfloat16)
    second_ref[...] = whole[:, :half]
    first_ref[...] = whole[:, half:]
    token_ref[...] = jnp.zeros_like(token_ref)


def join_kernel(count, *refs):
    out_ref, token_ref = refs[-2:]
    rows = refs[0].shape[0]
    for i, ref in enumerate(refs[:count]):
        out_ref[i * rows : (i + 1) * rows] = ref[...]
    token_ref[...] = jnp.zeros_like(token_ref)


def load_kernel(start, src_ref, *refs):
    dst_ref, token_ref, sems = refs[-3:]
    copies = load_copies(src_ref, dst_ref, sems, start)
    token_ref[...] = jnp.zeros_like(token_ref)
    for copy in copies:
        copy.wait()


def load_copies(src_ref, dst_ref, sems, start):
    copies = [
        pltpu.make_async_copy(src_ref.at[start + i], dst_ref.at[i], sems.at[i]) for i in range(dst_ref.shape[0])
    ]
    for copy in copies:
        copy.start()
    return copies


def swiglu(normed_ref, gate_ref, up_ref, hidden_ref, start):
    for i in range(hidden_ref.shape[0]):
        x = normed_ref[start + i]
        gate_act = jnp.dot(x, gate_ref[i], preferred_element_type=jnp.float32)
        up_act = jnp.dot(x, up_ref[i], preferred_element_type=jnp.float32)
        hidden_ref[i] = (gate_act / (1.0 + jnp.exp(-gate_act)) * up_act).astype(jnp.bfloat16)


def select_kernel(dims, pos_ref, gain_ref, *refs):
    n_fast, n_mid, n_tp, slow_n, tok_dev, top, exp_loc, rows, half = dims
    first, second = refs[:n_fast], refs[n_fast : 2 * n_fast]
    (gate_ref, up_ref, gate_far, up_far, hidden_ref, normed_ref, high_ref, low_ref, gate_near, up_near, sems) = refs[
        2 * n_fast :
    ]
    lead = gate_ref.shape[0]
    copies = load_copies(gate_far, gate_near, sems.at[0], lead) + load_copies(up_far, up_near, sems.at[1], lead)
    tp_pos, base = pos_ref[0], pos_ref[1]
    run = slow_n * tok_dev
    tokens = n_fast * n_mid * n_tp * run
    routing = jnp.concatenate([ref[:, half:] for ref in first], axis=0).astype(jnp.float32)
    ids = routing[:, :top]
    weights = routing[:, top : 2 * top] + (
        routing[:, 2 * top : 3 * top] + routing[:, 3 * top : 4 * top]
    )

    def number(shape, dim):
        at = lax.broadcasted_iota(jnp.int32, shape, dim)
        tp_at = lax.rem(lax.div(at, n_mid * run), n_tp)
        return at + (lax.rem(tp_pos - tp_at + n_tp, n_tp) - tp_at) * (n_mid * run)

    before = number((tokens, tokens), 1) < number((tokens, tokens), 0)
    match = [ids == (base + e).astype(jnp.float32) for e in range(exp_loc)]
    hits = [jnp.sum(m.astype(jnp.float32), axis=1, keepdims=True) for m in match]
    gates = [jnp.sum(jnp.where(m, weights, 0.0), axis=1, keepdims=True) for m in match]
    lane = lax.broadcasted_iota(jnp.int32, (tokens, LANES), 1)
    hit = functools.reduce(
        lambda a, e: jnp.where(lane == e, hits[e], a),
        range(exp_loc),
        jnp.zeros((tokens, LANES), jnp.float32),
    )
    position = jnp.dot(
        before.astype(jnp.float32).astype(jnp.bfloat16),
        hit.astype(jnp.bfloat16),
        preferred_element_type=jnp.float32,
    )
    slot = lax.broadcasted_iota(jnp.int32, (tokens, rows), 1).astype(jnp.float32)
    picks, spreads = [], []
    for e in range(exp_loc):
        place = jnp.where(hits[e] > 0, position[:, e : e + 1], -1.0)
        pick = slot == place
        picks.append(pick.astype(jnp.float32))
        spreads.append(jnp.where(pick, gates[e], 0.0))
    spread = jnp.concatenate(spreads, axis=1)
    blocks = []
    for f in range(n_fast):
        for m in range(n_mid):
            for s in range(slow_n):
                for t in range(n_tp):
                    start = (((f * n_tp + t) * n_mid + m) * slow_n + s) * tok_dev
                    blocks.append(spread[start : start + tok_dev])
    spread = jnp.concatenate(blocks, axis=0)
    high = spread.astype(jnp.bfloat16)
    high_ref[...] = high
    low_ref[...] = (spread - high.astype(jnp.float32)).astype(jnp.bfloat16)

    part = n_mid * n_tp * run
    gain = gain_ref[...].astype(jnp.float32)
    dims_of = (((0,), (0,)), ((), ()))
    for e in range(exp_loc):
        left, right = [], []
        for f in range(n_fast):
            pick = picks[e][f * part : (f + 1) * part]
            turned = jnp.concatenate(
                [
                    pick[(t * n_mid + m) * run : (t * n_mid + m + 1) * run]
                    for m in range(n_mid)
                    for t in range(n_tp)
                ],
                axis=0,
            )
            left.append(
                lax.dot_general(
                    turned.astype(jnp.bfloat16), second[f][...], dims_of, preferred_element_type=jnp.float32
                )
            )
            right.append(
                lax.dot_general(
                    pick.astype(jnp.bfloat16), first[f][:, :half], dims_of, preferred_element_type=jnp.float32
                )
            )
        left, right = sum(left[1:], left[0]), sum(right[1:], right[0])
        squares = jnp.sum(left * left, axis=1, keepdims=True) + jnp.sum(right * right, axis=1, keepdims=True)
        scale = lax.rsqrt(squares / (2 * half) + 1e-06)
        normed_ref[e, :, :half] = (left * scale * gain[:, :half]).astype(jnp.bfloat16)
        normed_ref[e, :, half:] = (right * scale * gain[:, half:]).astype(jnp.bfloat16)
    swiglu(normed_ref, gate_ref, up_ref, hidden_ref, 0)
    for copy in copies:
        copy.wait()


def up_kernel(start, normed_ref, gate_ref, up_ref, far_ref, hidden_ref, near_ref, sems):
    copies = load_copies(far_ref, near_ref, sems, 0)
    swiglu(normed_ref, gate_ref, up_ref, hidden_ref, start)
    for copy in copies:
        copy.wait()


def lower(n_tp, tp_pos, pieces, down_ref, i):
    hid_part = pieces[0].shape[2]
    total = 0.0
    for s in range(n_tp):
        begin = pl.multiple_of(lax.rem(tp_pos - s + n_tp, n_tp) * hid_part, hid_part)
        total = total + jnp.dot(
            pieces[s][i], down_ref[i, pl.ds(begin, hid_part), :], preferred_element_type=jnp.float32
        )
    return total.astype(jnp.bfloat16)


def down_kernel(n_tp, pos_ref, *refs):
    pieces, (down_ref, far_ref, out_ref, near_ref, sems) = refs[:n_tp], refs[n_tp:]
    rows = pieces[0].shape[1]
    copies = load_copies(far_ref, near_ref, sems, down_ref.shape[0])
    for i in range(down_ref.shape[0]):
        out_ref[i * rows : (i + 1) * rows] = lower(n_tp, pos_ref[0], pieces, down_ref, i)
    for copy in copies:
        copy.wait()


def mix_kernel(n_tp, pos_ref, high_ref, low_ref, *refs):
    pieces, down_ref, done, (partial_ref, out_ref) = refs[:n_tp], refs[n_tp], refs[n_tp + 1 : -2], refs[-2:]
    rows, at = pieces[0].shape[1], 0
    for ref in done:
        out_ref[at : at + ref.shape[0]] = ref[...]
        at += ref.shape[0]
    for i in range(down_ref.shape[0]):
        out_ref[at : at + rows] = lower(n_tp, pos_ref[0], pieces, down_ref, i)
        at += rows
    out = out_ref[...]
    partial = jnp.dot(high_ref[...], out, preferred_element_type=jnp.float32)
    partial = partial + jnp.dot(low_ref[...], out, preferred_element_type=jnp.float32)
    partial_ref[...] = partial.astype(jnp.bfloat16)


VMEM = pl.BlockSpec(memory_space=pltpu.VMEM)
SMEM = pl.BlockSpec(memory_space=pltpu.SMEM)
HBM = pl.BlockSpec(memory_space=pltpu.HBM)
KEPT = pltpu.VMEM


def local_call(kernel, shapes, operands, far=(), scratch=(), limit=8 << 20, flops=0, moved=0):
    specs, given = [], []
    for i, a in enumerate(operands):
        if i in far:
            specs.append(HBM)
            given.append(pltpu.with_memory_space_constraint(a, pltpu.HBM))
        else:
            specs.append(SMEM if a.dtype == jnp.int32 else VMEM)
            given.append(a)
    return pl.pallas_call(
        kernel,
        out_shape=shapes,
        in_specs=specs,
        out_specs=[VMEM] * len(shapes),
        scratch_shapes=list(scratch),
        compiler_params=pltpu.CompilerParams(vmem_limit_bytes=limit),
        cost_estimate=pl.CostEstimate(flops=flops, bytes_accessed=moved, transcendentals=0),
    )(*given)


TOKEN = jax.ShapeDtypeStruct((8, LANES), jnp.float32)


def loaded(array, start, count, after):
    size = (count,) + array.shape[1:]
    return local_call(
        functools.partial(load_kernel, start),
        [KEPT(size, array.dtype), TOKEN],
        [array] + after,
        far=[0],
        scratch=[pltpu.SemaphoreType.DMA((count,))],
        limit=1 << 20,
        moved=2 * count * array.size // array.shape[0],
    )


def joined(pieces, after):
    rows, columns = pieces[0].shape
    return local_call(
        functools.partial(join_kernel, len(pieces)),
        [jax.ShapeDtypeStruct((len(pieces) * rows, columns), pieces[0].dtype), TOKEN],
        list(pieces) + after,
        limit=4 << 20,
        moved=4 * len(pieces) * rows * columns,
    )


def by_tokens(hidden_in, norm_gain, expert_ids, gate_weights, w_gate, w_up, w_down):
    n_ep = lax.axis_size("ep")
    n_tp = lax.axis_size("tp")
    ep_pos = lax.axis_index("ep")
    tp_pos = lax.axis_index("tp")
    tok_dev, width = hidden_in.shape
    group, top = expert_ids.shape
    exp_loc, _, hid_part = w_gate.shape
    col_part = w_down.shape[2]
    experts = exp_loc * n_ep
    cap = max(2, 2 * top * group // experts)
    rows = cap * n_ep
    tokens = group * n_ep
    digits = factors_of(n_ep)
    fast, mid, slow = digits[0], digits[1:2], digits[2:]
    half = width // 2
    slow_n = n_ep
    for _, radix in [fast] + mid:
        slow_n //= radix
    n_fast, n_mid = fast[1], mid[0][1] if mid else 1

    bf16 = functools.partial(jax.ShapeDtypeStruct, dtype=jnp.bfloat16)
    slots = exp_loc * rows
    counts = [exp_loc - exp_loc // 2, exp_loc // 2] if exp_loc > 1 else [1]
    lead = counts[0]
    tail = counts[1:]
    gain = norm_gain.reshape(1, width)
    position = jnp.stack([tp_pos, ep_pos * exp_loc])
    (message,) = local_call(
        functools.partial(pack_kernel, top),
        [bf16((tok_dev, width + LANES))],
        [position, expert_ids.T, gate_weights.T, hidden_in],
        far=[1, 2, 3],
        scratch=[
            pltpu.VMEM((top, group), jnp.int32),
            pltpu.VMEM((top, group), jnp.float32),
            pltpu.SemaphoreType.DMA((3,)),
        ],
        limit=4 << 20,
    )
    around = [message]
    for digit in reversed(slow):
        around = [a for piece in around for a in arrivals(piece, "ep", n_ep, *digit)]
    gate_lead, sign = loaded(w_gate, 0, lead, [gain])
    first, second, sign = local_call(
        functools.partial(split_kernel, half),
        [bf16((slow_n * tok_dev, width + LANES - half)), bf16((slow_n * tok_dev, half)), TOKEN],
        around + [sign],
        limit=4 << 20,
    )
    along_tp = lambda a: arrivals(a, "tp", n_tp, 1, n_tp)
    along_mid = lambda a: arrivals(a, "ep", n_ep, *mid[0]) if mid else [a]
    first, second = along_mid(first), along_tp(second)
    first, join_sign = joined(first, [])
    second, _ = joined(second, [])
    up_lead, up_sign = loaded(w_up, 0, lead, [join_sign])
    first, second = along_tp(first), along_mid(second)
    first, _ = joined(first, [up_sign])
    second, _ = joined(second, [])
    first = arrivals(first, "ep", n_ep, *fast)
    second = arrivals(second, "ep", n_ep, *fast)

    dims = (n_fast, n_mid, n_tp, slow_n, tok_dev, top, exp_loc, rows, half)
    down_size = lambda count: KEPT((count,) + w_down.shape[1:], w_down.dtype)
    operands = [position, gain] + first + second + [gate_lead, up_lead, w_gate, w_up]
    up_size = lambda array: KEPT((exp_loc - lead,) + array.shape[1:], array.dtype)
    hidden, normed, high, low, gate_tail, up_tail = local_call(
        functools.partial(select_kernel, dims),
        [
            bf16((lead, rows, hid_part)),
            bf16((exp_loc, rows, width)),
            bf16((tokens, slots)),
            bf16((tokens, slots)),
            up_size(w_gate),
            up_size(w_up),
        ],
        operands,
        far=[len(operands) - 2, len(operands) - 1],
        scratch=[pltpu.SemaphoreType.DMA((2, exp_loc - lead))],
        flops=2 * slots * tokens * width + 4 * lead * rows * width * hid_part,
        moved=4 * lead * width * hid_part,
    )
    pieces = along_tp(hidden)
    partial_of = lambda pieces, down, done: local_call(
        functools.partial(mix_kernel, n_tp),
        [bf16((tokens, col_part))],
        [position, high, low] + pieces + [down] + done,
        scratch=[pltpu.VMEM((slots, col_part), jnp.bfloat16)],
        flops=2 * slots * n_tp * hid_part * col_part,
        moved=2 * exp_loc * n_tp * hid_part * col_part,
    )[0]
    if not tail:
        partial = partial_of(pieces, loaded(w_down, 0, lead, [])[0], [])
    else:
        hidden, down_lead = local_call(
            functools.partial(up_kernel, lead),
            [bf16((tail[0], rows, hid_part)), down_size(lead)],
            [normed, gate_tail, up_tail, w_down],
            far=[3],
            scratch=[pltpu.SemaphoreType.DMA((lead,))],
            flops=4 * tail[0] * rows * width * hid_part,
            moved=4 * tail[0] * width * hid_part,
        )
        late = along_tp(hidden)
        done, down_tail = local_call(
            functools.partial(down_kernel, n_tp),
            [bf16((lead * rows, col_part)), down_size(tail[0])],
            [position] + pieces + [down_lead, w_down],
            far=[len(pieces) + 2],
            scratch=[pltpu.SemaphoreType.DMA((tail[0],))],
            flops=2 * lead * rows * n_tp * hid_part * col_part,
            moved=2 * lead * n_tp * hid_part * col_part,
        )
        partial = partial_of(late, down_tail, [done])
    total = partial.reshape(n_fast, -1, group, col_part)
    total = scattered(total, "ep", n_ep, *fast)
    for digit in mid:
        total = scattered(total.reshape(digit[1], -1, group, col_part), "ep", n_ep, *digit)
    for digit in reversed(slow):
        total = scattered(total.reshape(digit[1], -1, group, col_part), "ep", n_ep, *digit)
    combined = total.reshape(n_tp, tok_dev, col_part)
    column = lambda a, at: lax.dynamic_slice_in_dim(a, at, col_part, 1)
    right = first[0].reshape(n_tp, -1, first[0].shape[1])[:, :tok_dev, :half]
    left = second[0].reshape(n_mid, n_tp, -1, half)[0, :, :tok_dev]
    own = jnp.concatenate([left, right], axis=2)
    residual = lax.dynamic_slice_in_dim(own, tp_pos * col_part, col_part, 2)
    result = (residual.astype(jnp.float32) + combined.astype(jnp.float32)).astype(jnp.bfloat16)
    order = [lax.rem(tp_pos - s + n_tp, n_tp) for s in range(n_tp)]
    turned = []
    for j in range(n_tp):
        piece = result[0]
        for s in range(1, n_tp):
            piece = jnp.where(order[s] == j, result[s], piece)
        turned.append(piece)
    return jnp.concatenate(turned, axis=0)


def by_slots(hidden_in, norm_gain, expert_ids, gate_weights, w_gate, w_up, w_down):
    n_ep = lax.axis_size("ep")
    tp_pos = lax.axis_index("tp")
    tok_dev, width = hidden_in.shape
    group, top = expert_ids.shape
    exp_loc, _, hid_part = w_gate.shape
    col_part = w_down.shape[2]
    experts = exp_loc * n_ep
    cap = max(2, 2 * top * group // experts)
    values = hidden_in.astype(jnp.float32)
    scale = lax.rsqrt(jnp.mean(values * values, axis=1, keepdims=True) + 1e-06)
    normed = (values * scale * norm_gain.astype(jnp.float32)).astype(jnp.bfloat16)
    flat_ids = expert_ids.reshape(-1)
    pairs = flat_ids.shape[0]
    hits = (flat_ids[:, None] == lax.broadcasted_iota(jnp.int32, (pairs, experts), 1)).astype(
        jnp.int32
    )
    before = jnp.cumsum(hits, axis=0) - hits
    position = jnp.sum(before * hits, axis=1)
    slot_index = flat_ids * cap + position
    places = lax.broadcasted_iota(jnp.int32, (experts * cap, group, top), 0)
    dispatch_map = jnp.any(places == slot_index.reshape(group, top)[None], axis=2).astype(
        jnp.bfloat16
    )
    whole_norm, whole_input = (
        lax.all_gather(normed, "tp", axis=0, tiled=True),
        lax.all_gather(hidden_in, "tp", axis=0, tiled=True),
    )
    residual = lax.dynamic_slice_in_dim(whole_input, tp_pos * col_part, col_part, 1)
    packed = jnp.dot(dispatch_map, whole_norm, preferred_element_type=jnp.float32).astype(
        jnp.bfloat16
    )
    packed = packed.reshape(n_ep, exp_loc, cap, width)
    arrived = lax.all_to_all(packed, "ep", split_axis=0, concat_axis=0, tiled=True)
    gate_act = jnp.einsum("secd,edh->sech", arrived, w_gate, preferred_element_type=jnp.float32)
    up_act = jnp.einsum("secd,edh->sech", arrived, w_up, preferred_element_type=jnp.float32)
    hidden = (jax.nn.silu(gate_act) * up_act).astype(jnp.bfloat16)
    outputs = jnp.einsum(
        "sech,ehf->secf",
        lax.all_gather(hidden, "tp", axis=3, tiled=True),
        w_down,
        preferred_element_type=jnp.float32,
    )
    returned = lax.all_to_all(
        outputs.astype(jnp.bfloat16), "ep", split_axis=0, concat_axis=0, tiled=True
    )
    flat_back = returned.reshape(experts * cap, col_part)
    picked = flat_back[slot_index].reshape(group, top, col_part).astype(jnp.float32)
    combined = jnp.sum(picked * gate_weights[:, :, None], axis=1)
    return (residual.astype(jnp.float32) + combined).astype(jnp.bfloat16)


def shards(hidden_in, norm_gain, expert_ids, gate_weights, w_gate, w_up, w_down):
    group, top = expert_ids.shape
    exp_loc = w_gate.shape[0]
    cap = max(2, 2 * top * group // (exp_loc * lax.axis_size("ep")))
    plan = by_tokens if exp_loc > 1 and exp_loc * cap >= group else by_slots
    return plan(hidden_in, norm_gain, expert_ids, gate_weights, w_gate, w_up, w_down)


def solution(mesh):
    in_specs = (
        P(("ep", "tp"), None),
        P(),
        P("ep", None),
        P("ep", None),
        P("ep", None, "tp"),
        P("ep", None, "tp"),
        P("ep", None, "tp"),
    )
    out_specs = P("ep", "tp")
    return jax.shard_map(shards, mesh=mesh, in_specs=in_specs, out_specs=out_specs, check_vma=False)
```

```python
import functools

import jax
import jax.numpy as jnp
from jax import lax
from jax.experimental import pallas as pl
from jax.experimental.pallas import tpu as pltpu
from jax.sharding import PartitionSpec as P

LANES = 128


def factors_of(n):
    digits, stride = [], 1
    for _ in range(2):
        if n % 2 == 0 and n > 1:
            digits.append((stride, 2))
            stride, n = stride * 2, n // 2
    while n > 1:
        radix = next(r for r in (4, 3, 2, n) if n % r == 0)
        digits.append((stride, radix))
        stride, n = stride * radix, n // radix
    return digits


def shifted(x, axis, size, stride, radix, by):
    pairs = []
    for i in range(size):
        digit = i // stride % radix
        pairs.append((i, i + ((digit + by) % radix - digit) * stride))
    return lax.ppermute(x, axis, pairs)


def arrivals(x, axis, size, stride, radix):
    return [x] + [shifted(x, axis, size, stride, radix, s) for s in range(1, radix)]


def gathered(x, axis, size, stride, radix):
    return jnp.stack(arrivals(x, axis, size, stride, radix))


def scattered(x, axis, size, stride, radix):
    total = x[0].astype(jnp.float32)
    for s in range(1, radix):
        total = total + shifted(x[s], axis, size, stride, radix, radix - s).astype(jnp.float32)
    return total.astype(x.dtype)


def pack_kernel(top, pos_ref, ids_ref, weights_ref, values_ref, message_ref, ids, weights, sems):
    tok_dev, width = values_ref.shape
    copies = [
        pltpu.make_async_copy(ids_ref, ids, sems.at[0]),
        pltpu.make_async_copy(weights_ref, weights, sems.at[1]),
        pltpu.make_async_copy(values_ref, message_ref.at[:, pl.ds(0, width)], sems.at[2]),
    ]
    for copy in copies:
        copy.start()
    copies[0].wait()
    copies[1].wait()
    group = ids.shape[1]
    high = weights[...].astype(jnp.bfloat16).astype(jnp.float32)
    rest = weights[...] - high
    mid = rest.astype(jnp.bfloat16).astype(jnp.float32)
    terms = [ids[...].astype(jnp.float32), high, mid, rest - mid]
    terms.append(jnp.zeros((LANES - 4 * top, group), jnp.float32))
    table = jnp.concatenate(terms, axis=0).astype(jnp.bfloat16)
    own = lax.broadcasted_iota(jnp.int32, (tok_dev, group), 0) + pos_ref[0] * tok_dev
    own = (own == lax.broadcasted_iota(jnp.int32, (tok_dev, group), 1)).astype(jnp.float32)
    routing = lax.dot_general(
        own.astype(jnp.bfloat16), table, (((1,), (1,)), ((), ())), preferred_element_type=jnp.float32
    )
    message_ref[:, width:] = routing.astype(jnp.bfloat16)
    copies[2].wait()


def split_kernel(half, *refs):
    pieces, (first_ref, second_ref, token_ref) = refs[:-3], refs[-3:]
    pieces = [ref for ref in pieces if ref.shape[1] > 2 * half]
    whole = jnp.concatenate([ref[...].astype(jnp.float32) for ref in pieces], axis=0).astype(jnp.bfloat16)
    second_ref[...] = whole[:, :half]
    first_ref[...] = whole[:, half:]
    token_ref[...] = jnp.zeros_like(token_ref)


def join_kernel(count, signs, *refs):
    out_ref = refs[count + signs]
    rows = refs[0].shape[0]
    for i, ref in enumerate(refs[:count]):
        out_ref[i * rows : (i + 1) * rows] = ref[...]
    for ref in refs[count + signs + 1 :]:
        ref[...] = jnp.zeros_like(ref)


def load_kernel(start, signs, src_ref, *refs):
    sign_ref, *near, sems = refs[signs:]
    copies = load_copies(src_ref, near, sems, start)
    sign_ref[...] = jnp.zeros_like(sign_ref)
    for copy in copies:
        copy.wait()


def load_copies(src_ref, near, sems, start):
    count, runs = sems.shape
    size = src_ref.shape[1] // runs
    copies = []
    for i in range(count):
        for r in range(runs):
            at = pl.ds(r * size, size)
            copies.append(pltpu.make_async_copy(src_ref.at[start + i, at], near[i].at[at], sems.at[i, r]))
    for copy in copies:
        copy.start()
    return copies


def swiglu(normed_ref, gates, ups, hidden_ref, start):
    for i, (gate_ref, up_ref) in enumerate(zip(gates, ups)):
        x = normed_ref[start + i]
        gate_act = jnp.dot(x, gate_ref[...], preferred_element_type=jnp.float32)
        up_act = jnp.dot(x, up_ref[...], preferred_element_type=jnp.float32)
        hidden_ref[i] = (gate_act / (1.0 + jnp.exp(-gate_act)) * up_act).astype(jnp.bfloat16)


def select_kernel(dims, lead, tail, pos_ref, gain_ref, *refs):
    n_fast, n_mid, n_tp, slow_n, tok_dev, top, exp_loc, rows, half = dims
    first, second = refs[:n_fast], refs[n_fast : 2 * n_fast]
    refs = refs[2 * n_fast :]
    gates, ups, refs = refs[:lead], refs[lead : 2 * lead], refs[2 * lead :]
    far_ref, hidden_ref, normed_ref, mix_ref, turned_ref, *near, sems = refs
    copies = load_copies(far_ref, near, sems, lead)
    tp_pos, base = pos_ref[0], pos_ref[1]
    run = slow_n * tok_dev
    tokens = n_fast * n_mid * n_tp * run
    routing = jnp.concatenate([ref[:, half:] for ref in first], axis=0).astype(jnp.float32)
    ids = routing[:, :top]
    weights = routing[:, top : 2 * top] + (
        routing[:, 2 * top : 3 * top] + routing[:, 3 * top : 4 * top]
    )

    def number(shape, dim):
        at = lax.broadcasted_iota(jnp.int32, shape, dim)
        tp_at = lax.rem(lax.div(at, n_mid * run), n_tp)
        return at + (lax.rem(tp_pos - tp_at + n_tp, n_tp) - tp_at) * (n_mid * run)

    before = number((tokens, tokens), 1) < number((tokens, tokens), 0)
    match = [ids == (base + e).astype(jnp.float32) for e in range(exp_loc)]
    hits = [jnp.sum(m.astype(jnp.float32), axis=1, keepdims=True) for m in match]
    shares = [jnp.sum(jnp.where(m, weights, 0.0), axis=1, keepdims=True) for m in match]
    lane = lax.broadcasted_iota(jnp.int32, (tokens, LANES), 1)
    hit = functools.reduce(
        lambda a, e: jnp.where(lane == e, hits[e], a),
        range(exp_loc),
        jnp.zeros((tokens, LANES), jnp.float32),
    )
    position = jnp.dot(
        before.astype(jnp.float32).astype(jnp.bfloat16),
        hit.astype(jnp.bfloat16),
        preferred_element_type=jnp.float32,
    )
    slot = lax.broadcasted_iota(jnp.int32, (tokens, rows), 1).astype(jnp.float32)
    picks, spreads = [], []
    for e in range(exp_loc):
        place = jnp.where(hits[e] > 0, position[:, e : e + 1], -1.0)
        pick = slot == place
        picks.append(pick.astype(jnp.float32))
        spreads.append(jnp.where(pick, shares[e], 0.0))
    spread = jnp.concatenate(spreads, axis=1)
    group = lambda f, m, s: [
        spread[start : start + tok_dev]
        for start in [(((f * n_tp + t) * n_mid + m) * slow_n + s) * tok_dev for t in range(n_tp)]
    ]
    blocks = [b for f in range(n_fast) for m in range(n_mid) for s in range(slow_n) for b in group(f, m, s)]
    turned = [b for f in range(n_fast) for s in range(slow_n) for m in range(n_mid) for b in group(f, m, s)]
    for ref, rows_of in ((mix_ref, blocks), (turned_ref, turned)):
        exact = jnp.concatenate(rows_of, axis=0)
        high = exact.astype(jnp.bfloat16)
        ref[0] = high
        ref[1] = (exact - high.astype(jnp.float32)).astype(jnp.bfloat16)

    part = n_mid * n_tp * run
    gain = gain_ref[...].astype(jnp.float32)
    dims_of = (((0,), (0,)), ((), ()))
    for e in range(exp_loc):
        left, right = [], []
        for f in range(n_fast):
            pick = picks[e][f * part : (f + 1) * part]
            turned = jnp.concatenate(
                [
                    pick[(t * n_mid + m) * run : (t * n_mid + m + 1) * run]
                    for m in range(n_mid)
                    for t in range(n_tp)
                ],
                axis=0,
            )
            left.append(
                lax.dot_general(
                    turned.astype(jnp.bfloat16), second[f][...], dims_of, preferred_element_type=jnp.float32
                )
            )
            right.append(
                lax.dot_general(
                    pick.astype(jnp.bfloat16), first[f][:, :half], dims_of, preferred_element_type=jnp.float32
                )
            )
        left, right = sum(left[1:], left[0]), sum(right[1:], right[0])
        squares = jnp.sum(left * left, axis=1, keepdims=True) + jnp.sum(right * right, axis=1, keepdims=True)
        scale = lax.rsqrt(squares / (2 * half) + 1e-06)
        normed_ref[e, :, :half] = (left * scale * gain[:, :half]).astype(jnp.bfloat16)
        normed_ref[e, :, half:] = (right * scale * gain[:, half:]).astype(jnp.bfloat16)
    swiglu(normed_ref, gates, ups, hidden_ref, 0)
    for copy in copies:
        copy.wait()


def up_kernel(start, count, normed_ref, *refs):
    gates, ups, (far_ref, hidden_ref, *near, sems) = refs[:count], refs[count : 2 * count], refs[2 * count :]
    copies = load_copies(far_ref, near, sems, 0)
    swiglu(normed_ref, gates, ups, hidden_ref, start)
    for copy in copies:
        copy.wait()


def lower(n_tp, tp_pos, pieces, i, down_ref, columns):
    hid_part = pieces[0].shape[2]
    total = 0.0
    for s in range(n_tp):
        begin = pl.multiple_of(lax.rem(tp_pos - s + n_tp, n_tp) * hid_part, hid_part)
        total = total + jnp.dot(
            pieces[s][i], down_ref[pl.ds(begin, hid_part), columns], preferred_element_type=jnp.float32
        )
    return total.astype(jnp.bfloat16)


def down_kernel(n_tp, done, pos_ref, *refs):
    pieces, refs = refs[:n_tp], refs[n_tp:]
    count, rows, _ = pieces[0].shape
    downs, (far_ref, out_ref, *near, sems) = refs[:count], refs[count:]
    copies = load_copies(far_ref, near, sems, done)
    for i, ref in enumerate(downs):
        out_ref[i * rows : (i + 1) * rows] = lower(n_tp, pos_ref[0], pieces, i, ref, slice(None))
    for copy in copies:
        copy.wait()


def mix_kernel(n_tp, begin, pos_ref, mix_ref, done_ref, *refs):
    pieces, (*downs, partial_ref, out_ref) = refs[:n_tp], refs[n_tp:]
    columns = pl.ds(begin, partial_ref.shape[1])
    _, rows, _ = pieces[0].shape
    at = done_ref.shape[0]
    out_ref[:at] = done_ref[:, columns]
    for i, ref in enumerate(downs):
        out_ref[at : at + rows] = lower(n_tp, pos_ref[0], pieces, i, ref, columns)
        at += rows
    out = out_ref[...]
    partial = jnp.dot(mix_ref[0], out, preferred_element_type=jnp.float32)
    partial = partial + jnp.dot(mix_ref[1], out, preferred_element_type=jnp.float32)
    partial_ref[...] = partial.astype(jnp.bfloat16)


VMEM = pl.BlockSpec(memory_space=pltpu.VMEM)
SMEM = pl.BlockSpec(memory_space=pltpu.SMEM)
HBM = pl.BlockSpec(memory_space=pltpu.HBM)
KEPT = pltpu.VMEM
TOKEN = jax.ShapeDtypeStruct((8, LANES), jnp.float32)


def local_call(kernel, shapes, operands, far=(), scratch=(), limit=8 << 20, flops=0, moved=0):
    specs, given = [], []
    for i, a in enumerate(operands):
        if i in far:
            specs.append(HBM)
            given.append(pltpu.with_memory_space_constraint(a, pltpu.HBM))
        else:
            specs.append(SMEM if a.dtype == jnp.int32 else VMEM)
            given.append(a)
    return pl.pallas_call(
        kernel,
        out_shape=shapes,
        in_specs=specs,
        out_specs=[VMEM] * len(shapes),
        scratch_shapes=list(scratch),
        compiler_params=pltpu.CompilerParams(vmem_limit_bytes=limit),
        cost_estimate=pl.CostEstimate(flops=flops, bytes_accessed=moved, transcendentals=0),
    )(*given)


def kept(array, count):
    return [KEPT(array.shape[1:], array.dtype)] * count


def runs_of(array):
    return 4 if array.shape[1] % 64 == 0 else 1


def loaded(array, start, count, after):
    sign, *near = local_call(
        functools.partial(load_kernel, start, len(after)),
        [TOKEN] + kept(array, count),
        [array] + after,
        far=[0],
        scratch=[pltpu.SemaphoreType.DMA((count, runs_of(array)))],
        limit=1 << 20,
        moved=2 * count * array.size // array.shape[0],
    )
    return near, sign


def joined(pieces, after, signed):
    rows, columns = pieces[0].shape
    return local_call(
        functools.partial(join_kernel, len(pieces), len(after)),
        [jax.ShapeDtypeStruct((len(pieces) * rows, columns), pieces[0].dtype)] + [TOKEN] * signed,
        list(pieces) + after,
        limit=4 << 20,
        moved=4 * len(pieces) * rows * columns,
    )


def by_tokens(hidden_in, norm_gain, expert_ids, gate_weights, w_gate, w_up, w_down):
    n_ep = lax.axis_size("ep")
    n_tp = lax.axis_size("tp")
    ep_pos = lax.axis_index("ep")
    tp_pos = lax.axis_index("tp")
    tok_dev, width = hidden_in.shape
    group, top = expert_ids.shape
    exp_loc, _, hid_part = w_gate.shape
    col_part = w_down.shape[2]
    experts = exp_loc * n_ep
    cap = max(2, 2 * top * group // experts)
    rows = cap * n_ep
    tokens = group * n_ep
    digits = factors_of(n_ep)
    fast, mid, slow = digits[0], digits[1:2], digits[2:]
    half = width // 2
    slow_n = n_ep
    for _, radix in [fast] + mid:
        slow_n //= radix
    n_fast, n_mid = fast[1], mid[0][1] if mid else 1

    bf16 = functools.partial(jax.ShapeDtypeStruct, dtype=jnp.bfloat16)
    slots = exp_loc * rows
    lead = exp_loc - exp_loc // 2
    tail = exp_loc - lead
    gain = norm_gain.reshape(1, width)
    position = jnp.stack([tp_pos, ep_pos * exp_loc])
    (message,) = local_call(
        functools.partial(pack_kernel, top),
        [bf16((tok_dev, width + LANES))],
        [position, expert_ids.T, gate_weights.T, hidden_in],
        far=[1, 2, 3],
        scratch=[
            pltpu.VMEM((top, group), jnp.int32),
            pltpu.VMEM((top, group), jnp.float32),
            pltpu.SemaphoreType.DMA((3,)),
        ],
        limit=4 << 20,
    )
    around = [message]
    for digit in reversed(slow):
        around = [a for piece in around for a in arrivals(piece, "ep", n_ep, *digit)]
    gate_lead, sign = loaded(w_gate, 0, lead, [gain])
    first, second, sign = local_call(
        functools.partial(split_kernel, half),
        [bf16((slow_n * tok_dev, width + LANES - half)), bf16((slow_n * tok_dev, half)), TOKEN],
        around + [sign],
        limit=4 << 20,
    )
    gate_tail, sign = loaded(w_gate, lead, tail, [sign])
    along_tp = lambda a: arrivals(a, "tp", n_tp, 1, n_tp)
    along_mid = lambda a: arrivals(a, "ep", n_ep, *mid[0]) if mid else [a]
    first, second = along_mid(first), along_tp(second)
    first, sign = joined(first, [sign], 1)
    (second,) = joined(second, [], 0)
    up_lead, sign = loaded(w_up, 0, lead, [sign])
    first, second = along_tp(first), along_mid(second)
    (first,) = joined(first, [sign], 0)
    (second,) = joined(second, [], 0)
    first = arrivals(first, "ep", n_ep, *fast)
    second = arrivals(second, "ep", n_ep, *fast)

    dims = (n_fast, n_mid, n_tp, slow_n, tok_dev, top, exp_loc, rows, half)
    sems = lambda array, count: pltpu.SemaphoreType.DMA((count, runs_of(array)))
    last = max(1, tail // 2)
    early = exp_loc - last
    operands = [position, gain] + first + second + gate_lead + up_lead + [w_up]
    hidden, normed, mix, turned, *up_tail = local_call(
        functools.partial(select_kernel, dims, lead, tail),
        [
            bf16((lead, rows, hid_part)),
            bf16((exp_loc, rows, width)),
            bf16((2, tokens, slots)),
            bf16((2, tokens, slots)),
        ]
        + kept(w_up, tail),
        operands,
        far=[len(operands) - 1],
        scratch=[sems(w_up, tail)],
        flops=2 * slots * tokens * width + 4 * lead * rows * width * hid_part,
        moved=4 * lead * width * hid_part,
    )
    pieces = along_tp(hidden)
    operands = [normed] + gate_tail + up_tail + [w_down]
    hidden, *down_early = local_call(
        functools.partial(up_kernel, lead, tail),
        [bf16((tail, rows, hid_part))] + kept(w_down, early),
        operands,
        far=[len(operands) - 1],
        scratch=[sems(w_down, early)],
        flops=4 * tail * rows * width * hid_part,
        moved=4 * tail * width * hid_part,
    )
    late = along_tp(hidden)
    operands = [position] + pieces + down_early[:lead] + [w_down]
    done, *down_last = local_call(
        functools.partial(down_kernel, n_tp, early),
        [bf16((lead * rows, col_part))] + kept(w_down, last),
        operands,
        far=[len(operands) - 1],
        scratch=[sems(w_down, last)],
        flops=2 * lead * rows * n_tp * hid_part * col_part,
        moved=2 * lead * n_tp * hid_part * col_part,
    )
    col_half = col_part // 2
    mixed_of = lambda table, begin: local_call(
        functools.partial(mix_kernel, n_tp, begin),
        [bf16((tokens, col_half))],
        [position, table, done] + late + down_early[lead:] + down_last,
        scratch=[pltpu.VMEM((slots, col_half), jnp.bfloat16)],
        flops=slots * n_tp * hid_part * col_part,
        moved=exp_loc * n_tp * hid_part * col_part,
    )[0]

    def over(total, digits):
        for digit in digits:
            total = scattered(total.reshape(digit[1], -1, group, col_half), "ep", n_ep, *digit)
        return total.reshape(n_tp, tok_dev, col_half)

    right = over(mixed_of(turned, col_half), [fast] + list(reversed(slow)) + mid)
    left = over(mixed_of(mix, 0), [fast] + mid + list(reversed(slow)))
    combined = jnp.concatenate([left, right], axis=2)
    column = lambda a, at: lax.dynamic_slice_in_dim(a, at, col_part, 1)
    right = first[0].reshape(n_tp, -1, first[0].shape[1])[:, :tok_dev, :half]
    left = second[0].reshape(n_mid, n_tp, -1, half)[0, :, :tok_dev]
    own = jnp.concatenate([left, right], axis=2)
    residual = lax.dynamic_slice_in_dim(own, tp_pos * col_part, col_part, 2)
    result = (residual.astype(jnp.float32) + combined.astype(jnp.float32)).astype(jnp.bfloat16)
    order = [lax.rem(tp_pos - s + n_tp, n_tp) for s in range(n_tp)]
    turned = []
    for j in range(n_tp):
        piece = result[0]
        for s in range(1, n_tp):
            piece = jnp.where(order[s] == j, result[s], piece)
        turned.append(piece)
    return jnp.concatenate(turned, axis=0)


def by_slots(hidden_in, norm_gain, expert_ids, gate_weights, w_gate, w_up, w_down):
    n_ep = lax.axis_size("ep")
    tp_pos = lax.axis_index("tp")
    tok_dev, width = hidden_in.shape
    group, top = expert_ids.shape
    exp_loc, _, hid_part = w_gate.shape
    col_part = w_down.shape[2]
    experts = exp_loc * n_ep
    cap = max(2, 2 * top * group // experts)
    values = hidden_in.astype(jnp.float32)
    scale = lax.rsqrt(jnp.mean(values * values, axis=1, keepdims=True) + 1e-06)
    normed = (values * scale * norm_gain.astype(jnp.float32)).astype(jnp.bfloat16)
    flat_ids = expert_ids.reshape(-1)
    pairs = flat_ids.shape[0]
    hits = (flat_ids[:, None] == lax.broadcasted_iota(jnp.int32, (pairs, experts), 1)).astype(
        jnp.int32
    )
    before = jnp.cumsum(hits, axis=0) - hits
    position = jnp.sum(before * hits, axis=1)
    slot_index = flat_ids * cap + position
    places = lax.broadcasted_iota(jnp.int32, (experts * cap, group, top), 0)
    dispatch_map = jnp.any(places == slot_index.reshape(group, top)[None], axis=2).astype(
        jnp.bfloat16
    )
    whole_norm, whole_input = (
        lax.all_gather(normed, "tp", axis=0, tiled=True),
        lax.all_gather(hidden_in, "tp", axis=0, tiled=True),
    )
    residual = lax.dynamic_slice_in_dim(whole_input, tp_pos * col_part, col_part, 1)
    packed = jnp.dot(dispatch_map, whole_norm, preferred_element_type=jnp.float32).astype(
        jnp.bfloat16
    )
    packed = packed.reshape(n_ep, exp_loc, cap, width)
    arrived = lax.all_to_all(packed, "ep", split_axis=0, concat_axis=0, tiled=True)
    gate_act = jnp.einsum("secd,edh->sech", arrived, w_gate, preferred_element_type=jnp.float32)
    up_act = jnp.einsum("secd,edh->sech", arrived, w_up, preferred_element_type=jnp.float32)
    hidden = (jax.nn.silu(gate_act) * up_act).astype(jnp.bfloat16)
    outputs = jnp.einsum(
        "sech,ehf->secf",
        lax.all_gather(hidden, "tp", axis=3, tiled=True),
        w_down,
        preferred_element_type=jnp.float32,
    )
    returned = lax.all_to_all(
        outputs.astype(jnp.bfloat16), "ep", split_axis=0, concat_axis=0, tiled=True
    )
    flat_back = returned.reshape(experts * cap, col_part)
    picked = flat_back[slot_index].reshape(group, top, col_part).astype(jnp.float32)
    combined = jnp.sum(picked * gate_weights[:, :, None], axis=1)
    return (residual.astype(jnp.float32) + combined).astype(jnp.bfloat16)


def shards(hidden_in, norm_gain, expert_ids, gate_weights, w_gate, w_up, w_down):
    group, top = expert_ids.shape
    exp_loc = w_gate.shape[0]
    cap = max(2, 2 * top * group // (exp_loc * lax.axis_size("ep")))
    plan = by_tokens if exp_loc > 1 and exp_loc * cap >= group else by_slots
    return plan(hidden_in, norm_gain, expert_ids, gate_weights, w_gate, w_up, w_down)


def solution(mesh):
    in_specs = (
        P(("ep", "tp"), None),
        P(),
        P("ep", None),
        P("ep", None),
        P("ep", None, "tp"),
        P("ep", None, "tp"),
        P("ep", None, "tp"),
    )
    out_specs = P("ep", "tp")
    return jax.shard_map(shards, mesh=mesh, in_specs=in_specs, out_specs=out_specs, check_vma=False)
```

```python
import functools

import jax
import jax.numpy as jnp
from jax import lax
from jax.experimental import pallas as pl
from jax.experimental.pallas import tpu as pltpu
from jax.sharding import PartitionSpec as P

LANES = 128


def factors_of(n):
    digits, stride = [], 1
    for _ in range(2):
        if n % 2 == 0 and n > 1:
            digits.append((stride, 2))
            stride, n = stride * 2, n // 2
    while n > 1:
        radix = next(r for r in (4, 3, 2, n) if n % r == 0)
        digits.append((stride, radix))
        stride, n = stride * radix, n // radix
    return digits


def shifted(x, axis, size, stride, radix, by):
    pairs = []
    for i in range(size):
        digit = i // stride % radix
        pairs.append((i, i + ((digit + by) % radix - digit) * stride))
    return lax.ppermute(x, axis, pairs)


def arrivals(x, axis, size, stride, radix):
    return [x] + [shifted(x, axis, size, stride, radix, s) for s in range(1, radix)]


def pack_kernel(top, pos_ref, ids_ref, weights_ref, values_ref, message_ref, ids, weights, sems):
    tok_dev, width = values_ref.shape
    copies = [
        pltpu.make_async_copy(ids_ref, ids, sems.at[0]),
        pltpu.make_async_copy(weights_ref, weights, sems.at[1]),
        pltpu.make_async_copy(values_ref, message_ref.at[:, pl.ds(0, width)], sems.at[2]),
    ]
    for copy in copies:
        copy.start()
    copies[0].wait()
    copies[1].wait()
    group = ids.shape[1]
    high = weights[...].astype(jnp.bfloat16).astype(jnp.float32)
    rest = weights[...] - high
    mid = rest.astype(jnp.bfloat16).astype(jnp.float32)
    terms = [ids[...].astype(jnp.float32), high, mid, rest - mid]
    terms.append(jnp.zeros((LANES - 4 * top, group), jnp.float32))
    table = jnp.concatenate(terms, axis=0).astype(jnp.bfloat16)
    own = lax.broadcasted_iota(jnp.int32, (tok_dev, group), 0) + pos_ref[0] * tok_dev
    own = (own == lax.broadcasted_iota(jnp.int32, (tok_dev, group), 1)).astype(jnp.float32)
    routing = lax.dot_general(
        own.astype(jnp.bfloat16), table, (((1,), (1,)), ((), ())), preferred_element_type=jnp.float32
    )
    message_ref[:, width:] = routing.astype(jnp.bfloat16)
    copies[2].wait()


def split_kernel(half, *refs):
    pieces, (first_ref, second_ref, token_ref) = refs[:-3], refs[-3:]
    pieces = [ref for ref in pieces if ref.shape[1] > 2 * half]
    whole = jnp.concatenate([ref[...].astype(jnp.float32) for ref in pieces], axis=0).astype(jnp.bfloat16)
    second_ref[...] = whole[:, :half]
    first_ref[...] = whole[:, half:]
    token_ref[...] = jnp.zeros_like(token_ref)


def join_kernel(count, signs, *refs):
    out_ref = refs[count + signs]
    rows = refs[0].shape[0]
    for i, ref in enumerate(refs[:count]):
        out_ref[i * rows : (i + 1) * rows] = ref[...]
    for ref in refs[count + signs + 1 :]:
        ref[...] = jnp.zeros_like(ref)


def load_kernel(experts, signs, *refs):
    count = len(experts)
    refs = refs[:count] + refs[count + signs :]
    far, (sign_ref, *near, sems) = refs[:count], refs[count:]
    copies = load_copies(far, near, sems, experts)
    sign_ref[...] = jnp.zeros_like(sign_ref)
    for copy in copies:
        copy.wait()


def load_copies(far, near, sems, experts):
    copies = []
    for i, (src_ref, dst_ref, expert) in enumerate(zip(far, near, experts)):
        runs = sems.shape[1]
        size = dst_ref.shape[0] // runs
        for r in range(runs):
            at = pl.ds(r * size, size)
            copies.append(pltpu.make_async_copy(src_ref.at[expert, at], dst_ref.at[at], sems.at[i, r]))
    for copy in copies:
        copy.start()
    return copies


def swiglu(normed_ref, gates, ups, hidden_ref, start):
    for i, (gate_ref, up_ref) in enumerate(zip(gates, ups)):
        x = normed_ref[start + i]
        gate_act = jnp.dot(x, gate_ref[...], preferred_element_type=jnp.float32)
        up_act = jnp.dot(x, up_ref[...], preferred_element_type=jnp.float32)
        hidden_ref[i] = (gate_act / (1.0 + jnp.exp(-gate_act)) * up_act).astype(jnp.bfloat16)


def select_kernel(dims, lead, tail, pos_ref, gain_ref, *refs):
    n_fast, n_mid, n_tp, slow_n, tok_dev, top, exp_loc, rows, half = dims
    first, second = refs[:n_fast], refs[n_fast : 2 * n_fast]
    refs = refs[2 * n_fast :]
    gates, ups, refs = refs[:lead], refs[lead : 2 * lead], refs[2 * lead :]
    far_ref, hidden_ref, normed_ref, mix_ref, turned_ref, *near, sems = refs
    copies = load_copies([far_ref] * tail, near, sems, range(lead, lead + tail))
    tp_pos, base = pos_ref[0], pos_ref[1]
    run = slow_n * tok_dev
    tokens = n_fast * n_mid * n_tp * run
    routing = jnp.concatenate([ref[:, half:] for ref in first], axis=0).astype(jnp.float32)
    ids = routing[:, :top]
    weights = routing[:, top : 2 * top] + (
        routing[:, 2 * top : 3 * top] + routing[:, 3 * top : 4 * top]
    )

    def number(shape, dim):
        at = lax.broadcasted_iota(jnp.int32, shape, dim)
        tp_at = lax.rem(lax.div(at, n_mid * run), n_tp)
        return at + (lax.rem(tp_pos - tp_at + n_tp, n_tp) - tp_at) * (n_mid * run)

    before = number((tokens, tokens), 1) < number((tokens, tokens), 0)
    match = [ids == (base + e).astype(jnp.float32) for e in range(exp_loc)]
    hits = [jnp.sum(m.astype(jnp.float32), axis=1, keepdims=True) for m in match]
    shares = [jnp.sum(jnp.where(m, weights, 0.0), axis=1, keepdims=True) for m in match]
    lane = lax.broadcasted_iota(jnp.int32, (tokens, LANES), 1)
    hit = functools.reduce(
        lambda a, e: jnp.where(lane == e, hits[e], a),
        range(exp_loc),
        jnp.zeros((tokens, LANES), jnp.float32),
    )
    position = jnp.dot(
        before.astype(jnp.float32).astype(jnp.bfloat16),
        hit.astype(jnp.bfloat16),
        preferred_element_type=jnp.float32,
    )
    slot = lax.broadcasted_iota(jnp.int32, (tokens, rows), 1).astype(jnp.float32)
    picks, spreads = [], []
    for e in range(exp_loc):
        place = jnp.where(hits[e] > 0, position[:, e : e + 1], -1.0)
        pick = slot == place
        picks.append(pick.astype(jnp.float32))
        spreads.append(jnp.where(pick, shares[e], 0.0))
    spread = jnp.concatenate(spreads, axis=1)
    group = lambda f, m, s: [
        spread[start : start + tok_dev]
        for start in [(((f * n_tp + t) * n_mid + m) * slow_n + s) * tok_dev for t in range(n_tp)]
    ]
    blocks = [b for f in range(n_fast) for m in range(n_mid) for s in range(slow_n) for b in group(f, m, s)]
    turned = [b for f in range(n_fast) for s in range(slow_n) for m in range(n_mid) for b in group(f, m, s)]
    for ref, rows_of in ((mix_ref, blocks), (turned_ref, turned)):
        exact = jnp.concatenate(rows_of, axis=0)
        high = exact.astype(jnp.bfloat16)
        ref[0] = high
        ref[1] = (exact - high.astype(jnp.float32)).astype(jnp.bfloat16)

    part = n_mid * n_tp * run
    gain = gain_ref[...].astype(jnp.float32)
    dims_of = (((0,), (0,)), ((), ()))
    for e in range(exp_loc):
        left, right = [], []
        for f in range(n_fast):
            pick = picks[e][f * part : (f + 1) * part]
            turned = jnp.concatenate(
                [
                    pick[(t * n_mid + m) * run : (t * n_mid + m + 1) * run]
                    for m in range(n_mid)
                    for t in range(n_tp)
                ],
                axis=0,
            )
            left.append(
                lax.dot_general(
                    turned.astype(jnp.bfloat16), second[f][...], dims_of, preferred_element_type=jnp.float32
                )
            )
            right.append(
                lax.dot_general(
                    pick.astype(jnp.bfloat16), first[f][:, :half], dims_of, preferred_element_type=jnp.float32
                )
            )
        left, right = sum(left[1:], left[0]), sum(right[1:], right[0])
        squares = jnp.sum(left * left, axis=1, keepdims=True) + jnp.sum(right * right, axis=1, keepdims=True)
        scale = lax.rsqrt(squares / (2 * half) + 1e-06)
        normed_ref[e, :, :half] = (left * scale * gain[:, :half]).astype(jnp.bfloat16)
        normed_ref[e, :, half:] = (right * scale * gain[:, half:]).astype(jnp.bfloat16)
    swiglu(normed_ref, gates, ups, hidden_ref, 0)
    for copy in copies:
        copy.wait()


def up_kernel(start, count, wanted, normed_ref, *refs):
    gates, ups, (far_ref, hidden_ref, *near, sems) = refs[:count], refs[count : 2 * count], refs[2 * count :]
    copies = load_copies([far_ref] * len(near), near, sems, wanted)
    swiglu(normed_ref, gates, ups, hidden_ref, start)
    for copy in copies:
        copy.wait()


def lower(n_tp, tp_pos, pieces, i, down_ref, columns):
    hid_part = pieces[0].shape[2]
    total = 0.0
    for s in range(n_tp):
        begin = pl.multiple_of(lax.rem(tp_pos - s + n_tp, n_tp) * hid_part, hid_part)
        total = total + jnp.dot(
            pieces[s][i], down_ref[pl.ds(begin, hid_part), columns], preferred_element_type=jnp.float32
        )
    return total.astype(jnp.bfloat16)


def down_kernel(n_tp, pos_ref, *refs):
    pieces, (*downs, out_ref) = refs[:n_tp], refs[n_tp:]
    _, rows, _ = pieces[0].shape
    for i, ref in enumerate(downs):
        out_ref[i * rows : (i + 1) * rows] = lower(n_tp, pos_ref[0], pieces, i, ref, slice(None))


def in_blocks(total, refs):
    rows = refs[0].shape[0]
    for i, ref in enumerate(refs):
        ref[...] = total[i * rows : (i + 1) * rows].astype(jnp.bfloat16)


def mix_kernel(n_tp, count, begin, pos_ref, mix_ref, done_ref, *refs):
    pieces, downs, (*partial_refs, out_ref) = refs[:n_tp], refs[n_tp : n_tp + count], refs[n_tp + count :]
    columns = pl.ds(begin, out_ref.shape[1])
    _, rows, _ = pieces[0].shape
    at = done_ref.shape[0]
    out_ref[:at] = done_ref[:, columns]
    for i, ref in enumerate(downs):
        out_ref[at : at + rows] = lower(n_tp, pos_ref[0], pieces, i, ref, columns)
        at += rows
    out = out_ref[...]
    partial = jnp.dot(mix_ref[0], out, preferred_element_type=jnp.float32)
    partial = partial + jnp.dot(mix_ref[1], out, preferred_element_type=jnp.float32)
    in_blocks(partial, partial_refs)


def total_of(refs):
    return functools.reduce(lambda a, ref: a + ref[...].astype(jnp.float32), refs[1:], refs[0][...].astype(jnp.float32))


def sum_kernel(count, signs, blocks, *refs):
    out_refs = refs[count + signs :]
    in_blocks(total_of(refs[:count]), out_refs[:blocks])
    for ref in out_refs[blocks:]:
        ref[...] = jnp.zeros_like(ref)


def final_kernel(dims, count, pos_ref, first_ref, second_ref, *refs):
    n_mid, n_tp, slow_n, tok_dev, half = dims
    left, right, (out_ref, own_ref) = refs[:count], refs[count:-2], refs[-2:]
    tp_pos = pos_ref[0]
    col_part = out_ref.shape[1]
    for s in range(n_tp):
        at = s * n_mid * slow_n * tok_dev
        own_ref[s * tok_dev : (s + 1) * tok_dev, half:] = first_ref[at : at + tok_dev, :half].astype(jnp.float32)
        at = s * slow_n * tok_dev
        own_ref[s * tok_dev : (s + 1) * tok_dev, :half] = second_ref[at : at + tok_dev].astype(jnp.float32)
    total = jnp.concatenate([total_of(left), total_of(right)], axis=1)
    total = total + own_ref[:, pl.ds(pl.multiple_of(tp_pos * col_part, col_part), col_part)]
    rows = []
    for j in range(n_tp):
        row = total[:tok_dev]
        for s in range(1, n_tp):
            here = lax.rem(tp_pos - s + n_tp, n_tp) == j
            row = jnp.where(here, total[s * tok_dev : (s + 1) * tok_dev], row)
        rows.append(row)
    out_ref[...] = jnp.concatenate(rows, axis=0).astype(jnp.bfloat16)


VMEM = pl.BlockSpec(memory_space=pltpu.VMEM)
SMEM = pl.BlockSpec(memory_space=pltpu.SMEM)
HBM = pl.BlockSpec(memory_space=pltpu.HBM)
KEPT = pltpu.VMEM
TOKEN = jax.ShapeDtypeStruct((8, LANES), jnp.float32)


def local_call(kernel, shapes, operands, far=(), scratch=(), limit=8 << 20, flops=0, moved=0):
    specs, given = [], []
    for i, a in enumerate(operands):
        if i in far:
            specs.append(HBM)
            given.append(pltpu.with_memory_space_constraint(a, pltpu.HBM))
        else:
            specs.append(SMEM if a.dtype == jnp.int32 else VMEM)
            given.append(a)
    return pl.pallas_call(
        kernel,
        out_shape=shapes,
        in_specs=specs,
        out_specs=[VMEM] * len(shapes),
        scratch_shapes=list(scratch),
        compiler_params=pltpu.CompilerParams(vmem_limit_bytes=limit),
        cost_estimate=pl.CostEstimate(flops=flops, bytes_accessed=moved, transcendentals=0),
    )(*given)


def kept(array, count):
    return [KEPT(array.shape[1:], array.dtype)] * count


def runs_of(array):
    return 4 if array.shape[1] % 64 == 0 else 1


def loaded(wanted, after):
    sign, *near = local_call(
        functools.partial(load_kernel, [expert for _, expert in wanted], len(after)),
        [TOKEN] + [KEPT(array.shape[1:], array.dtype) for array, _ in wanted],
        [array for array, _ in wanted] + after,
        far=range(len(wanted)),
        scratch=[pltpu.SemaphoreType.DMA((len(wanted), min(runs_of(array) for array, _ in wanted)))],
        limit=1 << 20,
        moved=2 * sum(array.size // array.shape[0] for array, _ in wanted),
    )
    return near, sign


def summed(pieces, blocks, after, signed):
    rows, columns = pieces[0].shape
    return local_call(
        functools.partial(sum_kernel, len(pieces), len(after), blocks),
        [jax.ShapeDtypeStruct((rows // blocks, columns), pieces[0].dtype)] * blocks + [TOKEN] * signed,
        list(pieces) + after,
        limit=4 << 20,
        moved=2 * (len(pieces) + 1) * rows * columns,
    )


def joined(pieces, after, signed):
    rows, columns = pieces[0].shape
    return local_call(
        functools.partial(join_kernel, len(pieces), len(after)),
        [jax.ShapeDtypeStruct((len(pieces) * rows, columns), pieces[0].dtype)] + [TOKEN] * signed,
        list(pieces) + after,
        limit=4 << 20,
        moved=4 * len(pieces) * rows * columns,
    )


def by_tokens(hidden_in, norm_gain, expert_ids, gate_weights, w_gate, w_up, w_down):
    n_ep = lax.axis_size("ep")
    n_tp = lax.axis_size("tp")
    ep_pos = lax.axis_index("ep")
    tp_pos = lax.axis_index("tp")
    tok_dev, width = hidden_in.shape
    group, top = expert_ids.shape
    exp_loc, _, hid_part = w_gate.shape
    col_part = w_down.shape[2]
    experts = exp_loc * n_ep
    cap = max(2, 2 * top * group // experts)
    rows = cap * n_ep
    tokens = group * n_ep
    digits = factors_of(n_ep)
    fast, mid, slow = digits[0], digits[1:2], digits[2:]
    half = width // 2
    slow_n = n_ep
    for _, radix in [fast] + mid:
        slow_n //= radix
    n_fast, n_mid = fast[1], mid[0][1] if mid else 1

    bf16 = functools.partial(jax.ShapeDtypeStruct, dtype=jnp.bfloat16)
    slots = exp_loc * rows
    lead = exp_loc - exp_loc // 2
    tail = exp_loc - lead
    gain = norm_gain.reshape(1, width)
    position = jnp.stack([tp_pos, ep_pos * exp_loc])
    (message,) = local_call(
        functools.partial(pack_kernel, top),
        [bf16((tok_dev, width + LANES))],
        [position, expert_ids.T, gate_weights.T, hidden_in],
        far=[1, 2, 3],
        scratch=[
            pltpu.VMEM((top, group), jnp.int32),
            pltpu.VMEM((top, group), jnp.float32),
            pltpu.SemaphoreType.DMA((3,)),
        ],
        limit=4 << 20,
    )
    around = [message]
    for digit in reversed(slow):
        around = [a for piece in around for a in arrivals(piece, "ep", n_ep, *digit)]
    gate_lead, sign = loaded([(w_gate, e) for e in range(lead)], [gain])
    first, second, sign = local_call(
        functools.partial(split_kernel, half),
        [bf16((slow_n * tok_dev, width + LANES - half)), bf16((slow_n * tok_dev, half)), TOKEN],
        around + [sign],
        limit=4 << 20,
    )
    gate_tail, sign = loaded([(w_gate, e) for e in range(lead, exp_loc)], [sign])
    along_tp = lambda a: arrivals(a, "tp", n_tp, 1, n_tp)
    along_mid = lambda a: arrivals(a, "ep", n_ep, *mid[0]) if mid else [a]
    first, second = along_mid(first), along_tp(second)
    first, sign = joined(first, [sign], 1)
    (second,) = joined(second, [], 0)
    up_lead, sign = loaded([(w_up, e) for e in range(lead)] + [(w_down, 0)], [sign])
    *up_lead, down_first = up_lead
    first, second = along_tp(first), along_mid(second)
    first, sign = joined(first, [sign], 1)
    down_lead, _ = loaded([(w_down, e) for e in range(1, lead)], [sign]) if lead > 1 else ([], None)
    down_lead = [down_first] + down_lead
    (second,) = joined(second, [], 0)
    first = arrivals(first, "ep", n_ep, *fast)
    second = arrivals(second, "ep", n_ep, *fast)

    dims = (n_fast, n_mid, n_tp, slow_n, tok_dev, top, exp_loc, rows, half)
    sems = lambda array, count: pltpu.SemaphoreType.DMA((count, runs_of(array)))
    operands = [position, gain] + first + second + gate_lead + up_lead + [w_up]
    hidden, normed, mix, turned, *up_tail = local_call(
        functools.partial(select_kernel, dims, lead, tail),
        [
            bf16((lead, rows, hid_part)),
            bf16((exp_loc, rows, width)),
            bf16((2, tokens, slots)),
            bf16((2, tokens, slots)),
        ]
        + kept(w_up, tail),
        operands,
        far=[len(operands) - 1],
        scratch=[sems(w_up, tail)],
        flops=2 * slots * tokens * width + 4 * lead * rows * width * hid_part,
        moved=4 * lead * width * hid_part,
    )
    pieces = along_tp(hidden)
    operands = [normed] + gate_tail + up_tail + [w_down]
    hidden, *down_tail = local_call(
        functools.partial(up_kernel, lead, tail, range(lead, exp_loc)),
        [bf16((tail, rows, hid_part))] + kept(w_down, tail),
        operands,
        far=[len(operands) - 1],
        scratch=[sems(w_down, tail)],
        flops=4 * tail * rows * width * hid_part,
        moved=4 * tail * width * hid_part,
    )
    late = along_tp(hidden)
    (done,) = local_call(
        functools.partial(down_kernel, n_tp),
        [bf16((lead * rows, col_part))],
        [position] + pieces + down_lead,
        flops=2 * lead * rows * n_tp * hid_part * col_part,
        moved=2 * lead * n_tp * hid_part * col_part,
    )
    col_half = col_part // 2
    mixed_of = lambda table, begin: local_call(
        functools.partial(mix_kernel, n_tp, tail, begin),
        [bf16((tokens // n_fast, col_half))] * n_fast,
        [position, table, done] + late + down_tail,
        scratch=[pltpu.VMEM((slots, col_half), jnp.bfloat16)],
        flops=slots * n_tp * hid_part * col_part,
        moved=exp_loc * n_tp * hid_part * col_part,
    )

    def swapped(blocks, digit):
        stride, radix = digit
        return [blocks[0]] + [shifted(blocks[s], "ep", n_ep, stride, radix, radix - s) for s in range(1, radix)]

    slow = list(reversed(slow))
    right_way, left_way = slow + mid, mid + slow
    right = summed(swapped(mixed_of(turned, col_half), fast), right_way[0][1], [], 0)
    left = summed(swapped(mixed_of(mix, 0), fast), left_way[0][1], [], 0)
    signs = []
    for digit, later in zip(left_way[:-1], left_way[1:]):
        *left, sign = summed(swapped(left, digit), later[1], [], 1)
        signs.append(sign)
    for digit, later in zip(right_way[:-1], right_way[1:]):
        right = summed(swapped(right, digit), later[1], signs, 0)
        signs = []
    left = swapped(left, left_way[-1])
    right = swapped(right, right_way[-1])
    (mixed,) = local_call(
        functools.partial(final_kernel, (n_mid, n_tp, slow_n, tok_dev, half), len(left)),
        [bf16((group, col_part))],
        [position, first[0], second[0]] + left + right,
        scratch=[pltpu.VMEM((group, width), jnp.float32)],
        limit=4 << 20,
        moved=2 * group * (width + 6 * col_part),
    )
    return mixed


def by_slots(hidden_in, norm_gain, expert_ids, gate_weights, w_gate, w_up, w_down):
    n_ep = lax.axis_size("ep")
    tp_pos = lax.axis_index("tp")
    tok_dev, width = hidden_in.shape
    group, top = expert_ids.shape
    exp_loc, _, hid_part = w_gate.shape
    col_part = w_down.shape[2]
    experts = exp_loc * n_ep
    cap = max(2, 2 * top * group // experts)
    values = hidden_in.astype(jnp.float32)
    scale = lax.rsqrt(jnp.mean(values * values, axis=1, keepdims=True) + 1e-06)
    normed = (values * scale * norm_gain.astype(jnp.float32)).astype(jnp.bfloat16)
    flat_ids = expert_ids.reshape(-1)
    pairs = flat_ids.shape[0]
    hits = (flat_ids[:, None] == lax.broadcasted_iota(jnp.int32, (pairs, experts), 1)).astype(
        jnp.int32
    )
    before = jnp.cumsum(hits, axis=0) - hits
    position = jnp.sum(before * hits, axis=1)
    slot_index = flat_ids * cap + position
    places = lax.broadcasted_iota(jnp.int32, (experts * cap, group, top), 0)
    dispatch_map = jnp.any(places == slot_index.reshape(group, top)[None], axis=2).astype(
        jnp.bfloat16
    )
    whole_norm, whole_input = (
        lax.all_gather(normed, "tp", axis=0, tiled=True),
        lax.all_gather(hidden_in, "tp", axis=0, tiled=True),
    )
    residual = lax.dynamic_slice_in_dim(whole_input, tp_pos * col_part, col_part, 1)
    packed = jnp.dot(dispatch_map, whole_norm, preferred_element_type=jnp.float32).astype(
        jnp.bfloat16
    )
    packed = packed.reshape(n_ep, exp_loc, cap, width)
    arrived = lax.all_to_all(packed, "ep", split_axis=0, concat_axis=0, tiled=True)
    gate_act = jnp.einsum("secd,edh->sech", arrived, w_gate, preferred_element_type=jnp.float32)
    up_act = jnp.einsum("secd,edh->sech", arrived, w_up, preferred_element_type=jnp.float32)
    hidden = (jax.nn.silu(gate_act) * up_act).astype(jnp.bfloat16)
    outputs = jnp.einsum(
        "sech,ehf->secf",
        lax.all_gather(hidden, "tp", axis=3, tiled=True),
        w_down,
        preferred_element_type=jnp.float32,
    )
    returned = lax.all_to_all(
        outputs.astype(jnp.bfloat16), "ep", split_axis=0, concat_axis=0, tiled=True
    )
    flat_back = returned.reshape(experts * cap, col_part)
    picked = flat_back[slot_index].reshape(group, top, col_part).astype(jnp.float32)
    combined = jnp.sum(picked * gate_weights[:, :, None], axis=1)
    return (residual.astype(jnp.float32) + combined).astype(jnp.bfloat16)


def shards(hidden_in, norm_gain, expert_ids, gate_weights, w_gate, w_up, w_down):
    group, top = expert_ids.shape
    exp_loc = w_gate.shape[0]
    cap = max(2, 2 * top * group // (exp_loc * lax.axis_size("ep")))
    plan = by_tokens if exp_loc > 1 and exp_loc * cap >= group else by_slots
    return plan(hidden_in, norm_gain, expert_ids, gate_weights, w_gate, w_up, w_down)


def solution(mesh):
    in_specs = (
        P(("ep", "tp"), None),
        P(),
        P("ep", None),
        P("ep", None),
        P("ep", None, "tp"),
        P("ep", None, "tp"),
        P("ep", None, "tp"),
    )
    out_specs = P("ep", "tp")
    return jax.shard_map(shards, mesh=mesh, in_specs=in_specs, out_specs=out_specs, check_vma=False)
```

```python
import functools

import jax
import jax.numpy as jnp
from jax import lax
from jax.experimental import pallas as pl
from jax.experimental.pallas import tpu as pltpu
from jax.sharding import PartitionSpec as P

LANES = 128


def factors_of(n):
    digits, stride = [], 1
    for _ in range(2):
        if n % 2 == 0 and n > 1:
            digits.append((stride, 2))
            stride, n = stride * 2, n // 2
    while n > 1:
        radix = next(r for r in (4, 3, 2, n) if n % r == 0)
        digits.append((stride, radix))
        stride, n = stride * radix, n // radix
    return digits


def shifted(x, axis, size, stride, radix, by):
    pairs = []
    for i in range(size):
        digit = i // stride % radix
        pairs.append((i, i + ((digit + by) % radix - digit) * stride))
    return lax.ppermute(x, axis, pairs)


def arrivals(x, axis, size, stride, radix):
    return [x] + [shifted(x, axis, size, stride, radix, s) for s in range(1, radix)]


def pack_kernel(top, pos_ref, ids_ref, weights_ref, values_ref, message_ref, ids, weights, sems):
    tok_dev, width = values_ref.shape
    copies = [
        pltpu.make_async_copy(ids_ref, ids, sems.at[0]),
        pltpu.make_async_copy(weights_ref, weights, sems.at[1]),
        pltpu.make_async_copy(values_ref, message_ref.at[:, pl.ds(0, width)], sems.at[2]),
    ]
    for copy in copies:
        copy.start()
    copies[0].wait()
    copies[1].wait()
    group = ids.shape[1]
    high = weights[...].astype(jnp.bfloat16).astype(jnp.float32)
    rest = weights[...] - high
    mid = rest.astype(jnp.bfloat16).astype(jnp.float32)
    terms = [ids[...].astype(jnp.float32), high, mid, rest - mid]
    terms.append(jnp.zeros((LANES - 4 * top, group), jnp.float32))
    table = jnp.concatenate(terms, axis=0).astype(jnp.bfloat16)
    own = lax.broadcasted_iota(jnp.int32, (tok_dev, group), 0) + pos_ref[0] * tok_dev
    own = (own == lax.broadcasted_iota(jnp.int32, (tok_dev, group), 1)).astype(jnp.float32)
    routing = lax.dot_general(
        own.astype(jnp.bfloat16), table, (((1,), (1,)), ((), ())), preferred_element_type=jnp.float32
    )
    message_ref[:, width:] = routing.astype(jnp.bfloat16)
    copies[2].wait()


def split_kernel(half, *refs):
    pieces, (first_ref, second_ref, token_ref) = refs[:-3], refs[-3:]
    pieces = [ref for ref in pieces if ref.shape[1] > 2 * half]
    whole = jnp.concatenate([ref[...].astype(jnp.float32) for ref in pieces], axis=0).astype(jnp.bfloat16)
    second_ref[...] = whole[:, :half]
    first_ref[...] = whole[:, half:]
    token_ref[...] = jnp.zeros_like(token_ref)


def join_kernel(count, signs, *refs):
    out_ref = refs[count + signs]
    rows = refs[0].shape[0]
    for i, ref in enumerate(refs[:count]):
        out_ref[i * rows : (i + 1) * rows] = ref[...]
    for ref in refs[count + signs + 1 :]:
        ref[...] = jnp.zeros_like(ref)


def load_kernel(experts, signs, *refs):
    count = len(experts)
    refs = refs[:count] + refs[count + signs :]
    far, (sign_ref, *near, sems) = refs[:count], refs[count:]
    copies = load_copies(far, near, sems, experts)
    sign_ref[...] = jnp.zeros_like(sign_ref)
    for copy in copies:
        copy.wait()


def load_copies(far, near, sems, experts):
    copies = []
    for i, (src_ref, dst_ref, expert) in enumerate(zip(far, near, experts)):
        runs = sems.shape[1]
        size = dst_ref.shape[0] // runs
        for r in range(runs):
            at = pl.ds(r * size, size)
            copies.append(pltpu.make_async_copy(src_ref.at[expert, at], dst_ref.at[at], sems.at[i, r]))
    for copy in copies:
        copy.start()
    return copies


def swiglu(normed_ref, gates, ups, hidden_ref, start):
    for i, (gate_ref, up_ref) in enumerate(zip(gates, ups)):
        x = normed_ref[start + i]
        gate_act = jnp.dot(x, gate_ref[...], preferred_element_type=jnp.float32)
        up_act = jnp.dot(x, up_ref[...], preferred_element_type=jnp.float32)
        hidden_ref[i] = (gate_act / (1.0 + jnp.exp(-gate_act)) * up_act).astype(jnp.bfloat16)


def select_body(dims, pos_ref, gain_ref, first, second, gates, ups, hidden_ref, normed_ref, mix_ref, turned_ref):
    n_fast, n_mid, n_tp, slow_n, tok_dev, top, exp_loc, rows, half = dims
    tp_pos, base = pos_ref[0], pos_ref[1]
    run = slow_n * tok_dev
    tokens = n_fast * n_mid * n_tp * run
    routing = jnp.concatenate([ref[:, half:] for ref in first], axis=0).astype(jnp.float32)
    ids = routing[:, :top]
    weights = routing[:, top : 2 * top] + (
        routing[:, 2 * top : 3 * top] + routing[:, 3 * top : 4 * top]
    )

    def number(shape, dim):
        at = lax.broadcasted_iota(jnp.int32, shape, dim)
        tp_at = lax.rem(lax.div(at, n_mid * run), n_tp)
        return at + (lax.rem(tp_pos - tp_at + n_tp, n_tp) - tp_at) * (n_mid * run)

    before = number((tokens, tokens), 1) < number((tokens, tokens), 0)
    match = [ids == (base + e).astype(jnp.float32) for e in range(exp_loc)]
    hits = [jnp.sum(m.astype(jnp.float32), axis=1, keepdims=True) for m in match]
    shares = [jnp.sum(jnp.where(m, weights, 0.0), axis=1, keepdims=True) for m in match]
    lane = lax.broadcasted_iota(jnp.int32, (tokens, LANES), 1)
    hit = functools.reduce(
        lambda a, e: jnp.where(lane == e, hits[e], a),
        range(exp_loc),
        jnp.zeros((tokens, LANES), jnp.float32),
    )
    position = jnp.dot(
        before.astype(jnp.float32).astype(jnp.bfloat16),
        hit.astype(jnp.bfloat16),
        preferred_element_type=jnp.float32,
    )
    slot = lax.broadcasted_iota(jnp.int32, (tokens, rows), 1).astype(jnp.float32)
    picks, spreads = [], []
    for e in range(exp_loc):
        place = jnp.where(hits[e] > 0, position[:, e : e + 1], -1.0)
        pick = slot == place
        picks.append(pick.astype(jnp.float32))
        spreads.append(jnp.where(pick, shares[e], 0.0))
    spread = jnp.concatenate(spreads, axis=1)
    group = lambda f, m, s: [
        spread[start : start + tok_dev]
        for start in [(((f * n_tp + t) * n_mid + m) * slow_n + s) * tok_dev for t in range(n_tp)]
    ]
    blocks = [b for f in range(n_fast) for m in range(n_mid) for s in range(slow_n) for b in group(f, m, s)]
    turned = [b for f in range(n_fast) for s in range(slow_n) for m in range(n_mid) for b in group(f, m, s)]
    for ref, rows_of in ((mix_ref, blocks), (turned_ref, turned)):
        exact = jnp.concatenate(rows_of, axis=0)
        high = exact.astype(jnp.bfloat16)
        ref[0] = high
        ref[1] = (exact - high.astype(jnp.float32)).astype(jnp.bfloat16)

    part = n_mid * n_tp * run
    gain = gain_ref[...].astype(jnp.float32)
    dims_of = (((0,), (0,)), ((), ()))
    for e in range(exp_loc):
        left, right = [], []
        for f in range(n_fast):
            pick = picks[e][f * part : (f + 1) * part]
            turned = jnp.concatenate(
                [
                    pick[(t * n_mid + m) * run : (t * n_mid + m + 1) * run]
                    for m in range(n_mid)
                    for t in range(n_tp)
                ],
                axis=0,
            )
            left.append(
                lax.dot_general(
                    turned.astype(jnp.bfloat16), second[f][...], dims_of, preferred_element_type=jnp.float32
                )
            )
            right.append(
                lax.dot_general(
                    pick.astype(jnp.bfloat16), first[f][:, :half], dims_of, preferred_element_type=jnp.float32
                )
            )
        left, right = sum(left[1:], left[0]), sum(right[1:], right[0])
        squares = jnp.sum(left * left, axis=1, keepdims=True) + jnp.sum(right * right, axis=1, keepdims=True)
        scale = lax.rsqrt(squares / (2 * half) + 1e-06)
        normed_ref[e, :, :half] = (left * scale * gain[:, :half]).astype(jnp.bfloat16)
        normed_ref[e, :, half:] = (right * scale * gain[:, half:]).astype(jnp.bfloat16)
    swiglu(normed_ref, gates, ups, hidden_ref, 0)


def select_kernel(dims, lead, tail, pos_ref, gain_ref, *refs):
    n_fast = dims[0]
    first, second, refs = refs[:n_fast], refs[n_fast : 2 * n_fast], refs[2 * n_fast :]
    gates, ups, refs = refs[:lead], refs[lead : 2 * lead], refs[2 * lead :]
    _, far_ref, hidden_ref, normed_ref, mix_ref, turned_ref, *near, sems = refs
    copies = load_copies([far_ref] * tail, near, sems, range(lead, lead + tail))

    @pl.when(pos_ref[0] >= 0)
    def _():
        select_body(dims, pos_ref, gain_ref, first, second, gates, ups, hidden_ref, normed_ref, mix_ref, turned_ref)

    for copy in copies:
        copy.wait()


def up_kernel(start, count, wanted, pos_ref, normed_ref, *refs):
    gates, ups, (far_ref, hidden_ref, *near, sems) = refs[:count], refs[count : 2 * count], refs[2 * count :]
    copies = load_copies([far_ref] * len(near), near, sems, wanted)

    @pl.when(pos_ref[0] >= 0)
    def _():
        swiglu(normed_ref, gates, ups, hidden_ref, start)

    for copy in copies:
        copy.wait()


def lower(n_tp, tp_pos, pieces, i, down_ref, columns):
    hid_part = pieces[0].shape[2]
    total = 0.0
    for s in range(n_tp):
        begin = pl.multiple_of(lax.rem(tp_pos - s + n_tp, n_tp) * hid_part, hid_part)
        total = total + jnp.dot(
            pieces[s][i], down_ref[pl.ds(begin, hid_part), columns], preferred_element_type=jnp.float32
        )
    return total.astype(jnp.bfloat16)


def down_kernel(n_tp, pos_ref, *refs):
    pieces, (*downs, out_ref) = refs[:n_tp], refs[n_tp:]
    _, rows, _ = pieces[0].shape
    for i, ref in enumerate(downs):
        out_ref[i * rows : (i + 1) * rows] = lower(n_tp, pos_ref[0], pieces, i, ref, slice(None))


def in_blocks(total, refs):
    rows = refs[0].shape[0]
    for i, ref in enumerate(refs):
        ref[...] = total[i * rows : (i + 1) * rows].astype(jnp.bfloat16)


def mix_kernel(n_tp, count, begin, pos_ref, mix_ref, done_ref, *refs):
    pieces, downs, (*partial_refs, out_ref) = refs[:n_tp], refs[n_tp : n_tp + count], refs[n_tp + count :]
    columns = pl.ds(begin, out_ref.shape[1])
    _, rows, _ = pieces[0].shape
    at = done_ref.shape[0]
    out_ref[:at] = done_ref[:, columns]
    for i, ref in enumerate(downs):
        out_ref[at : at + rows] = lower(n_tp, pos_ref[0], pieces, i, ref, columns)
        at += rows
    out = out_ref[...]
    partial = jnp.dot(mix_ref[0], out, preferred_element_type=jnp.float32)
    partial = partial + jnp.dot(mix_ref[1], out, preferred_element_type=jnp.float32)
    in_blocks(partial, partial_refs)


def total_of(refs):
    return functools.reduce(lambda a, ref: a + ref[...].astype(jnp.float32), refs[1:], refs[0][...].astype(jnp.float32))


def sum_kernel(count, signs, blocks, *refs):
    out_refs = refs[count + signs :]
    in_blocks(total_of(refs[:count]), out_refs[:blocks])
    for ref in out_refs[blocks:]:
        ref[...] = jnp.zeros_like(ref)


def final_kernel(dims, count, pos_ref, first_ref, second_ref, *refs):
    n_mid, n_tp, slow_n, tok_dev, half = dims
    left, right, (out_ref, own_ref) = refs[:count], refs[count:-2], refs[-2:]
    tp_pos = pos_ref[0]
    col_part = out_ref.shape[1]
    for s in range(n_tp):
        at = s * n_mid * slow_n * tok_dev
        own_ref[s * tok_dev : (s + 1) * tok_dev, half:] = first_ref[at : at + tok_dev, :half].astype(jnp.float32)
        at = s * slow_n * tok_dev
        own_ref[s * tok_dev : (s + 1) * tok_dev, :half] = second_ref[at : at + tok_dev].astype(jnp.float32)
    total = jnp.concatenate([total_of(left), total_of(right)], axis=1)
    total = total + own_ref[:, pl.ds(pl.multiple_of(tp_pos * col_part, col_part), col_part)]
    rows = []
    for j in range(n_tp):
        row = total[:tok_dev]
        for s in range(1, n_tp):
            here = lax.rem(tp_pos - s + n_tp, n_tp) == j
            row = jnp.where(here, total[s * tok_dev : (s + 1) * tok_dev], row)
        rows.append(row)
    out_ref[...] = jnp.concatenate(rows, axis=0).astype(jnp.bfloat16)


VMEM = pl.BlockSpec(memory_space=pltpu.VMEM)
SMEM = pl.BlockSpec(memory_space=pltpu.SMEM)
HBM = pl.BlockSpec(memory_space=pltpu.HBM)
KEPT = pltpu.VMEM
TOKEN = jax.ShapeDtypeStruct((8, LANES), jnp.float32)


def local_call(kernel, shapes, operands, far=(), scratch=(), limit=8 << 20, flops=0, moved=0):
    specs, given = [], []
    for i, a in enumerate(operands):
        if i in far:
            specs.append(HBM)
            given.append(pltpu.with_memory_space_constraint(a, pltpu.HBM))
        else:
            specs.append(SMEM if a.dtype == jnp.int32 else VMEM)
            given.append(a)
    return pl.pallas_call(
        kernel,
        out_shape=shapes,
        in_specs=specs,
        out_specs=[VMEM] * len(shapes),
        scratch_shapes=list(scratch),
        compiler_params=pltpu.CompilerParams(vmem_limit_bytes=limit),
        cost_estimate=pl.CostEstimate(flops=flops, bytes_accessed=moved, transcendentals=0),
    )(*given)


def kept(array, count):
    return [KEPT(array.shape[1:], array.dtype)] * count


def runs_of(array):
    return 4 if array.shape[1] % 64 == 0 else 1


def loaded(wanted, after):
    sign, *near = local_call(
        functools.partial(load_kernel, [expert for _, expert in wanted], len(after)),
        [TOKEN] + [KEPT(array.shape[1:], array.dtype) for array, _ in wanted],
        [array for array, _ in wanted] + after,
        far=range(len(wanted)),
        scratch=[pltpu.SemaphoreType.DMA((len(wanted), min(runs_of(array) for array, _ in wanted)))],
        limit=1 << 20,
        moved=2 * sum(array.size // array.shape[0] for array, _ in wanted),
    )
    return near, sign


def summed(pieces, blocks, after, signed):
    rows, columns = pieces[0].shape
    return local_call(
        functools.partial(sum_kernel, len(pieces), len(after), blocks),
        [jax.ShapeDtypeStruct((rows // blocks, columns), pieces[0].dtype)] * blocks + [TOKEN] * signed,
        list(pieces) + after,
        limit=4 << 20,
        moved=2 * (len(pieces) + 1) * rows * columns,
    )


def joined(pieces, after, signed):
    rows, columns = pieces[0].shape
    return local_call(
        functools.partial(join_kernel, len(pieces), len(after)),
        [jax.ShapeDtypeStruct((len(pieces) * rows, columns), pieces[0].dtype)] + [TOKEN] * signed,
        list(pieces) + after,
        limit=4 << 20,
        moved=4 * len(pieces) * rows * columns,
    )


def by_tokens(hidden_in, norm_gain, expert_ids, gate_weights, w_gate, w_up, w_down):
    n_ep = lax.axis_size("ep")
    n_tp = lax.axis_size("tp")
    ep_pos = lax.axis_index("ep")
    tp_pos = lax.axis_index("tp")
    tok_dev, width = hidden_in.shape
    group, top = expert_ids.shape
    exp_loc, _, hid_part = w_gate.shape
    col_part = w_down.shape[2]
    experts = exp_loc * n_ep
    cap = max(2, 2 * top * group // experts)
    rows = cap * n_ep
    tokens = group * n_ep
    digits = factors_of(n_ep)
    fast, mid, slow = digits[0], digits[1:2], digits[2:]
    half = width // 2
    slow_n = n_ep
    for _, radix in [fast] + mid:
        slow_n //= radix
    n_fast, n_mid = fast[1], mid[0][1] if mid else 1

    bf16 = functools.partial(jax.ShapeDtypeStruct, dtype=jnp.bfloat16)
    slots = exp_loc * rows
    lead = exp_loc - exp_loc // 2
    tail = exp_loc - lead
    gain = norm_gain.reshape(1, width)
    position = jnp.stack([tp_pos, ep_pos * exp_loc])
    (message,) = local_call(
        functools.partial(pack_kernel, top),
        [bf16((tok_dev, width + LANES))],
        [position, expert_ids.T, gate_weights.T, hidden_in],
        far=[1, 2, 3],
        scratch=[
            pltpu.VMEM((top, group), jnp.int32),
            pltpu.VMEM((top, group), jnp.float32),
            pltpu.SemaphoreType.DMA((3,)),
        ],
        limit=4 << 20,
    )
    around = [message]
    for digit in reversed(slow):
        around = [a for piece in around for a in arrivals(piece, "ep", n_ep, *digit)]
    gate_lead, sign = loaded([(w_gate, e) for e in range(lead)], [gain])
    first, second, sign = local_call(
        functools.partial(split_kernel, half),
        [bf16((slow_n * tok_dev, width + LANES - half)), bf16((slow_n * tok_dev, half)), TOKEN],
        around + [sign],
        limit=4 << 20,
    )
    gate_tail, sign = loaded([(w_gate, e) for e in range(lead, exp_loc)], [sign])
    along_tp = lambda a: arrivals(a, "tp", n_tp, 1, n_tp)
    along_mid = lambda a: arrivals(a, "ep", n_ep, *mid[0]) if mid else [a]
    first, second = along_mid(first), along_tp(second)
    first, sign = joined(first, [sign], 1)
    (second,) = joined(second, [], 0)
    up_lead, sign = loaded([(w_up, e) for e in range(lead)] + [(w_down, 0)], [sign])
    *up_lead, down_first = up_lead
    first, second = along_tp(first), along_mid(second)
    first, sign = joined(first, [sign], 1)
    down_lead, sign = loaded([(w_down, e) for e in range(1, lead)], [sign]) if lead > 1 else ([], sign)
    down_lead = [down_first] + down_lead
    (second,) = joined(second, [], 0)
    first = arrivals(first, "ep", n_ep, *fast)
    second = arrivals(second, "ep", n_ep, *fast)

    dims = (n_fast, n_mid, n_tp, slow_n, tok_dev, top, exp_loc, rows, half)
    sems = lambda array, count: pltpu.SemaphoreType.DMA((count, runs_of(array)))
    operands = [position, gain] + first + second + gate_lead + up_lead + [sign, w_up]
    hidden, normed, mix, turned, *up_tail = local_call(
        functools.partial(select_kernel, dims, lead, tail),
        [
            bf16((lead, rows, hid_part)),
            bf16((exp_loc, rows, width)),
            bf16((2, tokens, slots)),
            bf16((2, tokens, slots)),
        ]
        + kept(w_up, tail),
        operands,
        far=[len(operands) - 1],
        scratch=[sems(w_up, tail)],
        flops=2 * slots * tokens * width + 4 * lead * rows * width * hid_part,
        moved=4 * lead * width * hid_part,
    )
    pieces = along_tp(hidden)
    operands = [position, normed] + gate_tail + up_tail + [w_down]
    hidden, *down_tail = local_call(
        functools.partial(up_kernel, lead, tail, range(lead, exp_loc)),
        [bf16((tail, rows, hid_part))] + kept(w_down, tail),
        operands,
        far=[len(operands) - 1],
        scratch=[sems(w_down, tail)],
        flops=4 * tail * rows * width * hid_part,
        moved=4 * tail * width * hid_part,
    )
    late = along_tp(hidden)
    (done,) = local_call(
        functools.partial(down_kernel, n_tp),
        [bf16((lead * rows, col_part))],
        [position] + pieces + down_lead,
        flops=2 * lead * rows * n_tp * hid_part * col_part,
        moved=2 * lead * n_tp * hid_part * col_part,
    )
    col_half = col_part // 2
    mixed_of = lambda table, begin: local_call(
        functools.partial(mix_kernel, n_tp, tail, begin),
        [bf16((tokens // n_fast, col_half))] * n_fast,
        [position, table, done] + late + down_tail,
        scratch=[pltpu.VMEM((slots, col_half), jnp.bfloat16)],
        flops=slots * n_tp * hid_part * col_part,
        moved=exp_loc * n_tp * hid_part * col_part,
    )

    def swapped(blocks, digit):
        stride, radix = digit
        return [blocks[0]] + [shifted(blocks[s], "ep", n_ep, stride, radix, radix - s) for s in range(1, radix)]

    slow = list(reversed(slow))
    right_way, left_way = slow + mid, mid + slow
    right = summed(swapped(mixed_of(turned, col_half), fast), right_way[0][1], [], 0)
    left = summed(swapped(mixed_of(mix, 0), fast), left_way[0][1], [], 0)
    signs = []
    for digit, later in zip(left_way[:-1], left_way[1:]):
        *left, sign = summed(swapped(left, digit), later[1], [], 1)
        signs.append(sign)
    for digit, later in zip(right_way[:-1], right_way[1:]):
        right = summed(swapped(right, digit), later[1], signs, 0)
        signs = []
    left = swapped(left, left_way[-1])
    right = swapped(right, right_way[-1])
    (mixed,) = local_call(
        functools.partial(final_kernel, (n_mid, n_tp, slow_n, tok_dev, half), len(left)),
        [bf16((group, col_part))],
        [position, first[0], second[0]] + left + right,
        scratch=[pltpu.VMEM((group, width), jnp.float32)],
        limit=4 << 20,
        moved=2 * group * (width + 6 * col_part),
    )
    return mixed


def by_slots(hidden_in, norm_gain, expert_ids, gate_weights, w_gate, w_up, w_down):
    n_ep = lax.axis_size("ep")
    tp_pos = lax.axis_index("tp")
    tok_dev, width = hidden_in.shape
    group, top = expert_ids.shape
    exp_loc, _, hid_part = w_gate.shape
    col_part = w_down.shape[2]
    experts = exp_loc * n_ep
    cap = max(2, 2 * top * group // experts)
    values = hidden_in.astype(jnp.float32)
    scale = lax.rsqrt(jnp.mean(values * values, axis=1, keepdims=True) + 1e-06)
    normed = (values * scale * norm_gain.astype(jnp.float32)).astype(jnp.bfloat16)
    flat_ids = expert_ids.reshape(-1)
    pairs = flat_ids.shape[0]
    hits = (flat_ids[:, None] == lax.broadcasted_iota(jnp.int32, (pairs, experts), 1)).astype(
        jnp.int32
    )
    before = jnp.cumsum(hits, axis=0) - hits
    position = jnp.sum(before * hits, axis=1)
    slot_index = flat_ids * cap + position
    places = lax.broadcasted_iota(jnp.int32, (experts * cap, group, top), 0)
    dispatch_map = jnp.any(places == slot_index.reshape(group, top)[None], axis=2).astype(
        jnp.bfloat16
    )
    whole_norm, whole_input = (
        lax.all_gather(normed, "tp", axis=0, tiled=True),
        lax.all_gather(hidden_in, "tp", axis=0, tiled=True),
    )
    residual = lax.dynamic_slice_in_dim(whole_input, tp_pos * col_part, col_part, 1)
    packed = jnp.dot(dispatch_map, whole_norm, preferred_element_type=jnp.float32).astype(
        jnp.bfloat16
    )
    packed = packed.reshape(n_ep, exp_loc, cap, width)
    arrived = lax.all_to_all(packed, "ep", split_axis=0, concat_axis=0, tiled=True)
    gate_act = jnp.einsum("secd,edh->sech", arrived, w_gate, preferred_element_type=jnp.float32)
    up_act = jnp.einsum("secd,edh->sech", arrived, w_up, preferred_element_type=jnp.float32)
    hidden = (jax.nn.silu(gate_act) * up_act).astype(jnp.bfloat16)
    outputs = jnp.einsum(
        "sech,ehf->secf",
        lax.all_gather(hidden, "tp", axis=3, tiled=True),
        w_down,
        preferred_element_type=jnp.float32,
    )
    returned = lax.all_to_all(
        outputs.astype(jnp.bfloat16), "ep", split_axis=0, concat_axis=0, tiled=True
    )
    flat_back = returned.reshape(experts * cap, col_part)
    picked = flat_back[slot_index].reshape(group, top, col_part).astype(jnp.float32)
    combined = jnp.sum(picked * gate_weights[:, :, None], axis=1)
    return (residual.astype(jnp.float32) + combined).astype(jnp.bfloat16)


def shards(hidden_in, norm_gain, expert_ids, gate_weights, w_gate, w_up, w_down):
    group, top = expert_ids.shape
    exp_loc = w_gate.shape[0]
    cap = max(2, 2 * top * group // (exp_loc * lax.axis_size("ep")))
    plan = by_tokens if exp_loc > 1 and exp_loc * cap >= group else by_slots
    return plan(hidden_in, norm_gain, expert_ids, gate_weights, w_gate, w_up, w_down)


def solution(mesh):
    in_specs = (
        P(("ep", "tp"), None),
        P(),
        P("ep", None),
        P("ep", None),
        P("ep", None, "tp"),
        P("ep", None, "tp"),
        P("ep", None, "tp"),
    )
    out_specs = P("ep", "tp")
    return jax.shard_map(shards, mesh=mesh, in_specs=in_specs, out_specs=out_specs, check_vma=False)
```

```python
import functools

import jax
import jax.numpy as jnp
from jax import lax
from jax.experimental import pallas as pl
from jax.experimental.pallas import tpu as pltpu
from jax.sharding import PartitionSpec as P

LANES = 128


def factors_of(n):
    digits, stride = [], 1
    for _ in range(2):
        if n % 2 == 0 and n > 1:
            digits.append((stride, 2))
            stride, n = stride * 2, n // 2
    while n > 1:
        radix = next(r for r in (4, 3, 2, n) if n % r == 0)
        digits.append((stride, radix))
        stride, n = stride * radix, n // radix
    return digits


def shifted(x, axis, size, stride, radix, by):
    pairs = []
    for i in range(size):
        digit = i // stride % radix
        pairs.append((i, i + ((digit + by) % radix - digit) * stride))
    return lax.ppermute(x, axis, pairs)


def arrivals(x, axis, size, stride, radix):
    return [x] + [shifted(x, axis, size, stride, radix, s) for s in range(1, radix)]


def pack_kernel(top, pos_ref, ids_ref, weights_ref, values_ref, message_ref, ids, weights, sems):
    tok_dev, width = values_ref.shape
    copies = [
        pltpu.make_async_copy(ids_ref, ids, sems.at[0]),
        pltpu.make_async_copy(weights_ref, weights, sems.at[1]),
        pltpu.make_async_copy(values_ref, message_ref.at[:, pl.ds(0, width)], sems.at[2]),
    ]
    for copy in copies:
        copy.start()
    copies[0].wait()
    copies[1].wait()
    group = ids.shape[1]
    high = weights[...].astype(jnp.bfloat16).astype(jnp.float32)
    rest = weights[...] - high
    mid = rest.astype(jnp.bfloat16).astype(jnp.float32)
    terms = [ids[...].astype(jnp.float32), high, mid, rest - mid]
    terms.append(jnp.zeros((LANES - 4 * top, group), jnp.float32))
    table = jnp.concatenate(terms, axis=0).astype(jnp.bfloat16)
    own = lax.broadcasted_iota(jnp.int32, (tok_dev, group), 0) + pos_ref[0] * tok_dev
    own = (own == lax.broadcasted_iota(jnp.int32, (tok_dev, group), 1)).astype(jnp.float32)
    routing = lax.dot_general(
        own.astype(jnp.bfloat16), table, (((1,), (1,)), ((), ())), preferred_element_type=jnp.float32
    )
    message_ref[:, width:] = routing.astype(jnp.bfloat16)
    copies[2].wait()


def split_kernel(half, *refs):
    pieces, (first_ref, second_ref, token_ref) = refs[:-3], refs[-3:]
    pieces = [ref for ref in pieces if ref.shape[1] > 2 * half]
    whole = jnp.concatenate([ref[...].astype(jnp.float32) for ref in pieces], axis=0).astype(jnp.bfloat16)
    second_ref[...] = whole[:, :half]
    first_ref[...] = whole[:, half:]
    token_ref[...] = jnp.zeros_like(token_ref)


def join_kernel(count, signs, *refs):
    out_ref = refs[count + signs]
    rows = refs[0].shape[0]
    for i, ref in enumerate(refs[:count]):
        out_ref[i * rows : (i + 1) * rows] = ref[...]
    for ref in refs[count + signs + 1 :]:
        ref[...] = jnp.zeros_like(ref)


def load_kernel(experts, signs, *refs):
    count = len(experts)
    refs = refs[:count] + refs[count + signs :]
    far, (sign_ref, *near, sems) = refs[:count], refs[count:]
    copies = load_copies(far, near, sems, experts)
    sign_ref[...] = jnp.zeros_like(sign_ref)
    for copy in copies:
        copy.wait()


def load_copies(far, near, sems, experts):
    copies = []
    for i, (src_ref, dst_ref, expert) in enumerate(zip(far, near, experts)):
        runs = sems.shape[1]
        size = dst_ref.shape[0] // runs
        for r in range(runs):
            at = pl.ds(r * size, size)
            copies.append(pltpu.make_async_copy(src_ref.at[expert, at], dst_ref.at[at], sems.at[i, r]))
    for copy in copies:
        copy.start()
    return copies


def swiglu(normed_ref, gates, ups, hidden_ref, start):
    for i, (gate_ref, up_ref) in enumerate(zip(gates, ups)):
        x = normed_ref[start + i]
        gate_act = jnp.dot(x, gate_ref[...], preferred_element_type=jnp.float32)
        up_act = jnp.dot(x, up_ref[...], preferred_element_type=jnp.float32)
        hidden_ref[i] = (gate_act / (1.0 + jnp.exp(-gate_act)) * up_act).astype(jnp.bfloat16)


def select_body(dims, pos_ref, gain_ref, first, second, gates, ups, hidden_ref, normed_ref, mix_ref, turned_ref):
    n_fast, n_mid, n_tp, slow_n, tok_dev, top, exp_loc, rows, half = dims
    tp_pos, base = pos_ref[0], pos_ref[1]
    run = slow_n * tok_dev
    tokens = n_fast * n_mid * n_tp * run
    routing = jnp.concatenate([ref[:, half:] for ref in first], axis=0).astype(jnp.float32)
    ids = routing[:, :top]
    weights = routing[:, top : 2 * top] + (
        routing[:, 2 * top : 3 * top] + routing[:, 3 * top : 4 * top]
    )

    def number(shape, dim):
        at = lax.broadcasted_iota(jnp.int32, shape, dim)
        tp_at = lax.rem(lax.div(at, n_mid * run), n_tp)
        return at + (lax.rem(tp_pos - tp_at + n_tp, n_tp) - tp_at) * (n_mid * run)

    before = number((tokens, tokens), 1) < number((tokens, tokens), 0)
    match = [ids == (base + e).astype(jnp.float32) for e in range(exp_loc)]
    hits = [jnp.sum(m.astype(jnp.float32), axis=1, keepdims=True) for m in match]
    shares = [jnp.sum(jnp.where(m, weights, 0.0), axis=1, keepdims=True) for m in match]
    lane = lax.broadcasted_iota(jnp.int32, (tokens, LANES), 1)
    hit = functools.reduce(
        lambda a, e: jnp.where(lane == e, hits[e], a),
        range(exp_loc),
        jnp.zeros((tokens, LANES), jnp.float32),
    )
    position = jnp.dot(
        before.astype(jnp.float32).astype(jnp.bfloat16),
        hit.astype(jnp.bfloat16),
        preferred_element_type=jnp.float32,
    )
    slot = lax.broadcasted_iota(jnp.int32, (tokens, rows), 1).astype(jnp.float32)
    picks, spreads = [], []
    for e in range(exp_loc):
        place = jnp.where(hits[e] > 0, position[:, e : e + 1], -1.0)
        pick = slot == place
        picks.append(pick.astype(jnp.float32))
        spreads.append(jnp.where(pick, shares[e], 0.0))
    spread = jnp.concatenate(spreads, axis=1)
    group = lambda f, m, s: [
        spread[start : start + tok_dev]
        for start in [(((f * n_tp + t) * n_mid + m) * slow_n + s) * tok_dev for t in range(n_tp)]
    ]
    blocks = [b for f in range(n_fast) for m in range(n_mid) for s in range(slow_n) for b in group(f, m, s)]
    turned = [b for f in range(n_fast) for s in range(slow_n) for m in range(n_mid) for b in group(f, m, s)]
    for ref, rows_of in ((mix_ref, blocks), (turned_ref, turned)):
        exact = jnp.concatenate(rows_of, axis=0)
        high = exact.astype(jnp.bfloat16)
        ref[0] = high
        ref[1] = (exact - high.astype(jnp.float32)).astype(jnp.bfloat16)

    part = n_mid * n_tp * run
    pick = jnp.concatenate(picks, axis=1)
    chosen, swapped = [], []
    for f in range(n_fast):
        own = pick[f * part : (f + 1) * part]
        runs = [
            own[(t * n_mid + m) * run : (t * n_mid + m + 1) * run] for m in range(n_mid) for t in range(n_tp)
        ]
        chosen.append(own.T.astype(jnp.bfloat16))
        swapped.append(jnp.concatenate(runs, axis=0).T.astype(jnp.bfloat16))
    size = min(half, 4 * LANES)
    squares = 0.0
    for begin in range(0, 2 * half, size):
        table, side, at = (swapped, second, begin) if begin < half else (chosen, first, begin - half)
        values = 0.0
        for f in range(n_fast):
            values = values + jnp.dot(table[f], side[f][:, at : at + size], preferred_element_type=jnp.float32)
        squares = squares + jnp.sum(values * values, axis=1, keepdims=True)
        values = values.astype(jnp.bfloat16)
        for e in range(exp_loc):
            normed_ref[e, :, begin : begin + size] = values[e * rows : (e + 1) * rows]
    scale = lax.rsqrt(squares / (2 * half) + 1e-06)
    for begin in range(0, 2 * half, size):
        gain = gain_ref[:, begin : begin + size].astype(jnp.float32)
        for e in range(exp_loc):
            values = normed_ref[e, :, begin : begin + size].astype(jnp.float32)
            values = values * scale[e * rows : (e + 1) * rows] * gain
            normed_ref[e, :, begin : begin + size] = values.astype(jnp.bfloat16)
    swiglu(normed_ref, gates, ups, hidden_ref, 0)


def select_kernel(dims, lead, tail, pos_ref, gain_ref, *refs):
    n_fast = dims[0]
    first, second, refs = refs[:n_fast], refs[n_fast : 2 * n_fast], refs[2 * n_fast :]
    gates, ups, refs = refs[:lead], refs[lead : 2 * lead], refs[2 * lead :]
    _, far_ref, hidden_ref, normed_ref, mix_ref, turned_ref, *near, sems = refs
    copies = load_copies([far_ref] * tail, near, sems, range(lead, lead + tail))

    @pl.when(pos_ref[0] >= 0)
    def _():
        select_body(dims, pos_ref, gain_ref, first, second, gates, ups, hidden_ref, normed_ref, mix_ref, turned_ref)

    for copy in copies:
        copy.wait()


def up_kernel(start, count, wanted, pos_ref, normed_ref, *refs):
    gates, ups, (far_ref, hidden_ref, *near, sems) = refs[:count], refs[count : 2 * count], refs[2 * count :]
    copies = load_copies([far_ref] * len(near), near, sems, wanted)

    @pl.when(pos_ref[0] >= 0)
    def _():
        swiglu(normed_ref, gates, ups, hidden_ref, start)

    for copy in copies:
        copy.wait()


def lower(tp_pos, n_tp, piece, s, down_ref, columns):
    hid_part = piece.shape[1]
    begin = pl.multiple_of(lax.rem(tp_pos - s + n_tp, n_tp) * hid_part, hid_part)
    return jnp.dot(piece, down_ref[pl.ds(begin, hid_part), columns], preferred_element_type=jnp.float32)


def down_kernel(n_tp, count, pos_ref, own_ref, *refs):
    pieces, (*downs, out_ref, part_ref) = refs[:n_tp], refs[n_tp:]
    _, rows, _ = own_ref.shape
    every = slice(None)
    for i, ref in enumerate(downs[:count]):
        total = sum(lower(pos_ref[0], n_tp, pieces[s][i], s, ref, every) for s in range(n_tp))
        out_ref[i * rows : (i + 1) * rows] = total.astype(jnp.bfloat16)
    for i, ref in enumerate(downs[count:]):
        part_ref[i * rows : (i + 1) * rows] = lower(pos_ref[0], n_tp, own_ref[i], 0, ref, every)


def in_blocks(total, refs):
    rows = refs[0].shape[0]
    for i, ref in enumerate(refs):
        ref[...] = total[i * rows : (i + 1) * rows].astype(jnp.bfloat16)


def mix_kernel(n_tp, count, begin, pos_ref, mix_ref, done_ref, part_ref, *refs):
    pieces, refs = refs[: n_tp - 1], refs[n_tp - 1 :]
    downs, (*partial_refs, out_ref) = refs[:count], refs[count:]
    columns = pl.ds(begin, out_ref.shape[1])
    at = done_ref.shape[0]
    rows = part_ref.shape[0] // count
    out_ref[:at] = done_ref[:, columns]
    for i, ref in enumerate(downs):
        total = part_ref[i * rows : (i + 1) * rows, columns]
        for s in range(1, n_tp):
            total = total + lower(pos_ref[0], n_tp, pieces[s - 1][i], s, ref, columns)
        out_ref[at + i * rows : at + (i + 1) * rows] = total.astype(jnp.bfloat16)
    out = out_ref[...]
    partial = jnp.dot(mix_ref[0], out, preferred_element_type=jnp.float32)
    partial = partial + jnp.dot(mix_ref[1], out, preferred_element_type=jnp.float32)
    in_blocks(partial, partial_refs)


def total_of(refs):
    return functools.reduce(lambda a, ref: a + ref[...].astype(jnp.float32), refs[1:], refs[0][...].astype(jnp.float32))


def sum_kernel(count, signs, blocks, *refs):
    out_refs = refs[count + signs :]
    in_blocks(total_of(refs[:count]), out_refs[:blocks])
    for ref in out_refs[blocks:]:
        ref[...] = jnp.zeros_like(ref)


def final_kernel(dims, count, pos_ref, first_ref, second_ref, *refs):
    n_mid, n_tp, slow_n, tok_dev, half = dims
    left, right, (out_ref, own_ref) = refs[:count], refs[count:-2], refs[-2:]
    tp_pos = pos_ref[0]
    col_part = out_ref.shape[1]
    for s in range(n_tp):
        at = s * n_mid * slow_n * tok_dev
        own_ref[s * tok_dev : (s + 1) * tok_dev, half:] = first_ref[at : at + tok_dev, :half].astype(jnp.float32)
        at = s * slow_n * tok_dev
        own_ref[s * tok_dev : (s + 1) * tok_dev, :half] = second_ref[at : at + tok_dev].astype(jnp.float32)
    total = jnp.concatenate([total_of(left), total_of(right)], axis=1)
    total = total + own_ref[:, pl.ds(pl.multiple_of(tp_pos * col_part, col_part), col_part)]
    rows = []
    for j in range(n_tp):
        row = total[:tok_dev]
        for s in range(1, n_tp):
            here = lax.rem(tp_pos - s + n_tp, n_tp) == j
            row = jnp.where(here, total[s * tok_dev : (s + 1) * tok_dev], row)
        rows.append(row)
    out_ref[...] = jnp.concatenate(rows, axis=0).astype(jnp.bfloat16)


VMEM = pl.BlockSpec(memory_space=pltpu.VMEM)
SMEM = pl.BlockSpec(memory_space=pltpu.SMEM)
HBM = pl.BlockSpec(memory_space=pltpu.HBM)
KEPT = pltpu.VMEM
TOKEN = jax.ShapeDtypeStruct((8, LANES), jnp.float32)


def local_call(kernel, shapes, operands, far=(), scratch=(), limit=6 << 20, flops=0, moved=0):
    specs, given = [], []
    for i, a in enumerate(operands):
        if i in far:
            specs.append(HBM)
            given.append(pltpu.with_memory_space_constraint(a, pltpu.HBM))
        else:
            specs.append(SMEM if a.dtype == jnp.int32 else VMEM)
            given.append(a)
    return pl.pallas_call(
        kernel,
        out_shape=shapes,
        in_specs=specs,
        out_specs=[VMEM] * len(shapes),
        scratch_shapes=list(scratch),
        compiler_params=pltpu.CompilerParams(vmem_limit_bytes=limit),
        cost_estimate=pl.CostEstimate(flops=flops, bytes_accessed=moved, transcendentals=0),
    )(*given)


def kept(array, count):
    return [KEPT(array.shape[1:], array.dtype)] * count


def runs_of(array):
    return 4 if array.shape[1] % 64 == 0 else 1


def loaded(wanted, after):
    sign, *near = local_call(
        functools.partial(load_kernel, [expert for _, expert in wanted], len(after)),
        [TOKEN] + [KEPT(array.shape[1:], array.dtype) for array, _ in wanted],
        [array for array, _ in wanted] + after,
        far=range(len(wanted)),
        scratch=[pltpu.SemaphoreType.DMA((len(wanted), min(runs_of(array) for array, _ in wanted)))],
        limit=1 << 20,
        moved=2 * sum(array.size // array.shape[0] for array, _ in wanted),
    )
    return near, sign


def summed(pieces, blocks, after, signed):
    rows, columns = pieces[0].shape
    return local_call(
        functools.partial(sum_kernel, len(pieces), len(after), blocks),
        [jax.ShapeDtypeStruct((rows // blocks, columns), pieces[0].dtype)] * blocks + [TOKEN] * signed,
        list(pieces) + after,
        limit=4 << 20,
        moved=2 * (len(pieces) + 1) * rows * columns,
    )


def joined(pieces, after, signed):
    rows, columns = pieces[0].shape
    return local_call(
        functools.partial(join_kernel, len(pieces), len(after)),
        [jax.ShapeDtypeStruct((len(pieces) * rows, columns), pieces[0].dtype)] + [TOKEN] * signed,
        list(pieces) + after,
        limit=4 << 20,
        moved=4 * len(pieces) * rows * columns,
    )


def by_tokens(hidden_in, norm_gain, expert_ids, gate_weights, w_gate, w_up, w_down):
    n_ep = lax.axis_size("ep")
    n_tp = lax.axis_size("tp")
    ep_pos = lax.axis_index("ep")
    tp_pos = lax.axis_index("tp")
    tok_dev, width = hidden_in.shape
    group, top = expert_ids.shape
    exp_loc, _, hid_part = w_gate.shape
    col_part = w_down.shape[2]
    experts = exp_loc * n_ep
    cap = max(2, 2 * top * group // experts)
    rows = cap * n_ep
    tokens = group * n_ep
    digits = factors_of(n_ep)
    fast, mid, slow = digits[0], digits[1:2], digits[2:]
    half = width // 2
    slow_n = n_ep
    for _, radix in [fast] + mid:
        slow_n //= radix
    n_fast, n_mid = fast[1], mid[0][1] if mid else 1

    bf16 = functools.partial(jax.ShapeDtypeStruct, dtype=jnp.bfloat16)
    slots = exp_loc * rows
    lead = exp_loc - exp_loc // 2
    tail = exp_loc - lead
    gain = norm_gain.reshape(1, width)
    position = jnp.stack([tp_pos, ep_pos * exp_loc])
    (message,) = local_call(
        functools.partial(pack_kernel, top),
        [bf16((tok_dev, width + LANES))],
        [position, expert_ids.T, gate_weights.T, hidden_in],
        far=[1, 2, 3],
        scratch=[
            pltpu.VMEM((top, group), jnp.int32),
            pltpu.VMEM((top, group), jnp.float32),
            pltpu.SemaphoreType.DMA((3,)),
        ],
        limit=4 << 20,
    )
    around = [message]
    for digit in reversed(slow):
        around = [a for piece in around for a in arrivals(piece, "ep", n_ep, *digit)]
    gate_lead, sign = loaded([(w_gate, e) for e in range(lead)], [gain])
    first, second, sign = local_call(
        functools.partial(split_kernel, half),
        [bf16((slow_n * tok_dev, width + LANES - half)), bf16((slow_n * tok_dev, half)), TOKEN],
        around + [sign],
        limit=4 << 20,
    )
    gate_tail, sign = loaded([(w_gate, e) for e in range(lead, exp_loc)], [sign])
    along_tp = lambda a: arrivals(a, "tp", n_tp, 1, n_tp)
    along_mid = lambda a: arrivals(a, "ep", n_ep, *mid[0]) if mid else [a]
    first, second = along_mid(first), along_tp(second)
    first, sign = joined(first, [sign], 1)
    (second,) = joined(second, [], 0)
    up_lead, sign = loaded([(w_up, e) for e in range(lead)] + [(w_down, 0)], [sign])
    *up_lead, down_first = up_lead
    first, second = along_tp(first), along_mid(second)
    first, sign = joined(first, [sign], 1)
    down_lead, sign = loaded([(w_down, e) for e in range(1, lead)], [sign]) if lead > 1 else ([], sign)
    down_lead = [down_first] + down_lead
    (second,) = joined(second, [], 0)
    first = arrivals(first, "ep", n_ep, *fast)
    second = arrivals(second, "ep", n_ep, *fast)

    dims = (n_fast, n_mid, n_tp, slow_n, tok_dev, top, exp_loc, rows, half)
    sems = lambda array, count: pltpu.SemaphoreType.DMA((count, runs_of(array)))
    operands = [position, gain] + first + second + gate_lead + up_lead + [sign, w_up]
    hidden, normed, mix, turned, *up_tail = local_call(
        functools.partial(select_kernel, dims, lead, tail),
        [
            bf16((lead, rows, hid_part)),
            bf16((exp_loc, rows, width)),
            bf16((2, tokens, slots)),
            bf16((2, tokens, slots)),
        ]
        + kept(w_up, tail),
        operands,
        far=[len(operands) - 1],
        scratch=[sems(w_up, tail)],
        flops=2 * slots * tokens * width + 4 * lead * rows * width * hid_part,
        moved=4 * lead * width * hid_part,
    )
    pieces = along_tp(hidden)
    operands = [position, normed] + gate_tail + up_tail + [w_down]
    hidden, *down_tail = local_call(
        functools.partial(up_kernel, lead, tail, range(lead, exp_loc)),
        [bf16((tail, rows, hid_part))] + kept(w_down, tail),
        operands,
        far=[len(operands) - 1],
        scratch=[sems(w_down, tail)],
        flops=4 * tail * rows * width * hid_part,
        moved=4 * tail * width * hid_part,
    )
    late = along_tp(hidden)
    done, part = local_call(
        functools.partial(down_kernel, n_tp, lead),
        [bf16((lead * rows, col_part)), jax.ShapeDtypeStruct((tail * rows, col_part), jnp.float32)],
        [position, late[0]] + pieces + down_lead + down_tail,
        flops=2 * lead * rows * n_tp * hid_part * col_part,
        moved=2 * lead * n_tp * hid_part * col_part,
    )
    col_half = col_part // 2
    mixed_of = lambda table, begin: local_call(
        functools.partial(mix_kernel, n_tp, tail, begin),
        [bf16((tokens // n_fast, col_half))] * n_fast,
        [position, table, done, part] + late[1:] + down_tail,
        scratch=[pltpu.VMEM((slots, col_half), jnp.bfloat16)],
        flops=slots * n_tp * hid_part * col_part,
        moved=exp_loc * n_tp * hid_part * col_part,
    )

    def swapped(blocks, digit):
        stride, radix = digit
        return [blocks[0]] + [shifted(blocks[s], "ep", n_ep, stride, radix, radix - s) for s in range(1, radix)]

    slow = list(reversed(slow))
    right_way, left_way = slow + mid, mid + slow
    right = summed(swapped(mixed_of(turned, col_half), fast), right_way[0][1], [], 0)
    left = summed(swapped(mixed_of(mix, 0), fast), left_way[0][1], [], 0)
    signs = []
    for digit, later in zip(left_way[:-1], left_way[1:]):
        *left, sign = summed(swapped(left, digit), later[1], [], 1)
        signs.append(sign)
    for digit, later in zip(right_way[:-1], right_way[1:]):
        right = summed(swapped(right, digit), later[1], signs, 0)
        signs = []
    left = swapped(left, left_way[-1])
    right = swapped(right, right_way[-1])
    (mixed,) = local_call(
        functools.partial(final_kernel, (n_mid, n_tp, slow_n, tok_dev, half), len(left)),
        [bf16((group, col_part))],
        [position, first[0], second[0]] + left + right,
        scratch=[pltpu.VMEM((group, width), jnp.float32)],
        limit=4 << 20,
        moved=2 * group * (width + 6 * col_part),
    )
    return mixed


def by_slots(hidden_in, norm_gain, expert_ids, gate_weights, w_gate, w_up, w_down):
    n_ep = lax.axis_size("ep")
    tp_pos = lax.axis_index("tp")
    tok_dev, width = hidden_in.shape
    group, top = expert_ids.shape
    exp_loc, _, hid_part = w_gate.shape
    col_part = w_down.shape[2]
    experts = exp_loc * n_ep
    cap = max(2, 2 * top * group // experts)
    values = hidden_in.astype(jnp.float32)
    scale = lax.rsqrt(jnp.mean(values * values, axis=1, keepdims=True) + 1e-06)
    normed = (values * scale * norm_gain.astype(jnp.float32)).astype(jnp.bfloat16)
    flat_ids = expert_ids.reshape(-1)
    pairs = flat_ids.shape[0]
    hits = (flat_ids[:, None] == lax.broadcasted_iota(jnp.int32, (pairs, experts), 1)).astype(
        jnp.int32
    )
    before = jnp.cumsum(hits, axis=0) - hits
    position = jnp.sum(before * hits, axis=1)
    slot_index = flat_ids * cap + position
    places = lax.broadcasted_iota(jnp.int32, (experts * cap, group, top), 0)
    dispatch_map = jnp.any(places == slot_index.reshape(group, top)[None], axis=2).astype(
        jnp.bfloat16
    )
    whole_norm, whole_input = (
        lax.all_gather(normed, "tp", axis=0, tiled=True),
        lax.all_gather(hidden_in, "tp", axis=0, tiled=True),
    )
    residual = lax.dynamic_slice_in_dim(whole_input, tp_pos * col_part, col_part, 1)
    packed = jnp.dot(dispatch_map, whole_norm, preferred_element_type=jnp.float32).astype(
        jnp.bfloat16
    )
    packed = packed.reshape(n_ep, exp_loc, cap, width)
    arrived = lax.all_to_all(packed, "ep", split_axis=0, concat_axis=0, tiled=True)
    gate_act = jnp.einsum("secd,edh->sech", arrived, w_gate, preferred_element_type=jnp.float32)
    up_act = jnp.einsum("secd,edh->sech", arrived, w_up, preferred_element_type=jnp.float32)
    hidden = (jax.nn.silu(gate_act) * up_act).astype(jnp.bfloat16)
    outputs = jnp.einsum(
        "sech,ehf->secf",
        lax.all_gather(hidden, "tp", axis=3, tiled=True),
        w_down,
        preferred_element_type=jnp.float32,
    )
    returned = lax.all_to_all(
        outputs.astype(jnp.bfloat16), "ep", split_axis=0, concat_axis=0, tiled=True
    )
    flat_back = returned.reshape(experts * cap, col_part)
    picked = flat_back[slot_index].reshape(group, top, col_part).astype(jnp.float32)
    combined = jnp.sum(picked * gate_weights[:, :, None], axis=1)
    return (residual.astype(jnp.float32) + combined).astype(jnp.bfloat16)


def shards(hidden_in, norm_gain, expert_ids, gate_weights, w_gate, w_up, w_down):
    group, top = expert_ids.shape
    exp_loc = w_gate.shape[0]
    cap = max(2, 2 * top * group // (exp_loc * lax.axis_size("ep")))
    plan = by_tokens if exp_loc > 1 and exp_loc * cap >= group else by_slots
    return plan(hidden_in, norm_gain, expert_ids, gate_weights, w_gate, w_up, w_down)


def solution(mesh):
    in_specs = (
        P(("ep", "tp"), None),
        P(),
        P("ep", None),
        P("ep", None),
        P("ep", None, "tp"),
        P("ep", None, "tp"),
        P("ep", None, "tp"),
    )
    out_specs = P("ep", "tp")
    return jax.shard_map(shards, mesh=mesh, in_specs=in_specs, out_specs=out_specs, check_vma=False)
```

```python
import functools

import jax
import jax.numpy as jnp
from jax import lax
from jax.experimental import pallas as pl
from jax.experimental.pallas import tpu as pltpu
from jax.sharding import PartitionSpec as P

LANES = 128


def factors_of(n):
    digits, stride = [], 1
    for _ in range(2):
        if n % 2 == 0 and n > 1:
            digits.append((stride, 2))
            stride, n = stride * 2, n // 2
    while n > 1:
        radix = next(r for r in (4, 3, 2, n) if n % r == 0)
        digits.append((stride, radix))
        stride, n = stride * radix, n // radix
    return digits


def shifted(x, axis, size, stride, radix, by):
    pairs = []
    for i in range(size):
        digit = i // stride % radix
        pairs.append((i, i + ((digit + by) % radix - digit) * stride))
    return lax.ppermute(x, axis, pairs)


def arrivals(x, axis, size, stride, radix):
    return [x] + [shifted(x, axis, size, stride, radix, s) for s in range(1, radix)]


def pack_kernel(top, pos_ref, ids_ref, weights_ref, values_ref, message_ref, ids, weights, sems):
    tok_dev, width = values_ref.shape
    copies = [
        pltpu.make_async_copy(ids_ref, ids, sems.at[0]),
        pltpu.make_async_copy(weights_ref, weights, sems.at[1]),
    ] + [
        pltpu.make_async_copy(values_ref, message_ref.at[k, :, pl.ds(0, width)], sems.at[2 + k])
        for k in range(message_ref.shape[0])
    ]
    for copy in copies:
        copy.start()
    copies[0].wait()
    copies[1].wait()
    group = ids.shape[1]
    high = weights[...].astype(jnp.bfloat16).astype(jnp.float32)
    rest = weights[...] - high
    mid = rest.astype(jnp.bfloat16).astype(jnp.float32)
    terms = [ids[...].astype(jnp.float32), high, mid, rest - mid]
    terms.append(jnp.zeros((LANES - 4 * top, group), jnp.float32))
    table = jnp.concatenate(terms, axis=0).astype(jnp.bfloat16)
    own = lax.broadcasted_iota(jnp.int32, (tok_dev, group), 0) + pos_ref[0] * tok_dev
    own = (own == lax.broadcasted_iota(jnp.int32, (tok_dev, group), 1)).astype(jnp.float32)
    routing = lax.dot_general(
        own.astype(jnp.bfloat16), table, (((1,), (1,)), ((), ())), preferred_element_type=jnp.float32
    )
    for k in range(message_ref.shape[0]):
        message_ref[k, :, width:] = routing.astype(jnp.bfloat16)
    for copy in copies[2:]:
        copy.wait()


def split_kernel(half, whole_ref, sign_ref, first_ref, second_ref, token_ref):
    pieces = [whole_ref[k].astype(jnp.float32) for k in range(whole_ref.shape[0])]
    whole = jnp.concatenate(pieces, axis=0).astype(jnp.bfloat16)
    second_ref[...] = whole[:, :half]
    first_ref[...] = whole[:, half:]
    token_ref[...] = jnp.zeros_like(token_ref)


def join_kernel(count, signs, *refs):
    out_ref = refs[count + signs]
    rows = refs[0].shape[0]
    for i, ref in enumerate(refs[:count]):
        out_ref[i * rows : (i + 1) * rows] = ref[...]
    for ref in refs[count + signs + 1 :]:
        ref[...] = jnp.zeros_like(ref)


def load_kernel(experts, signs, *refs):
    count = len(experts)
    refs = refs[:count] + refs[count + signs :]
    far, (sign_ref, *near, sems) = refs[:count], refs[count:]
    copies = load_copies(far, near, sems, experts)
    sign_ref[...] = jnp.zeros_like(sign_ref)
    for copy in copies:
        copy.wait()


def load_copies(far, near, sems, experts):
    copies = []
    for i, (src_ref, dst_ref, expert) in enumerate(zip(far, near, experts)):
        runs = sems.shape[1]
        size = dst_ref.shape[0] // runs
        for r in range(runs):
            at = pl.ds(r * size, size)
            copies.append(pltpu.make_async_copy(src_ref.at[expert, at], dst_ref.at[at], sems.at[i, r]))
    for copy in copies:
        copy.start()
    return copies


def swiglu(normed_ref, gates, ups, hidden_ref, start):
    for i, (gate_ref, up_ref) in enumerate(zip(gates, ups)):
        x = normed_ref[start + i]
        gate_act = jnp.dot(x, gate_ref[...], preferred_element_type=jnp.float32)
        up_act = jnp.dot(x, up_ref[...], preferred_element_type=jnp.float32)
        hidden_ref[i] = (gate_act / (1.0 + jnp.exp(-gate_act)) * up_act).astype(jnp.bfloat16)


def select_body(dims, pos_ref, gain_ref, first, second, gates, ups, hidden_ref, normed_ref, mix_ref, turned_ref):
    n_fast, n_mid, n_tp, slow_n, tok_dev, top, exp_loc, rows, half = dims
    tp_pos, base = pos_ref[0], pos_ref[1]
    run = slow_n * tok_dev
    tokens = n_fast * n_mid * n_tp * run
    routing = jnp.concatenate([ref[:, half:] for ref in first], axis=0).astype(jnp.float32)
    ids = routing[:, :top]
    weights = routing[:, top : 2 * top] + (
        routing[:, 2 * top : 3 * top] + routing[:, 3 * top : 4 * top]
    )

    def number(shape, dim):
        at = lax.broadcasted_iota(jnp.int32, shape, dim)
        tp_at = lax.rem(lax.div(at, n_mid * run), n_tp)
        return at + (lax.rem(tp_pos - tp_at + n_tp, n_tp) - tp_at) * (n_mid * run)

    before = number((tokens, tokens), 1) < number((tokens, tokens), 0)
    match = [ids == (base + e).astype(jnp.float32) for e in range(exp_loc)]
    hits = [jnp.sum(m.astype(jnp.float32), axis=1, keepdims=True) for m in match]
    shares = [jnp.sum(jnp.where(m, weights, 0.0), axis=1, keepdims=True) for m in match]
    lane = lax.broadcasted_iota(jnp.int32, (tokens, LANES), 1)
    hit = functools.reduce(
        lambda a, e: jnp.where(lane == e, hits[e], a),
        range(exp_loc),
        jnp.zeros((tokens, LANES), jnp.float32),
    )
    position = jnp.dot(
        before.astype(jnp.float32).astype(jnp.bfloat16),
        hit.astype(jnp.bfloat16),
        preferred_element_type=jnp.float32,
    )
    slot = lax.broadcasted_iota(jnp.int32, (tokens, rows), 1).astype(jnp.float32)
    picks, spreads = [], []
    for e in range(exp_loc):
        place = jnp.where(hits[e] > 0, position[:, e : e + 1], -1.0)
        pick = slot == place
        picks.append(pick.astype(jnp.float32))
        spreads.append(jnp.where(pick, shares[e], 0.0))
    spread = jnp.concatenate(spreads, axis=1)
    group = lambda f, m, s: [
        spread[start : start + tok_dev]
        for start in [(((f * n_tp + t) * n_mid + m) * slow_n + s) * tok_dev for t in range(n_tp)]
    ]
    blocks = [b for f in range(n_fast) for m in range(n_mid) for s in range(slow_n) for b in group(f, m, s)]
    turned = [b for f in range(n_fast) for s in range(slow_n) for m in range(n_mid) for b in group(f, m, s)]
    for ref, rows_of in ((mix_ref, blocks), (turned_ref, turned)):
        exact = jnp.concatenate(rows_of, axis=0)
        high = exact.astype(jnp.bfloat16)
        ref[0] = high
        ref[1] = (exact - high.astype(jnp.float32)).astype(jnp.bfloat16)

    part = n_mid * n_tp * run
    pick = jnp.concatenate(picks, axis=1)
    swapped = jnp.concatenate(
        [
            pick[f * part + (t * n_mid + m) * run : f * part + (t * n_mid + m + 1) * run]
            for f in range(n_fast)
            for m in range(n_mid)
            for t in range(n_tp)
        ],
        axis=0,
    )
    chosen, swapped = pick.T.astype(jnp.bfloat16), swapped.T.astype(jnp.bfloat16)
    size = min(half, 4 * LANES)
    squares = 0.0
    for begin in range(0, 2 * half, size):
        table, side, at = (swapped, second, begin) if begin < half else (chosen, first, begin - half)
        values = jnp.concatenate([ref[:, at : at + size] for ref in side], axis=0)
        values = jnp.dot(table, values, preferred_element_type=jnp.float32)
        squares = squares + jnp.sum(values * values, axis=1, keepdims=True)
        values = values.astype(jnp.bfloat16)
        for e in range(exp_loc):
            normed_ref[e, :, begin : begin + size] = values[e * rows : (e + 1) * rows]
    scale = lax.rsqrt(squares / (2 * half) + 1e-06)
    for begin in range(0, 2 * half, size):
        gain = gain_ref[:, begin : begin + size].astype(jnp.float32)
        for e in range(exp_loc):
            values = normed_ref[e, :, begin : begin + size].astype(jnp.float32)
            values = values * scale[e * rows : (e + 1) * rows] * gain
            normed_ref[e, :, begin : begin + size] = values.astype(jnp.bfloat16)
    swiglu(normed_ref, gates, ups, hidden_ref, 0)


def select_kernel(dims, lead, tail, pos_ref, gain_ref, *refs):
    n_fast = dims[0]
    first, second, refs = refs[:n_fast], refs[n_fast : 2 * n_fast], refs[2 * n_fast :]
    gates, ups, refs = refs[:lead], refs[lead : 2 * lead], refs[2 * lead :]
    _, far_ref, hidden_ref, normed_ref, mix_ref, turned_ref, *near, sems = refs
    copies = load_copies([far_ref] * tail, near, sems, range(lead, lead + tail))

    @pl.when(pos_ref[0] >= 0)
    def _():
        select_body(dims, pos_ref, gain_ref, first, second, gates, ups, hidden_ref, normed_ref, mix_ref, turned_ref)

    for copy in copies:
        copy.wait()


def up_kernel(start, count, wanted, pos_ref, normed_ref, *refs):
    gates, ups, (far_ref, hidden_ref, *near, sems) = refs[:count], refs[count : 2 * count], refs[2 * count :]
    copies = load_copies([far_ref] * len(near), near, sems, wanted)

    @pl.when(pos_ref[0] >= 0)
    def _():
        swiglu(normed_ref, gates, ups, hidden_ref, start)

    for copy in copies:
        copy.wait()


def lower(tp_pos, n_tp, piece, s, down_ref, columns):
    hid_part = piece.shape[1]
    begin = pl.multiple_of(lax.rem(tp_pos - s + n_tp, n_tp) * hid_part, hid_part)
    return jnp.dot(piece, down_ref[pl.ds(begin, hid_part), columns], preferred_element_type=jnp.float32)


def down_kernel(n_tp, count, pos_ref, own_ref, *refs):
    pieces, (*downs, out_ref, part_ref) = refs[:n_tp], refs[n_tp:]
    _, rows, _ = own_ref.shape
    every = slice(None)
    for i, ref in enumerate(downs[:count]):
        total = sum(lower(pos_ref[0], n_tp, pieces[s][i], s, ref, every) for s in range(n_tp))
        out_ref[i * rows : (i + 1) * rows] = total.astype(jnp.bfloat16)
    for i, ref in enumerate(downs[count:]):
        part_ref[i * rows : (i + 1) * rows] = lower(pos_ref[0], n_tp, own_ref[i], 0, ref, every)


def in_blocks(total, refs):
    rows = refs[0].shape[0]
    for i, ref in enumerate(refs):
        ref[...] = total[i * rows : (i + 1) * rows].astype(jnp.bfloat16)


def mix_kernel(n_tp, count, begin, pos_ref, mix_ref, done_ref, part_ref, *refs):
    pieces, refs = refs[: n_tp - 1], refs[n_tp - 1 :]
    downs, (*partial_refs, out_ref) = refs[:count], refs[count:]
    columns = pl.ds(begin, out_ref.shape[1])
    at = done_ref.shape[0]
    rows = part_ref.shape[0] // count
    out_ref[:at] = done_ref[:, columns]
    for i, ref in enumerate(downs):
        total = part_ref[i * rows : (i + 1) * rows, columns]
        for s in range(1, n_tp):
            total = total + lower(pos_ref[0], n_tp, pieces[s - 1][i], s, ref, columns)
        out_ref[at + i * rows : at + (i + 1) * rows] = total.astype(jnp.bfloat16)
    out = out_ref[...]
    partial = jnp.dot(mix_ref[0], out, preferred_element_type=jnp.float32)
    partial = partial + jnp.dot(mix_ref[1], out, preferred_element_type=jnp.float32)
    in_blocks(partial, partial_refs)


def total_of(refs):
    return functools.reduce(lambda a, ref: a + ref[...].astype(jnp.float32), refs[1:], refs[0][...].astype(jnp.float32))


def sum_kernel(count, signs, blocks, *refs):
    out_refs = refs[count + signs :]
    pieces = refs[:count]
    if count == 1:
        pieces = [pieces[0].at[k] for k in range(pieces[0].shape[0])]
    total = total_of(pieces)
    if len(out_refs[0].shape) == 3:
        rows = out_refs[0].shape[1]
        for k in range(out_refs[0].shape[0]):
            out_refs[0][k] = total[k * rows : (k + 1) * rows].astype(jnp.bfloat16)
    else:
        in_blocks(total, out_refs[:blocks])
    for ref in out_refs[blocks:]:
        ref[...] = jnp.zeros_like(ref)


def final_kernel(dims, pos_ref, first_ref, second_ref, *refs):
    n_mid, n_tp, slow_n, tok_dev, half = dims
    (left_ref, *right), (out_ref, own_ref) = refs[:-2], refs[-2:]
    left = [left_ref.at[k] for k in range(left_ref.shape[0])]
    tp_pos = pos_ref[0]
    col_part = out_ref.shape[1]
    run = slow_n * tok_dev
    group = n_tp * tok_dev

    def own(ref, step):
        row = lax.broadcasted_iota(jnp.int32, (group, ref.shape[0]), 0)
        at = lax.div(row, tok_dev) * step + pos_ref[2] * tok_dev + lax.rem(row, tok_dev)
        table = (at == lax.broadcasted_iota(jnp.int32, (group, ref.shape[0]), 1)).astype(jnp.float32)
        return jnp.dot(table.astype(jnp.bfloat16), ref[:, :half], preferred_element_type=jnp.float32)

    own_ref[:, half:] = own(first_ref, n_mid * run)
    own_ref[:, :half] = own(second_ref, run)
    total = jnp.concatenate([total_of(left), total_of(right)], axis=1)
    total = total + own_ref[:, pl.ds(pl.multiple_of(tp_pos * col_part, col_part), col_part)]
    rows = []
    for j in range(n_tp):
        row = total[:tok_dev]
        for s in range(1, n_tp):
            here = lax.rem(tp_pos - s + n_tp, n_tp) == j
            row = jnp.where(here, total[s * tok_dev : (s + 1) * tok_dev], row)
        rows.append(row)
    out_ref[...] = jnp.concatenate(rows, axis=0).astype(jnp.bfloat16)


VMEM = pl.BlockSpec(memory_space=pltpu.VMEM)
SMEM = pl.BlockSpec(memory_space=pltpu.SMEM)
HBM = pl.BlockSpec(memory_space=pltpu.HBM)
KEPT = pltpu.VMEM
TOKEN = jax.ShapeDtypeStruct((8, LANES), jnp.float32)


def local_call(kernel, shapes, operands, far=(), scratch=(), limit=6 << 20, flops=0, moved=0):
    specs, given = [], []
    for i, a in enumerate(operands):
        if i in far:
            specs.append(HBM)
            given.append(pltpu.with_memory_space_constraint(a, pltpu.HBM))
        else:
            specs.append(SMEM if a.dtype == jnp.int32 else VMEM)
            given.append(a)
    return pl.pallas_call(
        kernel,
        out_shape=shapes,
        in_specs=specs,
        out_specs=[VMEM] * len(shapes),
        scratch_shapes=list(scratch),
        compiler_params=pltpu.CompilerParams(vmem_limit_bytes=limit),
        cost_estimate=pl.CostEstimate(flops=flops, bytes_accessed=moved, transcendentals=0),
    )(*given)


def kept(array, count):
    return [KEPT(array.shape[1:], array.dtype)] * count


def runs_of(array):
    return 4 if array.shape[1] % 64 == 0 else 1


def loaded(wanted, after):
    sign, *near = local_call(
        functools.partial(load_kernel, [expert for _, expert in wanted], len(after)),
        [TOKEN] + [KEPT(array.shape[1:], array.dtype) for array, _ in wanted],
        [array for array, _ in wanted] + after,
        far=range(len(wanted)),
        scratch=[pltpu.SemaphoreType.DMA((len(wanted), min(runs_of(array) for array, _ in wanted)))],
        limit=1 << 20,
        moved=2 * sum(array.size // array.shape[0] for array, _ in wanted),
    )
    return near, sign


def summed(pieces, blocks, stacked, after, signed):
    rows, columns = pieces[0].shape[-2:]
    shape = (blocks, rows // blocks, columns) if stacked else (rows // blocks, columns)
    outs = 1 if stacked else blocks
    return local_call(
        functools.partial(sum_kernel, len(pieces), len(after), outs),
        [jax.ShapeDtypeStruct(shape, pieces[0].dtype)] * outs + [TOKEN] * signed,
        list(pieces) + after,
        limit=4 << 20,
        moved=2 * (len(pieces) + 1) * rows * columns,
    )


def joined(pieces, after, signed):
    rows, columns = pieces[0].shape
    return local_call(
        functools.partial(join_kernel, len(pieces), len(after)),
        [jax.ShapeDtypeStruct((len(pieces) * rows, columns), pieces[0].dtype)] + [TOKEN] * signed,
        list(pieces) + after,
        limit=4 << 20,
        moved=4 * len(pieces) * rows * columns,
    )


def by_tokens(hidden_in, norm_gain, expert_ids, gate_weights, w_gate, w_up, w_down):
    n_ep = lax.axis_size("ep")
    n_tp = lax.axis_size("tp")
    ep_pos = lax.axis_index("ep")
    tp_pos = lax.axis_index("tp")
    tok_dev, width = hidden_in.shape
    group, top = expert_ids.shape
    exp_loc, _, hid_part = w_gate.shape
    col_part = w_down.shape[2]
    experts = exp_loc * n_ep
    cap = max(2, 2 * top * group // experts)
    rows = cap * n_ep
    tokens = group * n_ep
    digits = factors_of(n_ep)
    fast, mid = digits[0], digits[1:2]
    half = width // 2
    slow_n = n_ep
    for _, radix in [fast] + mid:
        slow_n //= radix
    n_fast, n_mid = fast[1], mid[0][1]

    bf16 = functools.partial(jax.ShapeDtypeStruct, dtype=jnp.bfloat16)
    slots = exp_loc * rows
    lead = exp_loc - exp_loc // 2
    tail = exp_loc - lead
    gain = norm_gain.reshape(1, width)
    position = jnp.stack([tp_pos, ep_pos * exp_loc, ep_pos // (n_ep // slow_n)])
    (message,) = local_call(
        functools.partial(pack_kernel, top),
        [bf16((slow_n, tok_dev, width + LANES))],
        [position, expert_ids.T, gate_weights.T, hidden_in],
        far=[1, 2, 3],
        scratch=[
            pltpu.VMEM((top, group), jnp.int32),
            pltpu.VMEM((top, group), jnp.float32),
            pltpu.SemaphoreType.DMA((2 + slow_n,)),
        ],
        limit=4 << 20,
    )
    stride = n_ep // slow_n
    alike = [[at + k * stride for k in range(slow_n)] for at in range(stride)]
    along_slow = lambda a: lax.all_to_all(a, "ep", 0, 0, axis_index_groups=alike, tiled=True)
    around = along_slow(message)
    gate_lead, sign = loaded([(w_gate, e) for e in range(lead)], [gain])
    first, second, sign = local_call(
        functools.partial(split_kernel, half),
        [bf16((slow_n * tok_dev, width + LANES - half)), bf16((slow_n * tok_dev, half)), TOKEN],
        [around, sign],
        limit=4 << 20,
    )
    gate_tail, sign = loaded([(w_gate, e) for e in range(lead, exp_loc)], [sign])
    along_tp = lambda a: arrivals(a, "tp", n_tp, 1, n_tp)
    along_mid = lambda a: arrivals(a, "ep", n_ep, *mid[0])
    first, second = along_mid(first), along_tp(second)
    first, sign = joined(first, [sign], 1)
    (second,) = joined(second, [], 0)
    up_lead, sign = loaded([(w_up, e) for e in range(lead)] + [(w_down, 0)], [sign])
    *up_lead, down_first = up_lead
    first, second = along_tp(first), along_mid(second)
    first, sign = joined(first, [sign], 1)
    down_lead, sign = loaded([(w_down, e) for e in range(1, lead)], [sign]) if lead > 1 else ([], sign)
    down_lead = [down_first] + down_lead
    (second,) = joined(second, [], 0)
    first = arrivals(first, "ep", n_ep, *fast)
    second = arrivals(second, "ep", n_ep, *fast)

    dims = (n_fast, n_mid, n_tp, slow_n, tok_dev, top, exp_loc, rows, half)
    sems = lambda array, count: pltpu.SemaphoreType.DMA((count, runs_of(array)))
    operands = [position, gain] + first + second + gate_lead + up_lead + [sign, w_up]
    hidden, normed, mix, turned, *up_tail = local_call(
        functools.partial(select_kernel, dims, lead, tail),
        [
            bf16((lead, rows, hid_part)),
            bf16((exp_loc, rows, width)),
            bf16((2, tokens, slots)),
            bf16((2, tokens, slots)),
        ]
        + kept(w_up, tail),
        operands,
        far=[len(operands) - 1],
        scratch=[sems(w_up, tail)],
        flops=2 * slots * tokens * width + 4 * lead * rows * width * hid_part,
        moved=4 * lead * width * hid_part,
    )
    pieces = along_tp(hidden)
    operands = [position, normed] + gate_tail + up_tail + [w_down]
    hidden, *down_tail = local_call(
        functools.partial(up_kernel, lead, tail, range(lead, exp_loc)),
        [bf16((tail, rows, hid_part))] + kept(w_down, tail),
        operands,
        far=[len(operands) - 1],
        scratch=[sems(w_down, tail)],
        flops=4 * tail * rows * width * hid_part,
        moved=4 * tail * width * hid_part,
    )
    late = along_tp(hidden)
    done, part = local_call(
        functools.partial(down_kernel, n_tp, lead),
        [bf16((lead * rows, col_part)), jax.ShapeDtypeStruct((tail * rows, col_part), jnp.float32)],
        [position, late[0]] + pieces + down_lead + down_tail,
        flops=2 * lead * rows * n_tp * hid_part * col_part,
        moved=2 * lead * n_tp * hid_part * col_part,
    )
    col_half = col_part // 2
    mixed_of = lambda table, begin: local_call(
        functools.partial(mix_kernel, n_tp, tail, begin),
        [bf16((tokens // n_fast, col_half))] * n_fast,
        [position, table, done, part] + late[1:] + down_tail,
        scratch=[pltpu.VMEM((slots, col_half), jnp.bfloat16)],
        flops=slots * n_tp * hid_part * col_part,
        moved=exp_loc * n_tp * hid_part * col_part,
    )

    def swapped(blocks, digit):
        stride, radix = digit
        return [blocks[0]] + [shifted(blocks[s], "ep", n_ep, stride, radix, radix - s) for s in range(1, radix)]

    (right,) = summed(swapped(mixed_of(turned, col_half), fast), slow_n, True, [], 0)
    left = summed(swapped(mixed_of(mix, 0), fast), n_mid, False, [], 0)
    right = along_slow(right)
    left, sign = summed(swapped(left, mid[0]), slow_n, True, [], 1)
    left = along_slow(left)
    right = swapped(summed([right], n_mid, False, [sign], 0), mid[0])
    (mixed,) = local_call(
        functools.partial(final_kernel, (n_mid, n_tp, slow_n, tok_dev, half)),
        [bf16((group, col_part))],
        [position, first[0], second[0], left] + right,
        scratch=[pltpu.VMEM((group, width), jnp.float32)],
        limit=4 << 20,
        moved=2 * group * (width + 6 * col_part),
    )
    return mixed


def by_slots(hidden_in, norm_gain, expert_ids, gate_weights, w_gate, w_up, w_down):
    n_ep = lax.axis_size("ep")
    tp_pos = lax.axis_index("tp")
    tok_dev, width = hidden_in.shape
    group, top = expert_ids.shape
    exp_loc, _, hid_part = w_gate.shape
    col_part = w_down.shape[2]
    experts = exp_loc * n_ep
    cap = max(2, 2 * top * group // experts)
    values = hidden_in.astype(jnp.float32)
    scale = lax.rsqrt(jnp.mean(values * values, axis=1, keepdims=True) + 1e-06)
    normed = (values * scale * norm_gain.astype(jnp.float32)).astype(jnp.bfloat16)
    flat_ids = expert_ids.reshape(-1)
    pairs = flat_ids.shape[0]
    hits = (flat_ids[:, None] == lax.broadcasted_iota(jnp.int32, (pairs, experts), 1)).astype(
        jnp.int32
    )
    before = jnp.cumsum(hits, axis=0) - hits
    position = jnp.sum(before * hits, axis=1)
    slot_index = flat_ids * cap + position
    places = lax.broadcasted_iota(jnp.int32, (experts * cap, group, top), 0)
    dispatch_map = jnp.any(places == slot_index.reshape(group, top)[None], axis=2).astype(
        jnp.bfloat16
    )
    whole_norm, whole_input = (
        lax.all_gather(normed, "tp", axis=0, tiled=True),
        lax.all_gather(hidden_in, "tp", axis=0, tiled=True),
    )
    residual = lax.dynamic_slice_in_dim(whole_input, tp_pos * col_part, col_part, 1)
    packed = jnp.dot(dispatch_map, whole_norm, preferred_element_type=jnp.float32).astype(
        jnp.bfloat16
    )
    packed = packed.reshape(n_ep, exp_loc, cap, width)
    arrived = lax.all_to_all(packed, "ep", split_axis=0, concat_axis=0, tiled=True)
    gate_act = jnp.einsum("secd,edh->sech", arrived, w_gate, preferred_element_type=jnp.float32)
    up_act = jnp.einsum("secd,edh->sech", arrived, w_up, preferred_element_type=jnp.float32)
    hidden = (jax.nn.silu(gate_act) * up_act).astype(jnp.bfloat16)
    outputs = jnp.einsum(
        "sech,ehf->secf",
        lax.all_gather(hidden, "tp", axis=3, tiled=True),
        w_down,
        preferred_element_type=jnp.float32,
    )
    returned = lax.all_to_all(
        outputs.astype(jnp.bfloat16), "ep", split_axis=0, concat_axis=0, tiled=True
    )
    flat_back = returned.reshape(experts * cap, col_part)
    picked = flat_back[slot_index].reshape(group, top, col_part).astype(jnp.float32)
    combined = jnp.sum(picked * gate_weights[:, :, None], axis=1)
    return (residual.astype(jnp.float32) + combined).astype(jnp.bfloat16)


def shards(hidden_in, norm_gain, expert_ids, gate_weights, w_gate, w_up, w_down):
    group, top = expert_ids.shape
    exp_loc = w_gate.shape[0]
    cap = max(2, 2 * top * group // (exp_loc * lax.axis_size("ep")))
    whole = exp_loc > 1 and len(factors_of(lax.axis_size("ep"))) > 2 and exp_loc * cap >= group
    plan = by_tokens if whole else by_slots
    return plan(hidden_in, norm_gain, expert_ids, gate_weights, w_gate, w_up, w_down)


def solution(mesh):
    in_specs = (
        P(("ep", "tp"), None),
        P(),
        P("ep", None),
        P("ep", None),
        P("ep", None, "tp"),
        P("ep", None, "tp"),
        P("ep", None, "tp"),
    )
    out_specs = P("ep", "tp")
    return jax.shard_map(shards, mesh=mesh, in_specs=in_specs, out_specs=out_specs, check_vma=False)
```

```python
import functools

import jax
import jax.numpy as jnp
from jax import lax
from jax.experimental import pallas as pl
from jax.experimental.pallas import tpu as pltpu
from jax.sharding import PartitionSpec as P

LANES = 128


def factors_of(n):
    digits, stride = [], 1
    for _ in range(2):
        if n % 2 == 0 and n > 1:
            digits.append((stride, 2))
            stride, n = stride * 2, n // 2
    while n > 1:
        radix = 4 if n % 4 == 0 else 2
        digits.append((stride, radix))
        stride, n = stride * radix, n // radix
    return digits


def traded(x, axis, size, stride, radix, by):
    pairs = []
    for i in range(size):
        digit = i // stride % radix
        pairs.append((i, i + ((digit ^ by) - digit) * stride))
    return lax.ppermute(x, axis, pairs)


def trades(blocks, axis, size, stride, radix):
    came = {s: traded(blocks[s], axis, size, stride, radix, s) for s in reversed(range(1, radix))}
    return [blocks[0]] + [came[s] for s in range(1, radix)]


def arrivals(x, axis, size, stride, radix):
    return trades([x] * radix, axis, size, stride, radix)


def pack_kernel(top, pos_ref, ids_ref, weights_ref, values_ref, message_ref, ids, weights, sems):
    tok_dev, width = values_ref.shape
    copies = [
        pltpu.make_async_copy(ids_ref, ids, sems.at[0]),
        pltpu.make_async_copy(weights_ref, weights, sems.at[1]),
        pltpu.make_async_copy(values_ref, message_ref.at[:, pl.ds(0, width)], sems.at[2]),
    ]
    for copy in copies:
        copy.start()
    copies[0].wait()
    copies[1].wait()
    group = ids.shape[1]
    high = weights[...].astype(jnp.bfloat16).astype(jnp.float32)
    rest = weights[...] - high
    mid = rest.astype(jnp.bfloat16).astype(jnp.float32)
    terms = [ids[...].astype(jnp.float32), high, mid, rest - mid]
    terms.append(jnp.zeros((LANES - 4 * top, group), jnp.float32))
    table = jnp.concatenate(terms, axis=0).astype(jnp.bfloat16)
    own = lax.broadcasted_iota(jnp.int32, (tok_dev, group), 0) + pos_ref[0] * tok_dev
    own = (own == lax.broadcasted_iota(jnp.int32, (tok_dev, group), 1)).astype(jnp.float32)
    routing = lax.dot_general(
        own.astype(jnp.bfloat16), table, (((1,), (1,)), ((), ())), preferred_element_type=jnp.float32
    )
    message_ref[:, width:] = routing.astype(jnp.bfloat16)
    copies[2].wait()


def split_kernel(half, *refs):
    pieces, (first_ref, second_ref, token_ref) = refs[:-3], refs[-3:]
    pieces = [ref for ref in pieces if ref.shape[1] > 2 * half]
    whole = jnp.concatenate([ref[...].astype(jnp.float32) for ref in pieces], axis=0).astype(jnp.bfloat16)
    second_ref[...] = whole[:, :half]
    first_ref[...] = whole[:, half:]
    token_ref[...] = jnp.zeros_like(token_ref)


def join_kernel(count, signs, *refs):
    out_ref = refs[count + signs]
    rows = refs[0].shape[0]
    for i, ref in enumerate(refs[:count]):
        out_ref[i * rows : (i + 1) * rows] = ref[...]
    for ref in refs[count + signs + 1 :]:
        ref[...] = jnp.zeros_like(ref)


def load_kernel(experts, signs, *refs):
    count = len(experts)
    refs = refs[:count] + refs[count + signs :]
    far, (sign_ref, *near, sems) = refs[:count], refs[count:]
    copies = load_copies(far, near, sems, experts)
    sign_ref[...] = jnp.zeros_like(sign_ref)
    for copy in copies:
        copy.wait()


def load_copies(far, near, sems, experts):
    copies = []
    for i, (src_ref, dst_ref, expert) in enumerate(zip(far, near, experts)):
        runs = sems.shape[1]
        size = dst_ref.shape[0] // runs
        for r in range(runs):
            at = pl.ds(r * size, size)
            copies.append(pltpu.make_async_copy(src_ref.at[expert, at], dst_ref.at[at], sems.at[i, r]))
    for copy in copies:
        copy.start()
    return copies


def swiglu(normed_ref, gates, ups, hidden_ref, start):
    for i, (gate_ref, up_ref) in enumerate(zip(gates, ups)):
        x = normed_ref[start + i]
        gate_act = jnp.dot(x, gate_ref[...], preferred_element_type=jnp.float32)
        up_act = jnp.dot(x, up_ref[...], preferred_element_type=jnp.float32)
        hidden_ref[i] = (gate_act / (1.0 + jnp.exp(-gate_act)) * up_act).astype(jnp.bfloat16)


def select_body(dims, pos_ref, gain_ref, first, second, gates, ups, hidden_ref, normed_ref, mix_ref, turned_ref):
    n_fast, n_mid, n_tp, slow_n, tok_dev, top, exp_loc, rows, half = dims
    tp_pos, base = pos_ref[0], pos_ref[1]
    run = slow_n * tok_dev
    tokens = n_fast * n_mid * n_tp * run
    routing = jnp.concatenate([ref[:, half:] for ref in first], axis=0).astype(jnp.float32)
    ids = routing[:, :top]
    weights = routing[:, top : 2 * top] + (
        routing[:, 2 * top : 3 * top] + routing[:, 3 * top : 4 * top]
    )

    def number(shape, dim):
        at = lax.broadcasted_iota(jnp.int32, shape, dim)
        tp_at = lax.rem(lax.div(at, n_mid * run), n_tp)
        return at + (lax.rem(tp_pos - tp_at + n_tp, n_tp) - tp_at) * (n_mid * run)

    before = number((tokens, tokens), 1) < number((tokens, tokens), 0)
    match = [ids == (base + e).astype(jnp.float32) for e in range(exp_loc)]
    hits = [jnp.sum(m.astype(jnp.float32), axis=1, keepdims=True) for m in match]
    shares = [jnp.sum(jnp.where(m, weights, 0.0), axis=1, keepdims=True) for m in match]
    lane = lax.broadcasted_iota(jnp.int32, (tokens, LANES), 1)
    hit = functools.reduce(
        lambda a, e: jnp.where(lane == e, hits[e], a),
        range(exp_loc),
        jnp.zeros((tokens, LANES), jnp.float32),
    )
    position = jnp.dot(
        before.astype(jnp.float32).astype(jnp.bfloat16),
        hit.astype(jnp.bfloat16),
        preferred_element_type=jnp.float32,
    )
    slot = lax.broadcasted_iota(jnp.int32, (tokens, rows), 1).astype(jnp.float32)
    picks, spreads = [], []
    for e in range(exp_loc):
        place = jnp.where(hits[e] > 0, position[:, e : e + 1], -1.0)
        pick = slot == place
        picks.append(pick.astype(jnp.float32))
        spreads.append(jnp.where(pick, shares[e], 0.0))
    spread = jnp.concatenate(spreads, axis=1)
    group = lambda f, m, s: [
        spread[start : start + tok_dev]
        for start in [(((f * n_tp + t) * n_mid + m) * slow_n + s) * tok_dev for t in range(n_tp)]
    ]
    blocks = [b for f in range(n_fast) for m in range(n_mid) for s in range(slow_n) for b in group(f, m, s)]
    turned = [b for f in range(n_fast) for s in range(slow_n) for m in range(n_mid) for b in group(f, m, s)]
    for ref, rows_of in ((mix_ref, blocks), (turned_ref, turned)):
        exact = jnp.concatenate(rows_of, axis=0)
        high = exact.astype(jnp.bfloat16)
        ref[0] = high
        ref[1] = (exact - high.astype(jnp.float32)).astype(jnp.bfloat16)

    part = n_mid * n_tp * run
    pick = jnp.concatenate(picks, axis=1)
    swapped = jnp.concatenate(
        [
            pick[f * part + (t * n_mid + m) * run : f * part + (t * n_mid + m + 1) * run]
            for f in range(n_fast)
            for m in range(n_mid)
            for t in range(n_tp)
        ],
        axis=0,
    )
    chosen, swapped = pick.T.astype(jnp.bfloat16), swapped.T.astype(jnp.bfloat16)
    size = min(half, 4 * LANES)
    squares = 0.0
    for begin in range(0, 2 * half, size):
        table, side, at = (swapped, second, begin) if begin < half else (chosen, first, begin - half)
        values = jnp.concatenate([ref[:, at : at + size] for ref in side], axis=0)
        values = jnp.dot(table, values, preferred_element_type=jnp.float32)
        squares = squares + jnp.sum(values * values, axis=1, keepdims=True)
        values = values.astype(jnp.bfloat16)
        for e in range(exp_loc):
            normed_ref[e, :, begin : begin + size] = values[e * rows : (e + 1) * rows]
    scale = lax.rsqrt(squares / (2 * half) + 1e-06)
    gain_all = gain_ref[...].astype(jnp.float32)
    for begin in range(0, 2 * half, size):
        gain = [gain_all[r : r + 1] for r in range(begin // LANES, (begin + size) // LANES)]
        gain = jnp.concatenate(gain, axis=1)
        for e in range(exp_loc):
            values = normed_ref[e, :, begin : begin + size].astype(jnp.float32)
            values = values * scale[e * rows : (e + 1) * rows] * gain
            normed_ref[e, :, begin : begin + size] = values.astype(jnp.bfloat16)
    swiglu(normed_ref, gates, ups, hidden_ref, 0)


def select_kernel(dims, lead, tail, pos_ref, gain_ref, *refs):
    n_fast = dims[0]
    first, second, refs = refs[:n_fast], refs[n_fast : 2 * n_fast], refs[2 * n_fast :]
    gates, ups, refs = refs[:lead], refs[lead : 2 * lead], refs[2 * lead :]
    _, far_ref, hidden_ref, normed_ref, mix_ref, turned_ref, *near, sems = refs
    copies = load_copies([far_ref] * tail, near, sems, range(lead, lead + tail))

    @pl.when(pos_ref[0] >= 0)
    def _():
        select_body(dims, pos_ref, gain_ref, first, second, gates, ups, hidden_ref, normed_ref, mix_ref, turned_ref)

    for copy in copies:
        copy.wait()


def up_kernel(start, count, wanted, pos_ref, normed_ref, *refs):
    gates, ups, (far_ref, hidden_ref, *near, sems) = refs[:count], refs[count : 2 * count], refs[2 * count :]
    copies = load_copies([far_ref] * len(near), near, sems, wanted)

    @pl.when(pos_ref[0] >= 0)
    def _():
        swiglu(normed_ref, gates, ups, hidden_ref, start)

    for copy in copies:
        copy.wait()


def lower(tp_pos, n_tp, piece, s, down_ref, columns):
    hid_part = piece.shape[1]
    begin = pl.multiple_of(lax.rem(tp_pos - s + n_tp, n_tp) * hid_part, hid_part)
    return jnp.dot(piece, down_ref[pl.ds(begin, hid_part), columns], preferred_element_type=jnp.float32)


def down_kernel(n_tp, count, pos_ref, own_ref, *refs):
    pieces, (*downs, out_ref, part_ref) = refs[:n_tp], refs[n_tp:]
    _, rows, _ = own_ref.shape
    every = slice(None)
    for i, ref in enumerate(downs[:count]):
        total = sum(lower(pos_ref[0], n_tp, pieces[s][i], s, ref, every) for s in range(n_tp))
        out_ref[i * rows : (i + 1) * rows] = total.astype(jnp.bfloat16)
    for i, ref in enumerate(downs[count:]):
        part_ref[i * rows : (i + 1) * rows] = lower(pos_ref[0], n_tp, own_ref[i], 0, ref, every)


def in_blocks(total, refs):
    rows = refs[0].shape[0]
    for i, ref in enumerate(refs):
        ref[...] = total[i * rows : (i + 1) * rows].astype(jnp.bfloat16)


def mix_kernel(n_tp, count, begin, pos_ref, mix_ref, done_ref, part_ref, *refs):
    pieces, refs = refs[: n_tp - 1], refs[n_tp - 1 :]
    downs, (*partial_refs, out_ref) = refs[:count], refs[count:]
    columns = pl.ds(begin, out_ref.shape[1])
    at = done_ref.shape[0]
    rows = part_ref.shape[0] // count
    out_ref[:at] = done_ref[:, columns]
    for i, ref in enumerate(downs):
        total = part_ref[i * rows : (i + 1) * rows, columns]
        for s in range(1, n_tp):
            total = total + lower(pos_ref[0], n_tp, pieces[s - 1][i], s, ref, columns)
        out_ref[at + i * rows : at + (i + 1) * rows] = total.astype(jnp.bfloat16)
    out = out_ref[...]
    partial = jnp.dot(mix_ref[0], out, preferred_element_type=jnp.float32)
    partial = partial + jnp.dot(mix_ref[1], out, preferred_element_type=jnp.float32)
    in_blocks(partial, partial_refs)


def total_of(refs):
    return functools.reduce(lambda a, ref: a + ref[...].astype(jnp.float32), refs[1:], refs[0][...].astype(jnp.float32))


def sum_kernel(count, signs, blocks, *refs):
    out_refs = refs[count + signs :]
    in_blocks(total_of(refs[:count]), out_refs[:blocks])
    for ref in out_refs[blocks:]:
        ref[...] = jnp.zeros_like(ref)


def final_kernel(dims, count, pos_ref, first_ref, second_ref, *refs):
    n_mid, n_tp, slow_n, tok_dev, half = dims
    left, right, (out_ref, own_ref) = refs[:count], refs[count:-2], refs[-2:]
    tp_pos = pos_ref[0]
    col_part = out_ref.shape[1]
    for s in range(n_tp):
        at = s * n_mid * slow_n * tok_dev
        own_ref[s * tok_dev : (s + 1) * tok_dev, half:] = first_ref[at : at + tok_dev, :half].astype(jnp.float32)
        at = s * slow_n * tok_dev
        own_ref[s * tok_dev : (s + 1) * tok_dev, :half] = second_ref[at : at + tok_dev].astype(jnp.float32)
    total = jnp.concatenate([total_of(left), total_of(right)], axis=1)
    total = total + own_ref[:, pl.ds(pl.multiple_of(tp_pos * col_part, col_part), col_part)]
    rows = []
    for j in range(n_tp):
        row = total[:tok_dev]
        for s in range(1, n_tp):
            here = lax.rem(tp_pos - s + n_tp, n_tp) == j
            row = jnp.where(here, total[s * tok_dev : (s + 1) * tok_dev], row)
        rows.append(row)
    out_ref[...] = jnp.concatenate(rows, axis=0).astype(jnp.bfloat16)


VMEM = pl.BlockSpec(memory_space=pltpu.VMEM)
SMEM = pl.BlockSpec(memory_space=pltpu.SMEM)
HBM = pl.BlockSpec(memory_space=pltpu.HBM)
KEPT = pltpu.VMEM
TOKEN = jax.ShapeDtypeStruct((8, LANES), jnp.float32)


def local_call(kernel, shapes, operands, far=(), scratch=(), limit=6 << 20, flops=0, moved=0):
    specs, given = [], []
    for i, a in enumerate(operands):
        if i in far:
            specs.append(HBM)
            given.append(pltpu.with_memory_space_constraint(a, pltpu.HBM))
        else:
            specs.append(SMEM if a.dtype == jnp.int32 else VMEM)
            given.append(a)
    return pl.pallas_call(
        kernel,
        out_shape=shapes,
        in_specs=specs,
        out_specs=[VMEM] * len(shapes),
        scratch_shapes=list(scratch),
        compiler_params=pltpu.CompilerParams(vmem_limit_bytes=limit),
        cost_estimate=pl.CostEstimate(flops=flops, bytes_accessed=moved, transcendentals=0),
    )(*given)


def kept(array, count):
    return [KEPT(array.shape[1:], array.dtype)] * count


def runs_of(array):
    return 4 if array.shape[1] % 64 == 0 else 1


def loaded(wanted, after):
    sign, *near = local_call(
        functools.partial(load_kernel, [expert for _, expert in wanted], len(after)),
        [TOKEN] + [KEPT(array.shape[1:], array.dtype) for array, _ in wanted],
        [array for array, _ in wanted] + after,
        far=range(len(wanted)),
        scratch=[pltpu.SemaphoreType.DMA((len(wanted), min(runs_of(array) for array, _ in wanted)))],
        limit=1 << 20,
        moved=2 * sum(array.size // array.shape[0] for array, _ in wanted),
    )
    return near, sign


def summed(pieces, blocks, after, signed):
    rows, columns = pieces[0].shape
    return local_call(
        functools.partial(sum_kernel, len(pieces), len(after), blocks),
        [jax.ShapeDtypeStruct((rows // blocks, columns), pieces[0].dtype)] * blocks + [TOKEN] * signed,
        list(pieces) + after,
        limit=4 << 20,
        moved=2 * (len(pieces) + 1) * rows * columns,
    )


def joined(pieces, after, signed):
    rows, columns = pieces[0].shape
    return local_call(
        functools.partial(join_kernel, len(pieces), len(after)),
        [jax.ShapeDtypeStruct((len(pieces) * rows, columns), pieces[0].dtype)] + [TOKEN] * signed,
        list(pieces) + after,
        limit=4 << 20,
        moved=4 * len(pieces) * rows * columns,
    )


def by_tokens(hidden_in, norm_gain, expert_ids, gate_weights, w_gate, w_up, w_down):
    n_ep = lax.axis_size("ep")
    n_tp = lax.axis_size("tp")
    ep_pos = lax.axis_index("ep")
    tp_pos = lax.axis_index("tp")
    tok_dev, width = hidden_in.shape
    group, top = expert_ids.shape
    exp_loc, _, hid_part = w_gate.shape
    col_part = w_down.shape[2]
    experts = exp_loc * n_ep
    cap = max(2, 2 * top * group // experts)
    rows = cap * n_ep
    tokens = group * n_ep
    digits = factors_of(n_ep)
    fast, mid, slow = digits[0], digits[1:2], digits[2:]
    half = width // 2
    slow_n = n_ep
    for _, radix in [fast] + mid:
        slow_n //= radix
    n_fast, n_mid = fast[1], mid[0][1] if mid else 1

    bf16 = functools.partial(jax.ShapeDtypeStruct, dtype=jnp.bfloat16)
    slots = exp_loc * rows
    lead = exp_loc - exp_loc // 2
    tail = exp_loc - lead
    gain = norm_gain.reshape(width // LANES, LANES)
    position = jnp.stack([tp_pos, ep_pos * exp_loc])
    (message,) = local_call(
        functools.partial(pack_kernel, top),
        [bf16((tok_dev, width + LANES))],
        [position, expert_ids.T, gate_weights.T, hidden_in],
        far=[1, 2, 3],
        scratch=[
            pltpu.VMEM((top, group), jnp.int32),
            pltpu.VMEM((top, group), jnp.float32),
            pltpu.SemaphoreType.DMA((3,)),
        ],
        limit=4 << 20,
    )
    around = [message]
    for digit in reversed(slow):
        around = [a for piece in around for a in arrivals(piece, "ep", n_ep, *digit)]
    gate_lead, sign = loaded([(w_gate, e) for e in range(lead)], [])
    first, second, sign = local_call(
        functools.partial(split_kernel, half),
        [bf16((slow_n * tok_dev, width + LANES - half)), bf16((slow_n * tok_dev, half)), TOKEN],
        around + [sign],
        limit=4 << 20,
    )
    gate_tail, sign = loaded([(w_gate, e) for e in range(lead, exp_loc)], [sign])
    along_tp = lambda a: arrivals(a, "tp", n_tp, 1, n_tp)
    along_mid = lambda a: arrivals(a, "ep", n_ep, *mid[0]) if mid else [a]
    first, second = along_mid(first), along_tp(second)
    first, sign = joined(first, [sign], 1)
    (second,) = joined(second, [], 0)
    up_lead, sign = loaded([(w_up, e) for e in range(lead)] + [(w_down, 0)], [sign])
    *up_lead, down_first = up_lead
    first, second = along_tp(first), along_mid(second)
    first, sign = joined(first, [sign], 1)
    down_lead, sign = loaded([(w_down, e) for e in range(1, lead)], [sign]) if lead > 1 else ([], sign)
    down_lead = [down_first] + down_lead
    (second,) = joined(second, [], 0)
    first = arrivals(first, "ep", n_ep, *fast)
    second = arrivals(second, "ep", n_ep, *fast)

    dims = (n_fast, n_mid, n_tp, slow_n, tok_dev, top, exp_loc, rows, half)
    sems = lambda array, count: pltpu.SemaphoreType.DMA((count, runs_of(array)))
    operands = [position, gain] + first + second + gate_lead + up_lead + [sign, w_up]
    hidden, normed, mix, turned, *up_tail = local_call(
        functools.partial(select_kernel, dims, lead, tail),
        [
            bf16((lead, rows, hid_part)),
            bf16((exp_loc, rows, width)),
            bf16((2, tokens, slots)),
            bf16((2, tokens, slots)),
        ]
        + kept(w_up, tail),
        operands,
        far=[len(operands) - 1],
        scratch=[sems(w_up, tail)],
        flops=2 * slots * tokens * width + 4 * lead * rows * width * hid_part,
        moved=4 * lead * width * hid_part,
    )
    pieces = along_tp(hidden)
    operands = [position, normed] + gate_tail + up_tail + [w_down]
    hidden, *down_tail = local_call(
        functools.partial(up_kernel, lead, tail, range(lead, exp_loc)),
        [bf16((tail, rows, hid_part))] + kept(w_down, tail),
        operands,
        far=[len(operands) - 1],
        scratch=[sems(w_down, tail)],
        flops=4 * tail * rows * width * hid_part,
        moved=4 * tail * width * hid_part,
    )
    late = along_tp(hidden)
    done, part = local_call(
        functools.partial(down_kernel, n_tp, lead),
        [bf16((lead * rows, col_part)), jax.ShapeDtypeStruct((tail * rows, col_part), jnp.float32)],
        [position, late[0]] + pieces + down_lead + down_tail,
        flops=2 * lead * rows * n_tp * hid_part * col_part,
        moved=2 * lead * n_tp * hid_part * col_part,
    )
    col_half = col_part // 2
    mixed_of = lambda table, begin: local_call(
        functools.partial(mix_kernel, n_tp, tail, begin),
        [bf16((tokens // n_fast, col_half))] * n_fast,
        [position, table, done, part] + late[1:] + down_tail,
        scratch=[pltpu.VMEM((slots, col_half), jnp.bfloat16)],
        flops=slots * n_tp * hid_part * col_part,
        moved=exp_loc * n_tp * hid_part * col_part,
    )

    def swapped(blocks, digit):
        own, *others = trades(blocks, "ep", n_ep, *digit)
        return [own] + others[::-1]

    slow = list(reversed(slow))
    right_way, left_way = slow + mid, mid + slow
    right = summed(swapped(mixed_of(turned, col_half), fast), right_way[0][1], [], 0)
    left = summed(swapped(mixed_of(mix, 0), fast), left_way[0][1], [], 0)
    signs = []
    for digit, later in zip(left_way[:-1], left_way[1:]):
        *left, sign = summed(swapped(left, digit), later[1], [], 1)
        signs.append(sign)
    for digit, later in zip(right_way[:-1], right_way[1:]):
        right = summed(swapped(right, digit), later[1], signs, 0)
        signs = []
    left = swapped(left, left_way[-1])
    right = swapped(right, right_way[-1])
    (mixed,) = local_call(
        functools.partial(final_kernel, (n_mid, n_tp, slow_n, tok_dev, half), len(left)),
        [bf16((group, col_part))],
        [position, first[0], second[0]] + left + right,
        scratch=[pltpu.VMEM((group, width), jnp.float32)],
        limit=4 << 20,
        moved=2 * group * (width + 6 * col_part),
    )
    return mixed


def by_slots(hidden_in, norm_gain, expert_ids, gate_weights, w_gate, w_up, w_down):
    n_ep = lax.axis_size("ep")
    tp_pos = lax.axis_index("tp")
    tok_dev, width = hidden_in.shape
    group, top = expert_ids.shape
    exp_loc, _, hid_part = w_gate.shape
    col_part = w_down.shape[2]
    experts = exp_loc * n_ep
    cap = max(2, 2 * top * group // experts)
    values = hidden_in.astype(jnp.float32)
    scale = lax.rsqrt(jnp.mean(values * values, axis=1, keepdims=True) + 1e-06)
    normed = (values * scale * norm_gain.astype(jnp.float32)).astype(jnp.bfloat16)
    flat_ids = expert_ids.reshape(-1)
    pairs = flat_ids.shape[0]
    hits = (flat_ids[:, None] == lax.broadcasted_iota(jnp.int32, (pairs, experts), 1)).astype(
        jnp.int32
    )
    before = jnp.cumsum(hits, axis=0) - hits
    position = jnp.sum(before * hits, axis=1)
    slot_index = flat_ids * cap + position
    places = lax.broadcasted_iota(jnp.int32, (experts * cap, group, top), 0)
    dispatch_map = jnp.any(places == slot_index.reshape(group, top)[None], axis=2).astype(
        jnp.bfloat16
    )
    whole_norm, whole_input = (
        lax.all_gather(normed, "tp", axis=0, tiled=True),
        lax.all_gather(hidden_in, "tp", axis=0, tiled=True),
    )
    residual = lax.dynamic_slice_in_dim(whole_input, tp_pos * col_part, col_part, 1)
    packed = jnp.dot(dispatch_map, whole_norm, preferred_element_type=jnp.float32).astype(
        jnp.bfloat16
    )
    packed = packed.reshape(n_ep, exp_loc, cap, width)
    arrived = lax.all_to_all(packed, "ep", split_axis=0, concat_axis=0, tiled=True)
    gate_act = jnp.einsum("secd,edh->sech", arrived, w_gate, preferred_element_type=jnp.float32)
    up_act = jnp.einsum("secd,edh->sech", arrived, w_up, preferred_element_type=jnp.float32)
    hidden = (jax.nn.silu(gate_act) * up_act).astype(jnp.bfloat16)
    outputs = jnp.einsum(
        "sech,ehf->secf",
        lax.all_gather(hidden, "tp", axis=3, tiled=True),
        w_down,
        preferred_element_type=jnp.float32,
    )
    returned = lax.all_to_all(
        outputs.astype(jnp.bfloat16), "ep", split_axis=0, concat_axis=0, tiled=True
    )
    flat_back = returned.reshape(experts * cap, col_part)
    picked = flat_back[slot_index].reshape(group, top, col_part).astype(jnp.float32)
    combined = jnp.sum(picked * gate_weights[:, :, None], axis=1)
    return (residual.astype(jnp.float32) + combined).astype(jnp.bfloat16)


def shards(hidden_in, norm_gain, expert_ids, gate_weights, w_gate, w_up, w_down):
    group, top = expert_ids.shape
    exp_loc = w_gate.shape[0]
    cap = max(2, 2 * top * group // (exp_loc * lax.axis_size("ep")))
    n_ep = lax.axis_size("ep")
    whole = exp_loc > 1 and exp_loc * cap >= group and n_ep > 4 and n_ep & (n_ep - 1) == 0
    plan = by_tokens if whole else by_slots
    return plan(hidden_in, norm_gain, expert_ids, gate_weights, w_gate, w_up, w_down)


def solution(mesh):
    in_specs = (
        P(("ep", "tp"), None),
        P(),
        P("ep", None),
        P("ep", None),
        P("ep", None, "tp"),
        P("ep", None, "tp"),
        P("ep", None, "tp"),
    )
    out_specs = P("ep", "tp")
    return jax.shard_map(shards, mesh=mesh, in_specs=in_specs, out_specs=out_specs, check_vma=False)
```

```python
import functools

import jax
import jax.numpy as jnp
from jax import lax
from jax.experimental import pallas as pl
from jax.experimental.pallas import tpu as pltpu
from jax.sharding import PartitionSpec as P

LANES = 128


def factors_of(n):
    digits, stride = [], 1
    for _ in range(2):
        if n % 2 == 0 and n > 1:
            digits.append((stride, 2))
            stride, n = stride * 2, n // 2
    while n > 1:
        radix = 4 if n % 4 == 0 else 2
        digits.append((stride, radix))
        stride, n = stride * radix, n // radix
    return digits


def traded(x, axis, size, stride, radix, by):
    pairs = []
    for i in range(size):
        digit = i // stride % radix
        pairs.append((i, i + ((digit ^ by) - digit) * stride))
    return lax.ppermute(x, axis, pairs)


def trades(blocks, axis, size, stride, radix):
    came = {s: traded(blocks[s], axis, size, stride, radix, s) for s in reversed(range(1, radix))}
    return [blocks[0]] + [came[s] for s in range(1, radix)]


def arrivals(x, axis, size, stride, radix):
    return trades([x] * radix, axis, size, stride, radix)


def pack_kernel(top, pos_ref, ids_ref, weights_ref, values_ref, message_ref, ids, weights, sems):
    tok_dev, width = values_ref.shape
    copies = [
        pltpu.make_async_copy(ids_ref, ids, sems.at[0]),
        pltpu.make_async_copy(weights_ref, weights, sems.at[1]),
        pltpu.make_async_copy(values_ref, message_ref.at[:, pl.ds(0, width)], sems.at[2]),
    ]
    for copy in copies:
        copy.start()
    copies[0].wait()
    copies[1].wait()
    group = ids.shape[1]
    high = weights[...].astype(jnp.bfloat16).astype(jnp.float32)
    rest = weights[...] - high
    mid = rest.astype(jnp.bfloat16).astype(jnp.float32)
    terms = [ids[...].astype(jnp.float32), high, mid, rest - mid]
    terms.append(jnp.zeros((LANES - 4 * top, group), jnp.float32))
    table = jnp.concatenate(terms, axis=0).astype(jnp.bfloat16)
    own = lax.broadcasted_iota(jnp.int32, (tok_dev, group), 0) + pos_ref[0] * tok_dev
    own = (own == lax.broadcasted_iota(jnp.int32, (tok_dev, group), 1)).astype(jnp.float32)
    routing = lax.dot_general(
        own.astype(jnp.bfloat16), table, (((1,), (1,)), ((), ())), preferred_element_type=jnp.float32
    )
    message_ref[:, width:] = routing.astype(jnp.bfloat16)
    copies[2].wait()


def split_kernel(half, *refs):
    pieces, (first_ref, second_ref, token_ref) = refs[:-3], refs[-3:]
    pieces = [ref for ref in pieces if ref.shape[1] > 2 * half]
    whole = jnp.concatenate([ref[...].astype(jnp.float32) for ref in pieces], axis=0).astype(jnp.bfloat16)
    second_ref[...] = whole[:, :half]
    first_ref[...] = whole[:, half:]
    token_ref[...] = jnp.zeros_like(token_ref)


def join_kernel(count, signs, *refs):
    out_ref = refs[count + signs]
    rows = refs[0].shape[0]
    for i, ref in enumerate(refs[:count]):
        out_ref[i * rows : (i + 1) * rows] = ref[...]
    for ref in refs[count + signs + 1 :]:
        ref[...] = jnp.zeros_like(ref)


def load_kernel(experts, signs, *refs):
    count = len(experts)
    refs = refs[:count] + refs[count + signs :]
    far, (sign_ref, *near, sems) = refs[:count], refs[count:]
    copies = load_copies(far, near, sems, experts)
    sign_ref[...] = jnp.zeros_like(sign_ref)
    for copy in copies:
        copy.wait()


def load_copies(far, near, sems, experts):
    copies = []
    for i, (src_ref, dst_ref, expert) in enumerate(zip(far, near, experts)):
        runs = sems.shape[1]
        size = dst_ref.shape[0] // runs
        for r in range(runs):
            at = pl.ds(r * size, size)
            copies.append(pltpu.make_async_copy(src_ref.at[expert, at], dst_ref.at[at], sems.at[i, r]))
    for copy in copies:
        copy.start()
    return copies


def swiglu(normed_ref, gates, ups, hidden_ref, start):
    for i, (gate_ref, up_ref) in enumerate(zip(gates, ups)):
        x = normed_ref[start + i]
        gate_act = jnp.dot(x, gate_ref[...], preferred_element_type=jnp.float32)
        up_act = jnp.dot(x, up_ref[...], preferred_element_type=jnp.float32)
        hidden_ref[i] = (gate_act / (1.0 + jnp.exp(-gate_act)) * up_act).astype(jnp.bfloat16)


def select_body(dims, pos_ref, gain_ref, first, second, gates, ups, hidden_ref, normed_ref, mix_ref, turned_ref):
    n_fast, n_mid, n_tp, slow_n, tok_dev, top, exp_loc, rows, half = dims
    tp_pos, base = pos_ref[0], pos_ref[1]
    run = slow_n * tok_dev
    tokens = n_fast * n_mid * n_tp * run
    routing = jnp.concatenate([ref[:, half:] for ref in first], axis=0).astype(jnp.float32)
    ids = routing[:, :top]
    weights = routing[:, top : 2 * top] + (
        routing[:, 2 * top : 3 * top] + routing[:, 3 * top : 4 * top]
    )

    def number(shape, dim):
        at = lax.broadcasted_iota(jnp.int32, shape, dim)
        tp_at = lax.rem(lax.div(at, n_mid * run), n_tp)
        return at + (lax.rem(tp_pos - tp_at + n_tp, n_tp) - tp_at) * (n_mid * run)

    before = number((tokens, tokens), 1) < number((tokens, tokens), 0)
    match = [ids == (base + e).astype(jnp.float32) for e in range(exp_loc)]
    hits = [jnp.sum(m.astype(jnp.float32), axis=1, keepdims=True) for m in match]
    shares = [jnp.sum(jnp.where(m, weights, 0.0), axis=1, keepdims=True) for m in match]
    lane = lax.broadcasted_iota(jnp.int32, (tokens, LANES), 1)
    hit = functools.reduce(
        lambda a, e: jnp.where(lane == e, hits[e], a),
        range(exp_loc),
        jnp.zeros((tokens, LANES), jnp.float32),
    )
    position = jnp.dot(
        before.astype(jnp.float32).astype(jnp.bfloat16),
        hit.astype(jnp.bfloat16),
        preferred_element_type=jnp.float32,
    )
    slot = lax.broadcasted_iota(jnp.int32, (tokens, rows), 1).astype(jnp.float32)
    picks, spreads = [], []
    for e in range(exp_loc):
        place = jnp.where(hits[e] > 0, position[:, e : e + 1], -1.0)
        pick = slot == place
        picks.append(pick.astype(jnp.float32))
        spreads.append(jnp.where(pick, shares[e], 0.0))
    spread = jnp.concatenate(spreads, axis=1)
    group = lambda f, m, s: [
        spread[start : start + tok_dev]
        for start in [(((f * n_tp + t) * n_mid + m) * slow_n + s) * tok_dev for t in range(n_tp)]
    ]
    blocks = [b for f in range(n_fast) for m in range(n_mid) for s in range(slow_n) for b in group(f, m, s)]
    turned = [b for f in range(n_fast) for s in range(slow_n) for m in range(n_mid) for b in group(f, m, s)]
    for ref, rows_of in ((mix_ref, blocks), (turned_ref, turned)):
        exact = jnp.concatenate(rows_of, axis=0)
        high = exact.astype(jnp.bfloat16)
        ref[0] = high
        ref[1] = (exact - high.astype(jnp.float32)).astype(jnp.bfloat16)

    part = n_mid * n_tp * run
    pick = jnp.concatenate(picks, axis=1)
    swapped = jnp.concatenate(
        [
            pick[f * part + (t * n_mid + m) * run : f * part + (t * n_mid + m + 1) * run]
            for f in range(n_fast)
            for m in range(n_mid)
            for t in range(n_tp)
        ],
        axis=0,
    )
    chosen, swapped = pick.T.astype(jnp.bfloat16), swapped.T.astype(jnp.bfloat16)
    size = min(half, 4 * LANES)
    squares = 0.0
    for begin in range(0, 2 * half, size):
        table, side, at = (swapped, second, begin) if begin < half else (chosen, first, begin - half)
        values = jnp.concatenate([ref[:, at : at + size] for ref in side], axis=0)
        values = jnp.dot(table, values, preferred_element_type=jnp.float32)
        squares = squares + jnp.sum(values * values, axis=1, keepdims=True)
        values = values.astype(jnp.bfloat16)
        for e in range(exp_loc):
            normed_ref[e, :, begin : begin + size] = values[e * rows : (e + 1) * rows]
    scale = lax.rsqrt(squares / (2 * half) + 1e-06)
    gain_all = gain_ref[...].astype(jnp.float32)
    for begin in range(0, 2 * half, size):
        gain = [gain_all[r : r + 1] for r in range(begin // LANES, (begin + size) // LANES)]
        gain = jnp.concatenate(gain, axis=1)
        for e in range(exp_loc):
            values = normed_ref[e, :, begin : begin + size].astype(jnp.float32)
            values = values * scale[e * rows : (e + 1) * rows] * gain
            normed_ref[e, :, begin : begin + size] = values.astype(jnp.bfloat16)
    swiglu(normed_ref, gates, ups, hidden_ref, 0)


def select_kernel(dims, lead, tail, pos_ref, gain_ref, *refs):
    n_fast = dims[0]
    first, second, refs = refs[:n_fast], refs[n_fast : 2 * n_fast], refs[2 * n_fast :]
    gates, ups, refs = refs[:lead], refs[lead : 2 * lead], refs[2 * lead :]
    gate_far, up_far, hidden_ref, normed_ref, mix_ref, turned_ref, *near, sems = refs
    wanted = [(gate_far, lead + tail - 1)] + [(up_far, e) for e in range(lead, lead + tail)]
    copies = load_copies([ref for ref, _ in wanted], near, sems, [e for _, e in wanted])

    @pl.when(pos_ref[0] >= 0)
    def _():
        select_body(dims, pos_ref, gain_ref, first, second, gates, ups, hidden_ref, normed_ref, mix_ref, turned_ref)

    for copy in copies:
        copy.wait()


def up_kernel(start, count, wanted, pos_ref, normed_ref, *refs):
    gates, ups, (far_ref, hidden_ref, *near, sems) = refs[:count], refs[count : 2 * count], refs[2 * count :]
    copies = load_copies([far_ref] * len(near), near, sems, wanted)

    @pl.when(pos_ref[0] >= 0)
    def _():
        swiglu(normed_ref, gates, ups, hidden_ref, start)

    for copy in copies:
        copy.wait()


def lower(tp_pos, n_tp, piece, s, down_ref, columns):
    hid_part = piece.shape[1]
    begin = pl.multiple_of(lax.rem(tp_pos - s + n_tp, n_tp) * hid_part, hid_part)
    return jnp.dot(piece, down_ref[pl.ds(begin, hid_part), columns], preferred_element_type=jnp.float32)


def down_kernel(n_tp, count, pos_ref, own_ref, *refs):
    pieces, (*downs, out_ref, part_ref) = refs[:n_tp], refs[n_tp:]
    _, rows, _ = own_ref.shape
    every = slice(None)
    for i, ref in enumerate(downs[:count]):
        total = sum(lower(pos_ref[0], n_tp, pieces[s][i], s, ref, every) for s in range(n_tp))
        out_ref[i * rows : (i + 1) * rows] = total.astype(jnp.bfloat16)
    for i, ref in enumerate(downs[count:]):
        part_ref[i * rows : (i + 1) * rows] = lower(pos_ref[0], n_tp, own_ref[i], 0, ref, every)


def in_blocks(total, refs):
    rows = refs[0].shape[0]
    for i, ref in enumerate(refs):
        ref[...] = total[i * rows : (i + 1) * rows].astype(jnp.bfloat16)


def mix_kernel(n_tp, count, begin, pos_ref, mix_ref, done_ref, part_ref, *refs):
    pieces, refs = refs[: n_tp - 1], refs[n_tp - 1 :]
    downs, (*partial_refs, out_ref) = refs[:count], refs[count:]
    columns = pl.ds(begin, out_ref.shape[1])
    at = done_ref.shape[0]
    rows = part_ref.shape[0] // count
    out_ref[:at] = done_ref[:, columns]
    for i, ref in enumerate(downs):
        total = part_ref[i * rows : (i + 1) * rows, columns]
        for s in range(1, n_tp):
            total = total + lower(pos_ref[0], n_tp, pieces[s - 1][i], s, ref, columns)
        out_ref[at + i * rows : at + (i + 1) * rows] = total.astype(jnp.bfloat16)
    out = out_ref[...]
    partial = jnp.dot(mix_ref[0], out, preferred_element_type=jnp.float32)
    partial = partial + jnp.dot(mix_ref[1], out, preferred_element_type=jnp.float32)
    in_blocks(partial, partial_refs)


def total_of(refs):
    return functools.reduce(lambda a, ref: a + ref[...].astype(jnp.float32), refs[1:], refs[0][...].astype(jnp.float32))


def sum_kernel(count, signs, blocks, *refs):
    out_refs = refs[count + signs :]
    in_blocks(total_of(refs[:count]), out_refs[:blocks])
    for ref in out_refs[blocks:]:
        ref[...] = jnp.zeros_like(ref)


def own_kernel(dims, pos_ref, first_ref, second_ref, _, out_ref, own_ref):
    n_mid, n_tp, slow_n, tok_dev, half = dims
    col_part = out_ref.shape[1]
    for s in range(n_tp):
        at = s * n_mid * slow_n * tok_dev
        own_ref[s * tok_dev : (s + 1) * tok_dev, half:] = first_ref[at : at + tok_dev, :half].astype(jnp.float32)
        at = s * slow_n * tok_dev
        own_ref[s * tok_dev : (s + 1) * tok_dev, :half] = second_ref[at : at + tok_dev].astype(jnp.float32)
    out_ref[...] = own_ref[:, pl.ds(pl.multiple_of(pos_ref[0] * col_part, col_part), col_part)]


def final_kernel(n_tp, count, pos_ref, own_ref, *refs):
    left, right, out_ref = refs[:count], refs[count:-1], refs[-1]
    begin, tok_dev = 0, own_ref.shape[0] // n_tp
    for side in (left, right):
        columns = pl.ds(begin, side[0].shape[1])
        total = total_of(side) + own_ref[:, columns]
        rows = []
        for j in range(n_tp):
            row = total[:tok_dev]
            for s in range(1, n_tp):
                here = lax.rem(pos_ref[0] - s + n_tp, n_tp) == j
                row = jnp.where(here, total[s * tok_dev : (s + 1) * tok_dev], row)
            rows.append(row)
        out_ref[:, columns] = jnp.concatenate(rows, axis=0).astype(jnp.bfloat16)
        begin += side[0].shape[1]


VMEM = pl.BlockSpec(memory_space=pltpu.VMEM)
SMEM = pl.BlockSpec(memory_space=pltpu.SMEM)
HBM = pl.BlockSpec(memory_space=pltpu.HBM)
KEPT = pltpu.VMEM
TOKEN = jax.ShapeDtypeStruct((8, LANES), jnp.float32)


def local_call(kernel, shapes, operands, far=(), scratch=(), limit=6 << 20, flops=0, moved=0):
    specs, given = [], []
    for i, a in enumerate(operands):
        if i in far:
            specs.append(HBM)
            given.append(pltpu.with_memory_space_constraint(a, pltpu.HBM))
        else:
            specs.append(SMEM if a.dtype == jnp.int32 else VMEM)
            given.append(a)
    return pl.pallas_call(
        kernel,
        out_shape=shapes,
        in_specs=specs,
        out_specs=[VMEM] * len(shapes),
        scratch_shapes=list(scratch),
        compiler_params=pltpu.CompilerParams(vmem_limit_bytes=limit),
        cost_estimate=pl.CostEstimate(flops=flops, bytes_accessed=moved, transcendentals=0),
    )(*given)


def kept(array, count):
    return [KEPT(array.shape[1:], array.dtype)] * count


def runs_of(array):
    return 4 if array.shape[1] % 64 == 0 else 1


def loaded(wanted, after):
    sign, *near = local_call(
        functools.partial(load_kernel, [expert for _, expert in wanted], len(after)),
        [TOKEN] + [KEPT(array.shape[1:], array.dtype) for array, _ in wanted],
        [array for array, _ in wanted] + after,
        far=range(len(wanted)),
        scratch=[pltpu.SemaphoreType.DMA((len(wanted), min(runs_of(array) for array, _ in wanted)))],
        limit=1 << 20,
        moved=2 * sum(array.size // array.shape[0] for array, _ in wanted),
    )
    return near, sign


def summed(pieces, blocks, after, signed):
    rows, columns = pieces[0].shape
    return local_call(
        functools.partial(sum_kernel, len(pieces), len(after), blocks),
        [jax.ShapeDtypeStruct((rows // blocks, columns), pieces[0].dtype)] * blocks + [TOKEN] * signed,
        list(pieces) + after,
        limit=4 << 20,
        moved=2 * (len(pieces) + 1) * rows * columns,
    )


def joined(pieces, after, signed):
    rows, columns = pieces[0].shape
    return local_call(
        functools.partial(join_kernel, len(pieces), len(after)),
        [jax.ShapeDtypeStruct((len(pieces) * rows, columns), pieces[0].dtype)] + [TOKEN] * signed,
        list(pieces) + after,
        limit=4 << 20,
        moved=4 * len(pieces) * rows * columns,
    )


def by_tokens(hidden_in, norm_gain, expert_ids, gate_weights, w_gate, w_up, w_down):
    n_ep = lax.axis_size("ep")
    n_tp = lax.axis_size("tp")
    ep_pos = lax.axis_index("ep")
    tp_pos = lax.axis_index("tp")
    tok_dev, width = hidden_in.shape
    group, top = expert_ids.shape
    exp_loc, _, hid_part = w_gate.shape
    col_part = w_down.shape[2]
    experts = exp_loc * n_ep
    cap = max(2, 2 * top * group // experts)
    rows = cap * n_ep
    tokens = group * n_ep
    digits = factors_of(n_ep)
    fast, mid, slow = digits[0], digits[1:2], digits[2:]
    half = width // 2
    slow_n = n_ep
    for _, radix in [fast] + mid:
        slow_n //= radix
    n_fast, n_mid = fast[1], mid[0][1] if mid else 1

    bf16 = functools.partial(jax.ShapeDtypeStruct, dtype=jnp.bfloat16)
    slots = exp_loc * rows
    lead = exp_loc - exp_loc // 2
    tail = exp_loc - lead
    gain = norm_gain.reshape(width // LANES, LANES)
    position = jnp.stack([tp_pos, ep_pos * exp_loc])
    (message,) = local_call(
        functools.partial(pack_kernel, top),
        [bf16((tok_dev, width + LANES))],
        [position, expert_ids.T, gate_weights.T, hidden_in],
        far=[1, 2, 3],
        scratch=[
            pltpu.VMEM((top, group), jnp.int32),
            pltpu.VMEM((top, group), jnp.float32),
            pltpu.SemaphoreType.DMA((3,)),
        ],
        limit=4 << 20,
    )
    around = [message]
    for digit in reversed(slow):
        around = [a for piece in around for a in arrivals(piece, "ep", n_ep, *digit)]
    loads, sign = loaded([(w_gate, e) for e in range(lead)] + [(w_up, 0)], [])
    gate_lead, up_lead = loads[:lead], loads[lead:]
    first, second, sign = local_call(
        functools.partial(split_kernel, half),
        [bf16((slow_n * tok_dev, width + LANES - half)), bf16((slow_n * tok_dev, half)), TOKEN],
        around + [sign],
        limit=4 << 20,
    )
    gate_tail, sign = loaded([(w_gate, e) for e in range(lead, exp_loc - 1)], [sign]) if tail > 1 else ([], sign)
    along_tp = lambda a: arrivals(a, "tp", n_tp, 1, n_tp)
    along_mid = lambda a: arrivals(a, "ep", n_ep, *mid[0]) if mid else [a]
    first, second = along_mid(first), along_tp(second)
    first, sign = joined(first, [sign], 1)
    (second,) = joined(second, [], 0)
    loads, sign = loaded([(w_up, e) for e in range(1, lead)] + [(w_down, e) for e in range(lead)], [sign])
    up_lead, down_lead = up_lead + loads[: lead - 1], loads[lead - 1 :]
    first, second = along_tp(first), along_mid(second)
    (first,) = joined(first, [sign], 0)
    (second,) = joined(second, [], 0)
    first = arrivals(first, "ep", n_ep, *fast)
    second = arrivals(second, "ep", n_ep, *fast)

    dims = (n_fast, n_mid, n_tp, slow_n, tok_dev, top, exp_loc, rows, half)
    sems = lambda array, count: pltpu.SemaphoreType.DMA((count, runs_of(array)))
    operands = [position, gain] + first + second + gate_lead + up_lead + [w_gate, w_up]
    hidden, normed, mix, turned, gate_last, *up_tail = local_call(
        functools.partial(select_kernel, dims, lead, tail),
        [
            bf16((lead, rows, hid_part)),
            bf16((exp_loc, rows, width)),
            bf16((2, tokens, slots)),
            bf16((2, tokens, slots)),
        ]
        + kept(w_gate, 1)
        + kept(w_up, tail),
        operands,
        far=[len(operands) - 2, len(operands) - 1],
        scratch=[sems(w_up, 1 + tail)],
        flops=2 * slots * tokens * width + 4 * lead * rows * width * hid_part,
        moved=4 * lead * width * hid_part,
    )
    pieces = along_tp(hidden)
    operands = [position, normed] + gate_tail + [gate_last] + up_tail + [w_down]
    hidden, *down_tail = local_call(
        functools.partial(up_kernel, lead, tail, range(lead, exp_loc)),
        [bf16((tail, rows, hid_part))] + kept(w_down, tail),
        operands,
        far=[len(operands) - 1],
        scratch=[sems(w_down, tail)],
        flops=4 * tail * rows * width * hid_part,
        moved=4 * tail * width * hid_part,
    )
    late = along_tp(hidden)
    done, part = local_call(
        functools.partial(down_kernel, n_tp, lead),
        [bf16((lead * rows, col_part)), jax.ShapeDtypeStruct((tail * rows, col_part), jnp.float32)],
        [position, late[0]] + pieces + down_lead + down_tail,
        flops=2 * lead * rows * n_tp * hid_part * col_part,
        moved=2 * lead * n_tp * hid_part * col_part,
    )
    col_half = col_part // 2
    mixed_of = lambda table, begin: local_call(
        functools.partial(mix_kernel, n_tp, tail, begin),
        [bf16((tokens // n_fast, col_half))] * n_fast,
        [position, table, done, part] + late[1:] + down_tail,
        scratch=[pltpu.VMEM((slots, col_half), jnp.bfloat16)],
        flops=slots * n_tp * hid_part * col_part,
        moved=exp_loc * n_tp * hid_part * col_part,
    )

    def swapped(blocks, digit):
        own, *others = trades(blocks, "ep", n_ep, *digit)
        return [own] + others[::-1]

    slow = list(reversed(slow))
    right_way, left_way = slow + mid, mid + slow
    right = summed(swapped(mixed_of(turned, col_half), fast), right_way[0][1], [], 0)
    left = summed(swapped(mixed_of(mix, 0), fast), left_way[0][1], [], 0)
    signs = []
    for digit, later in zip(left_way[:-1], left_way[1:]):
        *left, late_sign = summed(swapped(left, digit), later[1], [], 1)
        signs.append(late_sign)
    for digit, later in zip(right_way[:-1], right_way[1:]):
        right = summed(swapped(right, digit), later[1], signs, 0)
        signs = []
    left = swapped(left, left_way[-1])
    right = swapped(right, right_way[-1])
    (own,) = local_call(
        functools.partial(own_kernel, (n_mid, n_tp, slow_n, tok_dev, half)),
        [jax.ShapeDtypeStruct((group, col_part), jnp.float32)],
        [position, first[0], second[0], late_sign],
        scratch=[pltpu.VMEM((group, width), jnp.float32)],
        limit=4 << 20,
        moved=4 * group * width,
    )
    (mixed,) = local_call(
        functools.partial(final_kernel, n_tp, len(left)),
        [bf16((group, col_part))],
        [position, own] + left + right,
        limit=4 << 20,
        moved=2 * group * 8 * col_part,
    )
    return mixed


def by_slots(hidden_in, norm_gain, expert_ids, gate_weights, w_gate, w_up, w_down):
    n_ep = lax.axis_size("ep")
    tp_pos = lax.axis_index("tp")
    tok_dev, width = hidden_in.shape
    group, top = expert_ids.shape
    exp_loc, _, hid_part = w_gate.shape
    col_part = w_down.shape[2]
    experts = exp_loc * n_ep
    cap = max(2, 2 * top * group // experts)
    values = hidden_in.astype(jnp.float32)
    scale = lax.rsqrt(jnp.mean(values * values, axis=1, keepdims=True) + 1e-06)
    normed = (values * scale * norm_gain.astype(jnp.float32)).astype(jnp.bfloat16)
    flat_ids = expert_ids.reshape(-1)
    pairs = flat_ids.shape[0]
    hits = (flat_ids[:, None] == lax.broadcasted_iota(jnp.int32, (pairs, experts), 1)).astype(
        jnp.int32
    )
    before = jnp.cumsum(hits, axis=0) - hits
    position = jnp.sum(before * hits, axis=1)
    slot_index = flat_ids * cap + position
    places = lax.broadcasted_iota(jnp.int32, (experts * cap, group, top), 0)
    dispatch_map = jnp.any(places == slot_index.reshape(group, top)[None], axis=2).astype(
        jnp.bfloat16
    )
    whole_norm, whole_input = (
        lax.all_gather(normed, "tp", axis=0, tiled=True),
        lax.all_gather(hidden_in, "tp", axis=0, tiled=True),
    )
    residual = lax.dynamic_slice_in_dim(whole_input, tp_pos * col_part, col_part, 1)
    packed = jnp.dot(dispatch_map, whole_norm, preferred_element_type=jnp.float32).astype(
        jnp.bfloat16
    )
    packed = packed.reshape(n_ep, exp_loc, cap, width)
    arrived = lax.all_to_all(packed, "ep", split_axis=0, concat_axis=0, tiled=True)
    gate_act = jnp.einsum("secd,edh->sech", arrived, w_gate, preferred_element_type=jnp.float32)
    up_act = jnp.einsum("secd,edh->sech", arrived, w_up, preferred_element_type=jnp.float32)
    hidden = (jax.nn.silu(gate_act) * up_act).astype(jnp.bfloat16)
    outputs = jnp.einsum(
        "sech,ehf->secf",
        lax.all_gather(hidden, "tp", axis=3, tiled=True),
        w_down,
        preferred_element_type=jnp.float32,
    )
    returned = lax.all_to_all(
        outputs.astype(jnp.bfloat16), "ep", split_axis=0, concat_axis=0, tiled=True
    )
    flat_back = returned.reshape(experts * cap, col_part)
    picked = flat_back[slot_index].reshape(group, top, col_part).astype(jnp.float32)
    combined = jnp.sum(picked * gate_weights[:, :, None], axis=1)
    return (residual.astype(jnp.float32) + combined).astype(jnp.bfloat16)


def shards(hidden_in, norm_gain, expert_ids, gate_weights, w_gate, w_up, w_down):
    group, top = expert_ids.shape
    exp_loc = w_gate.shape[0]
    cap = max(2, 2 * top * group // (exp_loc * lax.axis_size("ep")))
    n_ep = lax.axis_size("ep")
    whole = exp_loc > 1 and exp_loc * cap >= group and n_ep > 4 and n_ep & (n_ep - 1) == 0
    plan = by_tokens if whole else by_slots
    return plan(hidden_in, norm_gain, expert_ids, gate_weights, w_gate, w_up, w_down)


def solution(mesh):
    in_specs = (
        P(("ep", "tp"), None),
        P(),
        P("ep", None),
        P("ep", None),
        P("ep", None, "tp"),
        P("ep", None, "tp"),
        P("ep", None, "tp"),
    )
    out_specs = P("ep", "tp")
    return jax.shard_map(shards, mesh=mesh, in_specs=in_specs, out_specs=out_specs, check_vma=False)
```

```python
import functools

import jax
import jax.numpy as jnp
from jax import lax
from jax.experimental import pallas as pl
from jax.experimental.pallas import tpu as pltpu
from jax.sharding import PartitionSpec as P

LANES = 128


def factors_of(n):
    digits, stride = [], 1
    for _ in range(2):
        if n % 2 == 0 and n > 1:
            digits.append((stride, 2))
            stride, n = stride * 2, n // 2
    while n > 1:
        radix = 4 if n % 4 == 0 else 2
        digits.append((stride, radix))
        stride, n = stride * radix, n // radix
    return digits


def traded(x, axis, size, stride, radix, by):
    pairs = []
    for i in range(size):
        digit = i // stride % radix
        pairs.append((i, i + ((digit ^ by) - digit) * stride))
    return lax.ppermute(x, axis, pairs)


def trades(blocks, axis, size, stride, radix):
    came = {s: traded(blocks[s], axis, size, stride, radix, s) for s in reversed(range(1, radix))}
    return [blocks[0]] + [came[s] for s in range(1, radix)]


def arrivals(x, axis, size, stride, radix):
    return trades([x] * radix, axis, size, stride, radix)


def pack_kernel(top, pos_ref, ids_ref, weights_ref, values_ref, message_ref, ids, weights, sems):
    tok_dev, width = values_ref.shape
    copies = [
        pltpu.make_async_copy(ids_ref, ids, sems.at[0]),
        pltpu.make_async_copy(weights_ref, weights, sems.at[1]),
        pltpu.make_async_copy(values_ref, message_ref.at[:, pl.ds(0, width)], sems.at[2]),
    ]
    for copy in copies:
        copy.start()
    copies[0].wait()
    copies[1].wait()
    group = ids.shape[1]
    high = weights[...].astype(jnp.bfloat16).astype(jnp.float32)
    rest = weights[...] - high
    mid = rest.astype(jnp.bfloat16).astype(jnp.float32)
    terms = [ids[...].astype(jnp.float32), high, mid, rest - mid]
    terms.append(jnp.zeros((LANES - 4 * top, group), jnp.float32))
    table = jnp.concatenate(terms, axis=0).astype(jnp.bfloat16)
    own = lax.broadcasted_iota(jnp.int32, (tok_dev, group), 0) + pos_ref[0] * tok_dev
    own = (own == lax.broadcasted_iota(jnp.int32, (tok_dev, group), 1)).astype(jnp.float32)
    routing = lax.dot_general(
        own.astype(jnp.bfloat16), table, (((1,), (1,)), ((), ())), preferred_element_type=jnp.float32
    )
    message_ref[:, width:] = routing.astype(jnp.bfloat16)
    copies[2].wait()


def split_kernel(half, *refs):
    pieces, (first_ref, second_ref, token_ref) = refs[:-3], refs[-3:]
    pieces = [ref for ref in pieces if ref.shape[1] > 2 * half]
    whole = jnp.concatenate([ref[...].astype(jnp.float32) for ref in pieces], axis=0).astype(jnp.bfloat16)
    second_ref[...] = whole[:, :half]
    first_ref[...] = whole[:, half:]
    token_ref[...] = jnp.zeros_like(token_ref)


def join_kernel(count, signs, *refs):
    out_ref = refs[count + signs]
    rows = refs[0].shape[0]
    for i, ref in enumerate(refs[:count]):
        out_ref[i * rows : (i + 1) * rows] = ref[...]
    for ref in refs[count + signs + 1 :]:
        ref[...] = jnp.zeros_like(ref)


def load_kernel(experts, signs, *refs):
    count = len(experts)
    refs = refs[:count] + refs[count + signs :]
    far, (sign_ref, *near, sems) = refs[:count], refs[count:]
    copies = load_copies(far, near, sems, experts)
    sign_ref[...] = jnp.zeros_like(sign_ref)
    for copy in copies:
        copy.wait()


def load_copies(far, near, sems, experts):
    copies = []
    for i, (src_ref, dst_ref, expert) in enumerate(zip(far, near, experts)):
        runs = sems.shape[1]
        size = dst_ref.shape[0] // runs
        for r in range(runs):
            at = pl.ds(r * size, size)
            copies.append(pltpu.make_async_copy(src_ref.at[expert, at], dst_ref.at[at], sems.at[i, r]))
    for copy in copies:
        copy.start()
    return copies


def swiglu(normed_ref, gates, ups, hidden_ref, start):
    for i, (gate_ref, up_ref) in enumerate(zip(gates, ups)):
        x = normed_ref[start + i]
        gate_act = jnp.dot(x, gate_ref[...], preferred_element_type=jnp.float32)
        up_act = jnp.dot(x, up_ref[...], preferred_element_type=jnp.float32)
        hidden_ref[i] = (gate_act / (1.0 + jnp.exp(-gate_act)) * up_act).astype(jnp.bfloat16)


def select_body(dims, pos_ref, gain_ref, first, second, gates, ups, hidden_ref, normed_ref, mix_ref, turned_ref):
    n_fast, n_mid, n_tp, slow_n, tok_dev, top, exp_loc, rows, half = dims
    tp_pos, base = pos_ref[0], pos_ref[1]
    run = slow_n * tok_dev
    tokens = n_fast * n_mid * n_tp * run
    routing = jnp.concatenate([ref[:, half:] for ref in first], axis=0).astype(jnp.float32)
    ids = routing[:, :top]
    weights = routing[:, top : 2 * top] + (
        routing[:, 2 * top : 3 * top] + routing[:, 3 * top : 4 * top]
    )

    def number(shape, dim):
        at = lax.broadcasted_iota(jnp.int32, shape, dim)
        tp_at = lax.rem(lax.div(at, n_mid * run), n_tp)
        return at + (lax.rem(tp_pos - tp_at + n_tp, n_tp) - tp_at) * (n_mid * run)

    before = number((tokens, tokens), 1) < number((tokens, tokens), 0)
    match = [ids == (base + e).astype(jnp.float32) for e in range(exp_loc)]
    hits = [jnp.sum(m.astype(jnp.float32), axis=1, keepdims=True) for m in match]
    shares = [jnp.sum(jnp.where(m, weights, 0.0), axis=1, keepdims=True) for m in match]
    lane = lax.broadcasted_iota(jnp.int32, (tokens, LANES), 1)
    hit = functools.reduce(
        lambda a, e: jnp.where(lane == e, hits[e], a),
        range(exp_loc),
        jnp.zeros((tokens, LANES), jnp.float32),
    )
    position = jnp.dot(
        before.astype(jnp.float32).astype(jnp.bfloat16),
        hit.astype(jnp.bfloat16),
        preferred_element_type=jnp.float32,
    )
    slot = lax.broadcasted_iota(jnp.int32, (tokens, rows), 1).astype(jnp.float32)
    picks, spreads = [], []
    for e in range(exp_loc):
        place = jnp.where(hits[e] > 0, position[:, e : e + 1], -1.0)
        pick = slot == place
        picks.append(pick.astype(jnp.float32))
        spreads.append(jnp.where(pick, shares[e], 0.0))
    spread = jnp.concatenate(spreads, axis=1)
    group = lambda f, m, s: [
        spread[start : start + tok_dev]
        for start in [(((f * n_tp + t) * n_mid + m) * slow_n + s) * tok_dev for t in range(n_tp)]
    ]
    blocks = [b for f in range(n_fast) for m in range(n_mid) for s in range(slow_n) for b in group(f, m, s)]
    turned = [b for f in range(n_fast) for s in range(slow_n) for m in range(n_mid) for b in group(f, m, s)]
    for ref, rows_of in ((mix_ref, blocks), (turned_ref, turned)):
        exact = jnp.concatenate(rows_of, axis=0)
        high = exact.astype(jnp.bfloat16)
        ref[0] = high
        ref[1] = (exact - high.astype(jnp.float32)).astype(jnp.bfloat16)

    part = n_mid * n_tp * run
    pick = jnp.concatenate(picks, axis=1)
    swapped = jnp.concatenate(
        [
            pick[f * part + (t * n_mid + m) * run : f * part + (t * n_mid + m + 1) * run]
            for f in range(n_fast)
            for m in range(n_mid)
            for t in range(n_tp)
        ],
        axis=0,
    )
    chosen, swapped = pick.T.astype(jnp.bfloat16), swapped.T.astype(jnp.bfloat16)
    size = min(half, 4 * LANES)
    squares = 0.0
    for begin in range(0, 2 * half, size):
        table, side, at = (swapped, second, begin) if begin < half else (chosen, first, begin - half)
        values = jnp.concatenate([ref[:, at : at + size] for ref in side], axis=0)
        values = jnp.dot(table, values, preferred_element_type=jnp.float32)
        squares = squares + jnp.sum(values * values, axis=1, keepdims=True)
        values = values.astype(jnp.bfloat16)
        for e in range(exp_loc):
            normed_ref[e, :, begin : begin + size] = values[e * rows : (e + 1) * rows]
    scale = lax.rsqrt(squares / (2 * half) + 1e-06)
    gain_all = gain_ref[...].astype(jnp.float32)
    for begin in range(0, 2 * half, size):
        gain = [gain_all[r : r + 1] for r in range(begin // LANES, (begin + size) // LANES)]
        gain = jnp.concatenate(gain, axis=1)
        for e in range(exp_loc):
            values = normed_ref[e, :, begin : begin + size].astype(jnp.float32)
            values = values * scale[e * rows : (e + 1) * rows] * gain
            normed_ref[e, :, begin : begin + size] = values.astype(jnp.bfloat16)
    swiglu(normed_ref, gates, ups, hidden_ref, 0)


def select_kernel(dims, lead, tail, pos_ref, gain_ref, *refs):
    n_fast = dims[0]
    first, second, refs = refs[:n_fast], refs[n_fast : 2 * n_fast], refs[2 * n_fast :]
    gates, ups, refs = refs[:lead], refs[lead : 2 * lead], refs[2 * lead :]
    gate_far, up_far, hidden_ref, normed_ref, mix_ref, turned_ref, *near, sems = refs
    wanted = [(gate_far, lead + tail - 1)] + [(up_far, e) for e in range(lead, lead + tail)]
    copies = load_copies([ref for ref, _ in wanted], near, sems, [e for _, e in wanted])

    @pl.when(pos_ref[0] >= 0)
    def _():
        select_body(dims, pos_ref, gain_ref, first, second, gates, ups, hidden_ref, normed_ref, mix_ref, turned_ref)

    for copy in copies:
        copy.wait()


def up_kernel(start, count, wanted, pos_ref, normed_ref, *refs):
    gates, ups, (far_ref, hidden_ref, *near, sems) = refs[:count], refs[count : 2 * count], refs[2 * count :]
    copies = load_copies([far_ref] * len(near), near, sems, wanted)

    @pl.when(pos_ref[0] >= 0)
    def _():
        swiglu(normed_ref, gates, ups, hidden_ref, start)

    for copy in copies:
        copy.wait()


def lower(tp_pos, n_tp, piece, s, down_ref, columns):
    hid_part = piece.shape[1]
    begin = pl.multiple_of(lax.rem(tp_pos - s + n_tp, n_tp) * hid_part, hid_part)
    return jnp.dot(piece, down_ref[pl.ds(begin, hid_part), columns], preferred_element_type=jnp.float32)


def down_kernel(n_tp, count, pos_ref, own_ref, *refs):
    pieces, (*downs, out_ref, part_ref) = refs[:n_tp], refs[n_tp:]
    _, rows, _ = own_ref.shape
    every = slice(None)
    for i, ref in enumerate(downs[:count]):
        total = sum(lower(pos_ref[0], n_tp, pieces[s][i], s, ref, every) for s in range(n_tp))
        out_ref[i * rows : (i + 1) * rows] = total.astype(jnp.bfloat16)
    for i, ref in enumerate(downs[count:]):
        part_ref[i * rows : (i + 1) * rows] = lower(pos_ref[0], n_tp, own_ref[i], 0, ref, every)


def in_blocks(total, refs):
    rows = refs[0].shape[0]
    for i, ref in enumerate(refs):
        ref[...] = total[i * rows : (i + 1) * rows].astype(jnp.bfloat16)


def mix_kernel(n_tp, count, begin, pos_ref, mix_ref, done_ref, part_ref, *refs):
    pieces, refs = refs[: n_tp - 1], refs[n_tp - 1 :]
    downs, (*partial_refs, out_ref) = refs[:count], refs[count:]
    columns = pl.ds(begin, out_ref.shape[1])
    at = done_ref.shape[0]
    rows = part_ref.shape[0] // count
    out_ref[:at] = done_ref[:, columns]
    for i, ref in enumerate(downs):
        total = part_ref[i * rows : (i + 1) * rows, columns]
        for s in range(1, n_tp):
            total = total + lower(pos_ref[0], n_tp, pieces[s - 1][i], s, ref, columns)
        out_ref[at + i * rows : at + (i + 1) * rows] = total.astype(jnp.bfloat16)
    out = out_ref[...]
    partial = jnp.dot(mix_ref[0], out, preferred_element_type=jnp.float32)
    partial = partial + jnp.dot(mix_ref[1], out, preferred_element_type=jnp.float32)
    in_blocks(partial, partial_refs)


def total_of(refs):
    return functools.reduce(lambda a, ref: a + ref[...].astype(jnp.float32), refs[1:], refs[0][...].astype(jnp.float32))


def sum_kernel(count, signs, blocks, *refs):
    out_refs = refs[count + signs :]
    in_blocks(total_of(refs[:count]), out_refs[:blocks])
    for ref in out_refs[blocks:]:
        ref[...] = jnp.zeros_like(ref)


def own_kernel(dims, pos_ref, first_ref, second_ref, _, out_ref, own_ref):
    n_mid, n_tp, slow_n, tok_dev, half = dims
    col_part = out_ref.shape[1]
    for s in range(n_tp):
        at = s * n_mid * slow_n * tok_dev
        own_ref[s * tok_dev : (s + 1) * tok_dev, half:] = first_ref[at : at + tok_dev, :half].astype(jnp.float32)
        at = s * slow_n * tok_dev
        own_ref[s * tok_dev : (s + 1) * tok_dev, :half] = second_ref[at : at + tok_dev].astype(jnp.float32)
    out_ref[...] = own_ref[:, pl.ds(pl.multiple_of(pos_ref[0] * col_part, col_part), col_part)]


def final_kernel(n_tp, count, pos_ref, own_ref, *refs):
    left, right, out_ref = refs[:count], refs[count:-1], refs[-1]
    begin, tok_dev = 0, own_ref.shape[0] // n_tp
    for side in (left, right):
        columns = pl.ds(begin, side[0].shape[1])
        total = total_of(side) + own_ref[:, columns]
        rows = []
        for j in range(n_tp):
            row = total[:tok_dev]
            for s in range(1, n_tp):
                here = lax.rem(pos_ref[0] - s + n_tp, n_tp) == j
                row = jnp.where(here, total[s * tok_dev : (s + 1) * tok_dev], row)
            rows.append(row)
        out_ref[:, columns] = jnp.concatenate(rows, axis=0).astype(jnp.bfloat16)
        begin += side[0].shape[1]


VMEM = pl.BlockSpec(memory_space=pltpu.VMEM)
SMEM = pl.BlockSpec(memory_space=pltpu.SMEM)
HBM = pl.BlockSpec(memory_space=pltpu.HBM)
KEPT = pltpu.VMEM
TOKEN = jax.ShapeDtypeStruct((8, LANES), jnp.float32)


def local_call(kernel, shapes, operands, far=(), scratch=(), limit=6 << 20, flops=0, moved=0):
    specs, given = [], []
    for i, a in enumerate(operands):
        if i in far:
            specs.append(HBM)
            given.append(pltpu.with_memory_space_constraint(a, pltpu.HBM))
        else:
            specs.append(SMEM if a.dtype == jnp.int32 else VMEM)
            given.append(a)
    return pl.pallas_call(
        kernel,
        out_shape=shapes,
        in_specs=specs,
        out_specs=[VMEM] * len(shapes),
        scratch_shapes=list(scratch),
        compiler_params=pltpu.CompilerParams(vmem_limit_bytes=limit),
        cost_estimate=pl.CostEstimate(flops=flops, bytes_accessed=moved, transcendentals=0),
    )(*given)


def kept(array, count):
    return [KEPT(array.shape[1:], array.dtype)] * count


def runs_of(array):
    return 4 if array.shape[1] % 64 == 0 else 1


def loaded(wanted, after):
    sign, *near = local_call(
        functools.partial(load_kernel, [expert for _, expert in wanted], len(after)),
        [TOKEN] + [KEPT(array.shape[1:], array.dtype) for array, _ in wanted],
        [array for array, _ in wanted] + after,
        far=range(len(wanted)),
        scratch=[pltpu.SemaphoreType.DMA((len(wanted), min(runs_of(array) for array, _ in wanted)))],
        limit=1 << 20,
        moved=2 * sum(array.size // array.shape[0] for array, _ in wanted),
    )
    return near, sign


def summed(pieces, blocks, after, signed):
    rows, columns = pieces[0].shape
    return local_call(
        functools.partial(sum_kernel, len(pieces), len(after), blocks),
        [jax.ShapeDtypeStruct((rows // blocks, columns), pieces[0].dtype)] * blocks + [TOKEN] * signed,
        list(pieces) + after,
        limit=4 << 20,
        moved=2 * (len(pieces) + 1) * rows * columns,
    )


def joined(pieces, after, signed):
    rows, columns = pieces[0].shape
    return local_call(
        functools.partial(join_kernel, len(pieces), len(after)),
        [jax.ShapeDtypeStruct((len(pieces) * rows, columns), pieces[0].dtype)] + [TOKEN] * signed,
        list(pieces) + after,
        limit=4 << 20,
        moved=4 * len(pieces) * rows * columns,
    )


def by_tokens(hidden_in, norm_gain, expert_ids, gate_weights, w_gate, w_up, w_down):
    n_ep = lax.axis_size("ep")
    n_tp = lax.axis_size("tp")
    ep_pos = lax.axis_index("ep")
    tp_pos = lax.axis_index("tp")
    tok_dev, width = hidden_in.shape
    group, top = expert_ids.shape
    exp_loc, _, hid_part = w_gate.shape
    col_part = w_down.shape[2]
    experts = exp_loc * n_ep
    cap = max(2, 2 * top * group // experts)
    rows = cap * n_ep
    tokens = group * n_ep
    digits = factors_of(n_ep)
    fast, mid, slow = digits[0], digits[1:2], digits[2:]
    half = width // 2
    slow_n = n_ep
    for _, radix in [fast] + mid:
        slow_n //= radix
    n_fast, n_mid = fast[1], mid[0][1] if mid else 1

    bf16 = functools.partial(jax.ShapeDtypeStruct, dtype=jnp.bfloat16)
    slots = exp_loc * rows
    lead = exp_loc - exp_loc // 2
    tail = exp_loc - lead
    gain = norm_gain.reshape(width // LANES, LANES)
    position = jnp.stack([tp_pos, ep_pos * exp_loc])
    (message,) = local_call(
        functools.partial(pack_kernel, top),
        [bf16((tok_dev, width + LANES))],
        [position, expert_ids.T, gate_weights.T, hidden_in],
        far=[1, 2, 3],
        scratch=[
            pltpu.VMEM((top, group), jnp.int32),
            pltpu.VMEM((top, group), jnp.float32),
            pltpu.SemaphoreType.DMA((3,)),
        ],
        limit=4 << 20,
    )
    around = [message]
    for digit in reversed(slow):
        around = [a for piece in around for a in arrivals(piece, "ep", n_ep, *digit)]
    loads, sign = loaded([(w_gate, e) for e in range(lead)] + [(w_up, 0)], [])
    gate_lead, up_lead = loads[:lead], loads[lead:]
    first, second, sign = local_call(
        functools.partial(split_kernel, half),
        [bf16((slow_n * tok_dev, width + LANES - half)), bf16((slow_n * tok_dev, half)), TOKEN],
        around + [sign],
        limit=4 << 20,
    )
    gate_tail, sign = loaded([(w_gate, e) for e in range(lead, exp_loc - 1)], [sign]) if tail > 1 else ([], sign)
    along_tp = lambda a: arrivals(a, "tp", n_tp, 1, n_tp)
    along_mid = lambda a: arrivals(a, "ep", n_ep, *mid[0]) if mid else [a]
    first, second = along_mid(first), along_tp(second)
    first, sign = joined(first, [sign], 1)
    (second,) = joined(second, [], 0)
    loads, sign = loaded([(w_up, e) for e in range(1, lead)] + [(w_down, e) for e in range(lead)], [sign])
    up_lead, down_lead = up_lead + loads[: lead - 1], loads[lead - 1 :]
    first, second = along_tp(first), along_mid(second)
    (first,) = joined(first, [sign], 0)
    (second,) = joined(second, [], 0)
    first = arrivals(first, "ep", n_ep, *fast)
    second = arrivals(second, "ep", n_ep, *fast)

    dims = (n_fast, n_mid, n_tp, slow_n, tok_dev, top, exp_loc, rows, half)
    sems = lambda array, count: pltpu.SemaphoreType.DMA((count, runs_of(array)))
    operands = [position, gain] + first + second + gate_lead + up_lead + [w_gate, w_up]
    hidden, normed, mix, turned, gate_last, *up_tail = local_call(
        functools.partial(select_kernel, dims, lead, tail),
        [
            bf16((lead, rows, hid_part)),
            bf16((exp_loc, rows, width)),
            bf16((2, tokens, slots)),
            bf16((2, tokens, slots)),
        ]
        + kept(w_gate, 1)
        + kept(w_up, tail),
        operands,
        far=[len(operands) - 2, len(operands) - 1],
        scratch=[sems(w_up, 1 + tail)],
        flops=2 * slots * tokens * width + 4 * lead * rows * width * hid_part,
        moved=4 * lead * width * hid_part,
    )
    pieces = along_tp(hidden)
    operands = [position, normed] + gate_tail + [gate_last] + up_tail + [w_down]
    hidden, *down_tail = local_call(
        functools.partial(up_kernel, lead, tail, range(lead, exp_loc)),
        [bf16((tail, rows, hid_part))] + kept(w_down, tail),
        operands,
        far=[len(operands) - 1],
        scratch=[sems(w_down, tail)],
        flops=4 * tail * rows * width * hid_part,
        moved=4 * tail * width * hid_part,
    )
    late = along_tp(hidden)
    done, part = local_call(
        functools.partial(down_kernel, n_tp, lead),
        [bf16((lead * rows, col_part)), jax.ShapeDtypeStruct((tail * rows, col_part), jnp.float32)],
        [position, late[0]] + pieces + down_lead + down_tail,
        flops=2 * lead * rows * n_tp * hid_part * col_part,
        moved=2 * lead * n_tp * hid_part * col_part,
    )
    left_cols = col_part * 5 // 8 // LANES * LANES
    right_cols = col_part - left_cols
    mixed_of = lambda table, begin, size: local_call(
        functools.partial(mix_kernel, n_tp, tail, begin),
        [bf16((tokens // n_fast, size))] * n_fast,
        [position, table, done, part] + late[1:] + down_tail,
        scratch=[pltpu.VMEM((slots, size), jnp.bfloat16)],
        flops=2 * slots * n_tp * hid_part * size,
        moved=2 * tail * n_tp * hid_part * size,
    )

    def swapped(blocks, digit):
        own, *others = trades(blocks, "ep", n_ep, *digit)
        return [own] + others[::-1]

    slow = list(reversed(slow))
    right_way, left_way = slow + mid, mid + slow
    right = summed(swapped(mixed_of(turned, left_cols, right_cols), fast), right_way[0][1], [], 0)
    left = summed(swapped(mixed_of(mix, 0, left_cols), fast), left_way[0][1], [], 0)
    signs = []
    for digit, later in zip(left_way[:-1], left_way[1:]):
        *left, late_sign = summed(swapped(left, digit), later[1], [], 1)
        signs.append(late_sign)
    for digit, later in zip(right_way[:-1], right_way[1:]):
        right = summed(swapped(right, digit), later[1], signs, 0)
        signs = []
    left = swapped(left, left_way[-1])
    right = swapped(right, right_way[-1])
    (own,) = local_call(
        functools.partial(own_kernel, (n_mid, n_tp, slow_n, tok_dev, half)),
        [jax.ShapeDtypeStruct((group, col_part), jnp.float32)],
        [position, first[0], second[0], late_sign],
        scratch=[pltpu.VMEM((group, width), jnp.float32)],
        limit=4 << 20,
        moved=4 * group * width,
    )
    (mixed,) = local_call(
        functools.partial(final_kernel, n_tp, len(left)),
        [bf16((group, col_part))],
        [position, own] + left + right,
        limit=4 << 20,
        moved=2 * group * 8 * col_part,
    )
    return mixed


def by_slots(hidden_in, norm_gain, expert_ids, gate_weights, w_gate, w_up, w_down):
    n_ep = lax.axis_size("ep")
    tp_pos = lax.axis_index("tp")
    tok_dev, width = hidden_in.shape
    group, top = expert_ids.shape
    exp_loc, _, hid_part = w_gate.shape
    col_part = w_down.shape[2]
    experts = exp_loc * n_ep
    cap = max(2, 2 * top * group // experts)
    values = hidden_in.astype(jnp.float32)
    scale = lax.rsqrt(jnp.mean(values * values, axis=1, keepdims=True) + 1e-06)
    normed = (values * scale * norm_gain.astype(jnp.float32)).astype(jnp.bfloat16)
    flat_ids = expert_ids.reshape(-1)
    pairs = flat_ids.shape[0]
    hits = (flat_ids[:, None] == lax.broadcasted_iota(jnp.int32, (pairs, experts), 1)).astype(
        jnp.int32
    )
    before = jnp.cumsum(hits, axis=0) - hits
    position = jnp.sum(before * hits, axis=1)
    slot_index = flat_ids * cap + position
    places = lax.broadcasted_iota(jnp.int32, (experts * cap, group, top), 0)
    dispatch_map = jnp.any(places == slot_index.reshape(group, top)[None], axis=2).astype(
        jnp.bfloat16
    )
    whole_norm, whole_input = (
        lax.all_gather(normed, "tp", axis=0, tiled=True),
        lax.all_gather(hidden_in, "tp", axis=0, tiled=True),
    )
    residual = lax.dynamic_slice_in_dim(whole_input, tp_pos * col_part, col_part, 1)
    packed = jnp.dot(dispatch_map, whole_norm, preferred_element_type=jnp.float32).astype(
        jnp.bfloat16
    )
    packed = packed.reshape(n_ep, exp_loc, cap, width)
    arrived = lax.all_to_all(packed, "ep", split_axis=0, concat_axis=0, tiled=True)
    gate_act = jnp.einsum("secd,edh->sech", arrived, w_gate, preferred_element_type=jnp.float32)
    up_act = jnp.einsum("secd,edh->sech", arrived, w_up, preferred_element_type=jnp.float32)
    hidden = (jax.nn.silu(gate_act) * up_act).astype(jnp.bfloat16)
    outputs = jnp.einsum(
        "sech,ehf->secf",
        lax.all_gather(hidden, "tp", axis=3, tiled=True),
        w_down,
        preferred_element_type=jnp.float32,
    )
    returned = lax.all_to_all(
        outputs.astype(jnp.bfloat16), "ep", split_axis=0, concat_axis=0, tiled=True
    )
    flat_back = returned.reshape(experts * cap, col_part)
    picked = flat_back[slot_index].reshape(group, top, col_part).astype(jnp.float32)
    combined = jnp.sum(picked * gate_weights[:, :, None], axis=1)
    return (residual.astype(jnp.float32) + combined).astype(jnp.bfloat16)


def shards(hidden_in, norm_gain, expert_ids, gate_weights, w_gate, w_up, w_down):
    group, top = expert_ids.shape
    exp_loc = w_gate.shape[0]
    cap = max(2, 2 * top * group // (exp_loc * lax.axis_size("ep")))
    n_ep = lax.axis_size("ep")
    whole = exp_loc > 1 and exp_loc * cap >= group and n_ep > 4 and n_ep & (n_ep - 1) == 0
    plan = by_tokens if whole else by_slots
    return plan(hidden_in, norm_gain, expert_ids, gate_weights, w_gate, w_up, w_down)


def solution(mesh):
    in_specs = (
        P(("ep", "tp"), None),
        P(),
        P("ep", None),
        P("ep", None),
        P("ep", None, "tp"),
        P("ep", None, "tp"),
        P("ep", None, "tp"),
    )
    out_specs = P("ep", "tp")
    return jax.shard_map(shards, mesh=mesh, in_specs=in_specs, out_specs=out_specs, check_vma=False)
```

```python
import functools

import jax
import jax.numpy as jnp
from jax import lax
from jax.experimental import pallas as pl
from jax.experimental.pallas import tpu as pltpu
from jax.sharding import PartitionSpec as P

LANES = 128


def factors_of(n):
    digits, stride = [], 1
    for _ in range(2):
        if n % 2 == 0 and n > 1:
            digits.append((stride, 2))
            stride, n = stride * 2, n // 2
    while n > 1:
        radix = 4 if n % 4 == 0 else 2
        digits.append((stride, radix))
        stride, n = stride * radix, n // radix
    return digits


def traded(x, axis, size, stride, radix, by):
    pairs = []
    for i in range(size):
        digit = i // stride % radix
        pairs.append((i, i + ((digit ^ by) - digit) * stride))
    return lax.ppermute(x, axis, pairs)


def trades(blocks, axis, size, stride, radix):
    came = {s: traded(blocks[s], axis, size, stride, radix, s) for s in reversed(range(1, radix))}
    return [blocks[0]] + [came[s] for s in range(1, radix)]


def arrivals(x, axis, size, stride, radix):
    return trades([x] * radix, axis, size, stride, radix)


def pack_kernel(top, pos_ref, ids_ref, weights_ref, values_ref, message_ref, ids, weights, sems):
    tok_dev, width = values_ref.shape
    copies = [
        pltpu.make_async_copy(ids_ref, ids, sems.at[0]),
        pltpu.make_async_copy(weights_ref, weights, sems.at[1]),
        pltpu.make_async_copy(values_ref, message_ref.at[:, pl.ds(0, width)], sems.at[2]),
    ]
    for copy in copies:
        copy.start()
    copies[0].wait()
    copies[1].wait()
    group = ids.shape[1]
    high = weights[...].astype(jnp.bfloat16).astype(jnp.float32)
    rest = weights[...] - high
    mid = rest.astype(jnp.bfloat16).astype(jnp.float32)
    terms = [ids[...].astype(jnp.float32), high, mid, rest - mid]
    terms.append(jnp.zeros((LANES - 4 * top, group), jnp.float32))
    table = jnp.concatenate(terms, axis=0).astype(jnp.bfloat16)
    own = lax.broadcasted_iota(jnp.int32, (tok_dev, group), 0) + pos_ref[0] * tok_dev
    own = (own == lax.broadcasted_iota(jnp.int32, (tok_dev, group), 1)).astype(jnp.float32)
    routing = lax.dot_general(
        own.astype(jnp.bfloat16), table, (((1,), (1,)), ((), ())), preferred_element_type=jnp.float32
    )
    message_ref[:, width:] = routing.astype(jnp.bfloat16)
    copies[2].wait()


def split_kernel(half, *refs):
    pieces, (first_ref, second_ref, token_ref) = refs[:-3], refs[-3:]
    pieces = [ref for ref in pieces if ref.shape[1] > 2 * half]
    whole = jnp.concatenate([ref[...].astype(jnp.float32) for ref in pieces], axis=0).astype(jnp.bfloat16)
    second_ref[...] = whole[:, :half]
    first_ref[...] = whole[:, half:]
    token_ref[...] = jnp.zeros_like(token_ref)


def join_kernel(count, signs, *refs):
    out_ref = refs[count + signs]
    rows = refs[0].shape[0]
    for i, ref in enumerate(refs[:count]):
        out_ref[i * rows : (i + 1) * rows] = ref[...]
    for ref in refs[count + signs + 1 :]:
        ref[...] = jnp.zeros_like(ref)


def load_kernel(experts, signs, *refs):
    count = len(experts)
    refs = refs[:count] + refs[count + signs :]
    far, (sign_ref, *near, sems) = refs[:count], refs[count:]
    copies = load_copies(far, near, sems, experts)
    sign_ref[...] = jnp.zeros_like(sign_ref)
    for copy in copies:
        copy.wait()


def load_copies(far, near, sems, experts):
    copies = []
    for i, (src_ref, dst_ref, expert) in enumerate(zip(far, near, experts)):
        runs = sems.shape[1]
        size = dst_ref.shape[0] // runs
        for r in range(runs):
            at = pl.ds(r * size, size)
            copies.append(pltpu.make_async_copy(src_ref.at[expert, at], dst_ref.at[at], sems.at[i, r]))
    for copy in copies:
        copy.start()
    return copies


def swiglu(normed_ref, gates, ups, hidden_ref, start):
    for i, (gate_ref, up_ref) in enumerate(zip(gates, ups)):
        x = normed_ref[start + i]
        gate_act = jnp.dot(x, gate_ref[...], preferred_element_type=jnp.float32)
        up_act = jnp.dot(x, up_ref[...], preferred_element_type=jnp.float32)
        hidden_ref[i] = (gate_act / (1.0 + jnp.exp(-gate_act)) * up_act).astype(jnp.bfloat16)


def route_kernel(dims, pos_ref, *refs):
    n_fast, n_mid, n_tp, slow_n, tok_dev, top, exp_loc, rows, half = dims
    first, (right_ref, squares_ref, swapped_ref, mix_ref, turned_ref) = refs[:n_fast], refs[n_fast:]
    tp_pos, base = pos_ref[0], pos_ref[1]
    run = slow_n * tok_dev
    tokens = n_fast * n_mid * n_tp * run
    routing = jnp.concatenate([ref[:, half:] for ref in first], axis=0).astype(jnp.float32)
    ids = routing[:, :top]
    weights = routing[:, top : 2 * top] + (
        routing[:, 2 * top : 3 * top] + routing[:, 3 * top : 4 * top]
    )

    def number(shape, dim):
        at = lax.broadcasted_iota(jnp.int32, shape, dim)
        tp_at = lax.rem(lax.div(at, n_mid * run), n_tp)
        return at + (lax.rem(tp_pos - tp_at + n_tp, n_tp) - tp_at) * (n_mid * run)

    before = number((tokens, tokens), 1) < number((tokens, tokens), 0)
    match = [ids == (base + e).astype(jnp.float32) for e in range(exp_loc)]
    hits = [jnp.sum(m.astype(jnp.float32), axis=1, keepdims=True) for m in match]
    shares = [jnp.sum(jnp.where(m, weights, 0.0), axis=1, keepdims=True) for m in match]
    lane = lax.broadcasted_iota(jnp.int32, (tokens, LANES), 1)
    hit = functools.reduce(
        lambda a, e: jnp.where(lane == e, hits[e], a),
        range(exp_loc),
        jnp.zeros((tokens, LANES), jnp.float32),
    )
    position = jnp.dot(
        before.astype(jnp.float32).astype(jnp.bfloat16),
        hit.astype(jnp.bfloat16),
        preferred_element_type=jnp.float32,
    )
    slot = lax.broadcasted_iota(jnp.int32, (tokens, rows), 1).astype(jnp.float32)
    picks, spreads = [], []
    for e in range(exp_loc):
        place = jnp.where(hits[e] > 0, position[:, e : e + 1], -1.0)
        pick = slot == place
        picks.append(pick.astype(jnp.float32))
        spreads.append(jnp.where(pick, shares[e], 0.0))
    spread = jnp.concatenate(spreads, axis=1)
    group = lambda f, m, s: [
        spread[start : start + tok_dev]
        for start in [(((f * n_tp + t) * n_mid + m) * slow_n + s) * tok_dev for t in range(n_tp)]
    ]
    blocks = [b for f in range(n_fast) for m in range(n_mid) for s in range(slow_n) for b in group(f, m, s)]
    turned = [b for f in range(n_fast) for s in range(slow_n) for m in range(n_mid) for b in group(f, m, s)]
    for ref, rows_of in ((mix_ref, blocks), (turned_ref, turned)):
        exact = jnp.concatenate(rows_of, axis=0)
        high = exact.astype(jnp.bfloat16)
        ref[0] = high
        ref[1] = (exact - high.astype(jnp.float32)).astype(jnp.bfloat16)

    part = n_mid * n_tp * run
    pick = jnp.concatenate(picks, axis=1)
    swapped = jnp.concatenate(
        [
            pick[f * part + (t * n_mid + m) * run : f * part + (t * n_mid + m + 1) * run]
            for f in range(n_fast)
            for m in range(n_mid)
            for t in range(n_tp)
        ],
        axis=0,
    )
    swapped_ref[...] = swapped.T.astype(jnp.bfloat16)
    squares = choose(pick.T.astype(jnp.bfloat16), first, right_ref, half)
    squares_ref[...] = jnp.broadcast_to(squares, squares_ref.shape)


def choose(table, pieces, out_ref, half):
    exp_loc, rows, _ = out_ref.shape
    size, squares = min(half, 4 * LANES), 0.0
    for begin in range(0, half, size):
        values = jnp.concatenate([ref[:, begin : begin + size] for ref in pieces], axis=0)
        values = jnp.dot(table, values, preferred_element_type=jnp.float32)
        squares = squares + jnp.sum(values * values, axis=1, keepdims=True)
        values = values.astype(jnp.bfloat16)
        for e in range(exp_loc):
            out_ref[e, :, begin : begin + size] = values[e * rows : (e + 1) * rows]
    return squares


def select_body(half, gain_ref, right_ref, squares_ref, swapped_ref, second, gates, ups, hidden_ref, normed_ref):
    exp_loc, rows, _ = normed_ref.shape
    squares = squares_ref[:, :1] + choose(swapped_ref[...], second, normed_ref, half)
    scale = lax.rsqrt(squares / (2 * half) + 1e-06)
    gain_all = gain_ref[...].astype(jnp.float32)
    size = min(half, 4 * LANES)
    for begin in range(0, 2 * half, size):
        gain = [gain_all[r : r + 1] for r in range(begin // LANES, (begin + size) // LANES)]
        gain = jnp.concatenate(gain, axis=1)
        source, at = (normed_ref, begin) if begin < half else (right_ref, begin - half)
        for e in range(exp_loc):
            values = source[e, :, at : at + size].astype(jnp.float32)
            values = values * scale[e * rows : (e + 1) * rows] * gain
            normed_ref[e, :, begin : begin + size] = values.astype(jnp.bfloat16)
    swiglu(normed_ref, gates, ups, hidden_ref, 0)


def select_kernel(half, n_fast, lead, tail, pos_ref, gain_ref, right_ref, squares_ref, swapped_ref, *refs):
    second, refs = refs[:n_fast], refs[n_fast:]
    gates, ups, refs = refs[:lead], refs[lead : 2 * lead], refs[2 * lead :]
    gate_far, up_far, hidden_ref, normed_ref, *near, sems = refs
    wanted = [(gate_far, lead + tail - 1)] + [(up_far, e) for e in range(lead, lead + tail)]
    copies = load_copies([ref for ref, _ in wanted], near, sems, [e for _, e in wanted])

    @pl.when(pos_ref[0] >= 0)
    def _():
        select_body(half, gain_ref, right_ref, squares_ref, swapped_ref, second, gates, ups, hidden_ref, normed_ref)

    for copy in copies:
        copy.wait()


def up_kernel(start, count, wanted, pos_ref, normed_ref, *refs):
    gates, ups, (far_ref, hidden_ref, *near, sems) = refs[:count], refs[count : 2 * count], refs[2 * count :]
    copies = load_copies([far_ref] * len(near), near, sems, wanted)

    @pl.when(pos_ref[0] >= 0)
    def _():
        swiglu(normed_ref, gates, ups, hidden_ref, start)

    for copy in copies:
        copy.wait()


def lower(tp_pos, n_tp, piece, s, down_ref, columns):
    hid_part = piece.shape[1]
    begin = pl.multiple_of(lax.rem(tp_pos - s + n_tp, n_tp) * hid_part, hid_part)
    return jnp.dot(piece, down_ref[pl.ds(begin, hid_part), columns], preferred_element_type=jnp.float32)


def down_kernel(n_tp, count, pos_ref, own_ref, *refs):
    pieces, (*downs, out_ref, part_ref) = refs[:n_tp], refs[n_tp:]
    _, rows, _ = own_ref.shape
    every = slice(None)
    for i, ref in enumerate(downs[:count]):
        total = sum(lower(pos_ref[0], n_tp, pieces[s][i], s, ref, every) for s in range(n_tp))
        out_ref[i * rows : (i + 1) * rows] = total.astype(jnp.bfloat16)
    for i, ref in enumerate(downs[count:]):
        part_ref[i * rows : (i + 1) * rows] = lower(pos_ref[0], n_tp, own_ref[i], 0, ref, every)


def in_blocks(total, refs):
    rows = refs[0].shape[0]
    for i, ref in enumerate(refs):
        ref[...] = total[i * rows : (i + 1) * rows].astype(jnp.bfloat16)


def mix_kernel(n_tp, count, begin, pos_ref, mix_ref, done_ref, part_ref, *refs):
    pieces, refs = refs[: n_tp - 1], refs[n_tp - 1 :]
    downs, (*partial_refs, out_ref) = refs[:count], refs[count:]
    columns = pl.ds(begin, out_ref.shape[1])
    at = done_ref.shape[0]
    rows = part_ref.shape[0] // count
    out_ref[:at] = done_ref[:, columns]
    for i, ref in enumerate(downs):
        total = part_ref[i * rows : (i + 1) * rows, columns]
        for s in range(1, n_tp):
            total = total + lower(pos_ref[0], n_tp, pieces[s - 1][i], s, ref, columns)
        out_ref[at + i * rows : at + (i + 1) * rows] = total.astype(jnp.bfloat16)
    out = out_ref[...]
    partial = jnp.dot(mix_ref[0], out, preferred_element_type=jnp.float32)
    partial = partial + jnp.dot(mix_ref[1], out, preferred_element_type=jnp.float32)
    in_blocks(partial, partial_refs)


def total_of(refs):
    return functools.reduce(lambda a, ref: a + ref[...].astype(jnp.float32), refs[1:], refs[0][...].astype(jnp.float32))


def sum_kernel(count, signs, blocks, *refs):
    out_refs = refs[count + signs :]
    in_blocks(total_of(refs[:count]), out_refs[:blocks])
    for ref in out_refs[blocks:]:
        ref[...] = jnp.zeros_like(ref)


def own_kernel(dims, pos_ref, first_ref, second_ref, _, out_ref, own_ref):
    n_mid, n_tp, slow_n, tok_dev, half = dims
    col_part = out_ref.shape[1]
    for s in range(n_tp):
        at = s * n_mid * slow_n * tok_dev
        own_ref[s * tok_dev : (s + 1) * tok_dev, half:] = first_ref[at : at + tok_dev, :half].astype(jnp.float32)
        at = s * slow_n * tok_dev
        own_ref[s * tok_dev : (s + 1) * tok_dev, :half] = second_ref[at : at + tok_dev].astype(jnp.float32)
    out_ref[...] = own_ref[:, pl.ds(pl.multiple_of(pos_ref[0] * col_part, col_part), col_part)]


def final_kernel(n_tp, count, pos_ref, own_ref, *refs):
    left, right, out_ref = refs[:count], refs[count:-1], refs[-1]
    begin, tok_dev = 0, own_ref.shape[0] // n_tp
    for side in (left, right):
        columns = pl.ds(begin, side[0].shape[1])
        total = total_of(side) + own_ref[:, columns]
        rows = []
        for j in range(n_tp):
            row = total[:tok_dev]
            for s in range(1, n_tp):
                here = lax.rem(pos_ref[0] - s + n_tp, n_tp) == j
                row = jnp.where(here, total[s * tok_dev : (s + 1) * tok_dev], row)
            rows.append(row)
        out_ref[:, columns] = jnp.concatenate(rows, axis=0).astype(jnp.bfloat16)
        begin += side[0].shape[1]


VMEM = pl.BlockSpec(memory_space=pltpu.VMEM)
SMEM = pl.BlockSpec(memory_space=pltpu.SMEM)
HBM = pl.BlockSpec(memory_space=pltpu.HBM)
KEPT = pltpu.VMEM
TOKEN = jax.ShapeDtypeStruct((8, LANES), jnp.float32)


def local_call(kernel, shapes, operands, far=(), scratch=(), limit=6 << 20, flops=0, moved=0):
    specs, given = [], []
    for i, a in enumerate(operands):
        if i in far:
            specs.append(HBM)
            given.append(pltpu.with_memory_space_constraint(a, pltpu.HBM))
        else:
            specs.append(SMEM if a.dtype == jnp.int32 else VMEM)
            given.append(a)
    return pl.pallas_call(
        kernel,
        out_shape=shapes,
        in_specs=specs,
        out_specs=[VMEM] * len(shapes),
        scratch_shapes=list(scratch),
        compiler_params=pltpu.CompilerParams(vmem_limit_bytes=limit),
        cost_estimate=pl.CostEstimate(flops=flops, bytes_accessed=moved, transcendentals=0),
    )(*given)


def kept(array, count):
    return [KEPT(array.shape[1:], array.dtype)] * count


def runs_of(array):
    return 4 if array.shape[1] % 64 == 0 else 1


def loaded(wanted, after):
    sign, *near = local_call(
        functools.partial(load_kernel, [expert for _, expert in wanted], len(after)),
        [TOKEN] + [KEPT(array.shape[1:], array.dtype) for array, _ in wanted],
        [array for array, _ in wanted] + after,
        far=range(len(wanted)),
        scratch=[pltpu.SemaphoreType.DMA((len(wanted), min(runs_of(array) for array, _ in wanted)))],
        limit=1 << 20,
        moved=2 * sum(array.size // array.shape[0] for array, _ in wanted),
    )
    return near, sign


def summed(pieces, blocks, after, signed):
    rows, columns = pieces[0].shape
    return local_call(
        functools.partial(sum_kernel, len(pieces), len(after), blocks),
        [jax.ShapeDtypeStruct((rows // blocks, columns), pieces[0].dtype)] * blocks + [TOKEN] * signed,
        list(pieces) + after,
        limit=4 << 20,
        moved=2 * (len(pieces) + 1) * rows * columns,
    )


def joined(pieces, after, signed):
    rows, columns = pieces[0].shape
    return local_call(
        functools.partial(join_kernel, len(pieces), len(after)),
        [jax.ShapeDtypeStruct((len(pieces) * rows, columns), pieces[0].dtype)] + [TOKEN] * signed,
        list(pieces) + after,
        limit=4 << 20,
        moved=4 * len(pieces) * rows * columns,
    )


def by_tokens(hidden_in, norm_gain, expert_ids, gate_weights, w_gate, w_up, w_down):
    n_ep = lax.axis_size("ep")
    n_tp = lax.axis_size("tp")
    ep_pos = lax.axis_index("ep")
    tp_pos = lax.axis_index("tp")
    tok_dev, width = hidden_in.shape
    group, top = expert_ids.shape
    exp_loc, _, hid_part = w_gate.shape
    col_part = w_down.shape[2]
    experts = exp_loc * n_ep
    cap = max(2, 2 * top * group // experts)
    rows = cap * n_ep
    tokens = group * n_ep
    digits = factors_of(n_ep)
    fast, mid, slow = digits[0], digits[1:2], digits[2:]
    half = width // 2
    slow_n = n_ep
    for _, radix in [fast] + mid:
        slow_n //= radix
    n_fast, n_mid = fast[1], mid[0][1] if mid else 1

    bf16 = functools.partial(jax.ShapeDtypeStruct, dtype=jnp.bfloat16)
    slots = exp_loc * rows
    lead = exp_loc - exp_loc // 2
    tail = exp_loc - lead
    gain = norm_gain.reshape(width // LANES, LANES)
    position = jnp.stack([tp_pos, ep_pos * exp_loc])
    (message,) = local_call(
        functools.partial(pack_kernel, top),
        [bf16((tok_dev, width + LANES))],
        [position, expert_ids.T, gate_weights.T, hidden_in],
        far=[1, 2, 3],
        scratch=[
            pltpu.VMEM((top, group), jnp.int32),
            pltpu.VMEM((top, group), jnp.float32),
            pltpu.SemaphoreType.DMA((3,)),
        ],
        limit=4 << 20,
    )
    around = [message]
    for digit in reversed(slow):
        around = [a for piece in around for a in arrivals(piece, "ep", n_ep, *digit)]
    loads, sign = loaded([(w_gate, e) for e in range(lead)] + [(w_up, 0)], [])
    gate_lead, up_lead = loads[:lead], loads[lead:]
    first, second, sign = local_call(
        functools.partial(split_kernel, half),
        [bf16((slow_n * tok_dev, width + LANES - half)), bf16((slow_n * tok_dev, half)), TOKEN],
        around + [sign],
        limit=4 << 20,
    )
    gate_tail, sign = loaded([(w_gate, e) for e in range(lead, exp_loc - 1)], [sign]) if tail > 1 else ([], sign)
    along_tp = lambda a: arrivals(a, "tp", n_tp, 1, n_tp)
    along_mid = lambda a: arrivals(a, "ep", n_ep, *mid[0]) if mid else [a]
    first, second = along_mid(first), along_tp(second)
    first, sign = joined(first, [sign], 1)
    (second,) = joined(second, [], 0)
    loads, sign = loaded([(w_up, e) for e in range(1, lead)] + [(w_down, e) for e in range(lead - 1)], [sign])
    up_lead, down_lead = up_lead + loads[: lead - 1], loads[lead - 1 :]
    first, second = along_tp(first), along_mid(second)
    (first,) = joined(first, [sign], 0)
    (second,) = joined(second, [], 0)
    first = arrivals(first, "ep", n_ep, *fast)
    second = arrivals(second, "ep", n_ep, *fast)

    dims = (n_fast, n_mid, n_tp, slow_n, tok_dev, top, exp_loc, rows, half)
    sems = lambda array, count: pltpu.SemaphoreType.DMA((count, runs_of(array)))
    right, squares, swapped, mix, turned = local_call(
        functools.partial(route_kernel, dims),
        [
            bf16((exp_loc, rows, half)),
            jax.ShapeDtypeStruct((slots, LANES), jnp.float32),
            bf16((slots, tokens)),
            bf16((2, tokens, slots)),
            bf16((2, tokens, slots)),
        ],
        [position] + first,
        flops=slots * tokens * width,
        moved=4 * slots * width,
    )
    operands = [position, gain, right, squares, swapped] + second + gate_lead + up_lead + [w_gate, w_up]
    hidden, normed, gate_last, *up_tail = local_call(
        functools.partial(select_kernel, half, n_fast, lead, tail),
        [bf16((lead, rows, hid_part)), bf16((exp_loc, rows, width))]
        + kept(w_gate, 1)
        + kept(w_up, tail),
        operands,
        far=[len(operands) - 2, len(operands) - 1],
        scratch=[sems(w_up, 1 + tail)],
        flops=slots * tokens * width + 4 * lead * rows * width * hid_part,
        moved=4 * lead * width * hid_part,
    )
    pieces = along_tp(hidden)
    operands = [position, normed] + gate_tail + [gate_last] + up_tail + [w_down]
    hidden, *down_tail = local_call(
        functools.partial(up_kernel, lead, tail, range(lead - 1, exp_loc)),
        [bf16((tail, rows, hid_part))] + kept(w_down, tail + 1),
        operands,
        far=[len(operands) - 1],
        scratch=[sems(w_down, tail + 1)],
        flops=4 * tail * rows * width * hid_part,
        moved=4 * tail * width * hid_part,
    )
    down_lead, down_tail = down_lead + down_tail[:1], down_tail[1:]
    late = along_tp(hidden)
    done, part = local_call(
        functools.partial(down_kernel, n_tp, lead),
        [bf16((lead * rows, col_part)), jax.ShapeDtypeStruct((tail * rows, col_part), jnp.float32)],
        [position, late[0]] + pieces + down_lead + down_tail,
        flops=2 * lead * rows * n_tp * hid_part * col_part,
        moved=2 * lead * n_tp * hid_part * col_part,
    )
    left_cols = col_part * 5 // 8 // LANES * LANES
    right_cols = col_part - left_cols
    mixed_of = lambda table, begin, size: local_call(
        functools.partial(mix_kernel, n_tp, tail, begin),
        [bf16((tokens // n_fast, size))] * n_fast,
        [position, table, done, part] + late[1:] + down_tail,
        scratch=[pltpu.VMEM((slots, size), jnp.bfloat16)],
        flops=2 * slots * n_tp * hid_part * size,
        moved=2 * tail * n_tp * hid_part * size,
    )

    def around(blocks, digit):
        own, *others = trades(blocks, "ep", n_ep, *digit)
        return [own] + others[::-1]

    slow = list(reversed(slow))
    right_way, left_way = slow + mid, mid + slow
    right = summed(around(mixed_of(turned, left_cols, right_cols), fast), right_way[0][1], [], 0)
    left = summed(around(mixed_of(mix, 0, left_cols), fast), left_way[0][1], [], 0)
    signs = []
    for digit, later in zip(left_way[:-1], left_way[1:]):
        *left, late_sign = summed(around(left, digit), later[1], [], 1)
        signs.append(late_sign)
    for digit, later in zip(right_way[:-1], right_way[1:]):
        right = summed(around(right, digit), later[1], signs, 0)
        signs = []
    left = around(left, left_way[-1])
    right = around(right, right_way[-1])
    (own,) = local_call(
        functools.partial(own_kernel, (n_mid, n_tp, slow_n, tok_dev, half)),
        [jax.ShapeDtypeStruct((group, col_part), jnp.float32)],
        [position, first[0], second[0], late_sign],
        scratch=[pltpu.VMEM((group, width), jnp.float32)],
        limit=4 << 20,
        moved=4 * group * width,
    )
    (mixed,) = local_call(
        functools.partial(final_kernel, n_tp, len(left)),
        [bf16((group, col_part))],
        [position, own] + left + right,
        limit=4 << 20,
        moved=2 * group * 8 * col_part,
    )
    return mixed


def by_slots(hidden_in, norm_gain, expert_ids, gate_weights, w_gate, w_up, w_down):
    n_ep = lax.axis_size("ep")
    tp_pos = lax.axis_index("tp")
    tok_dev, width = hidden_in.shape
    group, top = expert_ids.shape
    exp_loc, _, hid_part = w_gate.shape
    col_part = w_down.shape[2]
    experts = exp_loc * n_ep
    cap = max(2, 2 * top * group // experts)
    values = hidden_in.astype(jnp.float32)
    scale = lax.rsqrt(jnp.mean(values * values, axis=1, keepdims=True) + 1e-06)
    normed = (values * scale * norm_gain.astype(jnp.float32)).astype(jnp.bfloat16)
    flat_ids = expert_ids.reshape(-1)
    pairs = flat_ids.shape[0]
    hits = (flat_ids[:, None] == lax.broadcasted_iota(jnp.int32, (pairs, experts), 1)).astype(
        jnp.int32
    )
    before = jnp.cumsum(hits, axis=0) - hits
    position = jnp.sum(before * hits, axis=1)
    slot_index = flat_ids * cap + position
    places = lax.broadcasted_iota(jnp.int32, (experts * cap, group, top), 0)
    dispatch_map = jnp.any(places == slot_index.reshape(group, top)[None], axis=2).astype(
        jnp.bfloat16
    )
    whole_norm, whole_input = (
        lax.all_gather(normed, "tp", axis=0, tiled=True),
        lax.all_gather(hidden_in, "tp", axis=0, tiled=True),
    )
    residual = lax.dynamic_slice_in_dim(whole_input, tp_pos * col_part, col_part, 1)
    packed = jnp.dot(dispatch_map, whole_norm, preferred_element_type=jnp.float32).astype(
        jnp.bfloat16
    )
    packed = packed.reshape(n_ep, exp_loc, cap, width)
    arrived = lax.all_to_all(packed, "ep", split_axis=0, concat_axis=0, tiled=True)
    gate_act = jnp.einsum("secd,edh->sech", arrived, w_gate, preferred_element_type=jnp.float32)
    up_act = jnp.einsum("secd,edh->sech", arrived, w_up, preferred_element_type=jnp.float32)
    hidden = (jax.nn.silu(gate_act) * up_act).astype(jnp.bfloat16)
    outputs = jnp.einsum(
        "sech,ehf->secf",
        lax.all_gather(hidden, "tp", axis=3, tiled=True),
        w_down,
        preferred_element_type=jnp.float32,
    )
    returned = lax.all_to_all(
        outputs.astype(jnp.bfloat16), "ep", split_axis=0, concat_axis=0, tiled=True
    )
    flat_back = returned.reshape(experts * cap, col_part)
    picked = flat_back[slot_index].reshape(group, top, col_part).astype(jnp.float32)
    combined = jnp.sum(picked * gate_weights[:, :, None], axis=1)
    return (residual.astype(jnp.float32) + combined).astype(jnp.bfloat16)


def shards(hidden_in, norm_gain, expert_ids, gate_weights, w_gate, w_up, w_down):
    group, top = expert_ids.shape
    exp_loc = w_gate.shape[0]
    cap = max(2, 2 * top * group // (exp_loc * lax.axis_size("ep")))
    n_ep = lax.axis_size("ep")
    whole = exp_loc > 1 and exp_loc * cap >= group and n_ep > 4 and n_ep & (n_ep - 1) == 0
    plan = by_tokens if whole else by_slots
    return plan(hidden_in, norm_gain, expert_ids, gate_weights, w_gate, w_up, w_down)


def solution(mesh):
    in_specs = (
        P(("ep", "tp"), None),
        P(),
        P("ep", None),
        P("ep", None),
        P("ep", None, "tp"),
        P("ep", None, "tp"),
        P("ep", None, "tp"),
    )
    out_specs = P("ep", "tp")
    return jax.shard_map(shards, mesh=mesh, in_specs=in_specs, out_specs=out_specs, check_vma=False)
```

```python
import functools

import jax
import jax.numpy as jnp
from jax import lax
from jax.experimental import pallas as pl
from jax.experimental.pallas import tpu as pltpu
from jax.sharding import PartitionSpec as P

LANES = 128


def factors_of(n):
    digits, stride = [], 1
    for _ in range(2):
        if n % 2 == 0 and n > 1:
            digits.append((stride, 2))
            stride, n = stride * 2, n // 2
    while n > 1:
        radix = 4 if n % 4 == 0 else 2
        digits.append((stride, radix))
        stride, n = stride * radix, n // radix
    return digits


def traded(x, axis, size, stride, radix, by):
    pairs = []
    for i in range(size):
        digit = i // stride % radix
        pairs.append((i, i + ((digit ^ by) - digit) * stride))
    return lax.ppermute(x, axis, pairs)


def trades(blocks, axis, size, stride, radix):
    came = {s: traded(blocks[s], axis, size, stride, radix, s) for s in reversed(range(1, radix))}
    return [blocks[0]] + [came[s] for s in range(1, radix)]


def arrivals(x, axis, size, stride, radix):
    return trades([x] * radix, axis, size, stride, radix)


def pack_kernel(top, pos_ref, ids_ref, weights_ref, values_ref, message_ref, ids, weights, sems):
    tok_dev, width = values_ref.shape
    copies = [
        pltpu.make_async_copy(ids_ref, ids, sems.at[0]),
        pltpu.make_async_copy(weights_ref, weights, sems.at[1]),
        pltpu.make_async_copy(values_ref, message_ref.at[:, pl.ds(0, width)], sems.at[2]),
    ]
    for copy in copies:
        copy.start()
    copies[0].wait()
    copies[1].wait()
    group = ids.shape[1]
    high = weights[...].astype(jnp.bfloat16).astype(jnp.float32)
    rest = weights[...] - high
    mid = rest.astype(jnp.bfloat16).astype(jnp.float32)
    terms = [ids[...].astype(jnp.float32), high, mid, rest - mid]
    terms.append(jnp.zeros((LANES - 4 * top, group), jnp.float32))
    table = jnp.concatenate(terms, axis=0).astype(jnp.bfloat16)
    own = lax.broadcasted_iota(jnp.int32, (tok_dev, group), 0) + pos_ref[0] * tok_dev
    own = (own == lax.broadcasted_iota(jnp.int32, (tok_dev, group), 1)).astype(jnp.float32)
    routing = lax.dot_general(
        own.astype(jnp.bfloat16), table, (((1,), (1,)), ((), ())), preferred_element_type=jnp.float32
    )
    message_ref[:, width:] = routing.astype(jnp.bfloat16)
    copies[2].wait()


def split_kernel(half, *refs):
    pieces, (first_ref, second_ref, token_ref) = refs[:-3], refs[-3:]
    pieces = [ref for ref in pieces if ref.shape[1] > 2 * half]
    whole = jnp.concatenate([ref[...].astype(jnp.float32) for ref in pieces], axis=0).astype(jnp.bfloat16)
    second_ref[...] = whole[:, :half]
    first_ref[...] = whole[:, half:]
    token_ref[...] = jnp.zeros_like(token_ref)


def join_kernel(count, signs, *refs):
    out_ref = refs[count + signs]
    rows = refs[0].shape[0]
    for i, ref in enumerate(refs[:count]):
        out_ref[i * rows : (i + 1) * rows] = ref[...]
    for ref in refs[count + signs + 1 :]:
        ref[...] = jnp.zeros_like(ref)


def load_kernel(experts, signs, *refs):
    count = len(experts)
    refs = refs[:count] + refs[count + signs :]
    far, (sign_ref, *near, sems) = refs[:count], refs[count:]
    copies = load_copies(far, near, sems, experts)
    sign_ref[...] = jnp.zeros_like(sign_ref)
    for copy in copies:
        copy.wait()


def load_copies(far, near, sems, experts):
    copies = []
    for i, (src_ref, dst_ref, expert) in enumerate(zip(far, near, experts)):
        runs = sems.shape[1]
        size = dst_ref.shape[0] // runs
        for r in range(runs):
            at = pl.ds(r * size, size)
            copies.append(pltpu.make_async_copy(src_ref.at[expert, at], dst_ref.at[at], sems.at[i, r]))
    for copy in copies:
        copy.start()
    return copies


def swiglu(normed_ref, gates, ups, hidden_ref, start):
    for i, (gate_ref, up_ref) in enumerate(zip(gates, ups)):
        x = normed_ref[start + i]
        gate_act = jnp.dot(x, gate_ref[...], preferred_element_type=jnp.float32)
        up_act = jnp.dot(x, up_ref[...], preferred_element_type=jnp.float32)
        hidden_ref[i] = (gate_act / (1.0 + jnp.exp(-gate_act)) * up_act).astype(jnp.bfloat16)


def select_body(dims, pos_ref, gain_ref, first, second, gates, ups, hidden_ref, normed_ref, mix_ref, turned_ref):
    n_fast, n_mid, n_tp, slow_n, tok_dev, top, exp_loc, rows, half = dims
    tp_pos, base = pos_ref[0], pos_ref[1]
    run = slow_n * tok_dev
    tokens = n_fast * n_mid * n_tp * run
    routing = jnp.concatenate([ref[:, half:] for ref in first], axis=0).astype(jnp.float32)
    ids = routing[:, :top]
    weights = routing[:, top : 2 * top] + (
        routing[:, 2 * top : 3 * top] + routing[:, 3 * top : 4 * top]
    )

    def number(shape, dim):
        at = lax.broadcasted_iota(jnp.int32, shape, dim)
        tp_at = lax.rem(lax.div(at, n_mid * run), n_tp)
        return at + (lax.rem(tp_pos - tp_at + n_tp, n_tp) - tp_at) * (n_mid * run)

    before = number((tokens, tokens), 1) < number((tokens, tokens), 0)
    match = [ids == (base + e).astype(jnp.float32) for e in range(exp_loc)]
    hits = [jnp.sum(m.astype(jnp.float32), axis=1, keepdims=True) for m in match]
    shares = [jnp.sum(jnp.where(m, weights, 0.0), axis=1, keepdims=True) for m in match]
    lane = lax.broadcasted_iota(jnp.int32, (tokens, LANES), 1)
    hit = functools.reduce(
        lambda a, e: jnp.where(lane == e, hits[e], a),
        range(exp_loc),
        jnp.zeros((tokens, LANES), jnp.float32),
    )
    position = jnp.dot(
        before.astype(jnp.float32).astype(jnp.bfloat16),
        hit.astype(jnp.bfloat16),
        preferred_element_type=jnp.float32,
    )
    slot = lax.broadcasted_iota(jnp.int32, (tokens, rows), 1).astype(jnp.float32)
    picks, spreads = [], []
    for e in range(exp_loc):
        place = jnp.where(hits[e] > 0, position[:, e : e + 1], -1.0)
        pick = slot == place
        picks.append(pick.astype(jnp.float32))
        spreads.append(jnp.where(pick, shares[e], 0.0))
    spread = jnp.concatenate(spreads, axis=1)
    group = lambda f, m, s: [
        spread[start : start + tok_dev]
        for start in [(((f * n_tp + t) * n_mid + m) * slow_n + s) * tok_dev for t in range(n_tp)]
    ]
    blocks = [b for f in range(n_fast) for m in range(n_mid) for s in range(slow_n) for b in group(f, m, s)]
    turned = [b for f in range(n_fast) for s in range(slow_n) for m in range(n_mid) for b in group(f, m, s)]
    for ref, rows_of in ((mix_ref, blocks), (turned_ref, turned)):
        exact = jnp.concatenate(rows_of, axis=0)
        high = exact.astype(jnp.bfloat16)
        ref[0] = high
        ref[1] = (exact - high.astype(jnp.float32)).astype(jnp.bfloat16)

    part = n_mid * n_tp * run
    pick = jnp.concatenate(picks, axis=1)
    swapped = jnp.concatenate(
        [
            pick[f * part + (t * n_mid + m) * run : f * part + (t * n_mid + m + 1) * run]
            for f in range(n_fast)
            for m in range(n_mid)
            for t in range(n_tp)
        ],
        axis=0,
    )
    chosen, swapped = pick.T.astype(jnp.bfloat16), swapped.T.astype(jnp.bfloat16)
    size = min(half, 4 * LANES)
    squares = 0.0
    for begin in range(0, 2 * half, size):
        table, side, at = (swapped, second, begin) if begin < half else (chosen, first, begin - half)
        values = jnp.concatenate([ref[:, at : at + size] for ref in side], axis=0)
        values = jnp.dot(table, values, preferred_element_type=jnp.float32)
        squares = squares + jnp.sum(values * values, axis=1, keepdims=True)
        values = values.astype(jnp.bfloat16)
        for e in range(exp_loc):
            normed_ref[e, :, begin : begin + size] = values[e * rows : (e + 1) * rows]
    scale = lax.rsqrt(squares / (2 * half) + 1e-06)
    gain_all = gain_ref[...].astype(jnp.float32)
    for begin in range(0, 2 * half, size):
        gain = [gain_all[r : r + 1] for r in range(begin // LANES, (begin + size) // LANES)]
        gain = jnp.concatenate(gain, axis=1)
        for e in range(exp_loc):
            values = normed_ref[e, :, begin : begin + size].astype(jnp.float32)
            values = values * scale[e * rows : (e + 1) * rows] * gain
            normed_ref[e, :, begin : begin + size] = values.astype(jnp.bfloat16)
    swiglu(normed_ref, gates, ups, hidden_ref, 0)


def select_kernel(dims, lead, tail, pos_ref, gain_ref, *refs):
    n_fast = dims[0]
    first, second, refs = refs[:n_fast], refs[n_fast : 2 * n_fast], refs[2 * n_fast :]
    gates, ups, refs = refs[:lead], refs[lead : 2 * lead], refs[2 * lead :]
    gate_far, up_far, hidden_ref, normed_ref, mix_ref, turned_ref, *near, sems = refs
    wanted = [(gate_far, lead + tail - 1)] + [(up_far, e) for e in range(lead, lead + tail)]
    copies = load_copies([ref for ref, _ in wanted], near, sems, [e for _, e in wanted])

    @pl.when(pos_ref[0] >= 0)
    def _():
        select_body(dims, pos_ref, gain_ref, first, second, gates, ups, hidden_ref, normed_ref, mix_ref, turned_ref)

    for copy in copies:
        copy.wait()


def up_kernel(start, count, wanted, pos_ref, normed_ref, *refs):
    gates, ups, (far_ref, hidden_ref, *near, sems) = refs[:count], refs[count : 2 * count], refs[2 * count :]
    copies = load_copies([far_ref] * len(near), near, sems, wanted)

    @pl.when(pos_ref[0] >= 0)
    def _():
        swiglu(normed_ref, gates, ups, hidden_ref, start)

    for copy in copies:
        copy.wait()


def lower(tp_pos, n_tp, piece, s, down_ref, columns):
    hid_part = piece.shape[1]
    begin = pl.multiple_of(lax.rem(tp_pos - s + n_tp, n_tp) * hid_part, hid_part)
    return jnp.dot(piece, down_ref[pl.ds(begin, hid_part), columns], preferred_element_type=jnp.float32)


def down_kernel(n_tp, count, pos_ref, own_ref, *refs):
    pieces, (*downs, out_ref, part_ref) = refs[:n_tp], refs[n_tp:]
    _, rows, _ = own_ref.shape
    every = slice(None)
    for i, ref in enumerate(downs[:count]):
        total = sum(lower(pos_ref[0], n_tp, pieces[s][i], s, ref, every) for s in range(n_tp))
        out_ref[i * rows : (i + 1) * rows] = total.astype(jnp.bfloat16)
    for i, ref in enumerate(downs[count:]):
        part_ref[i * rows : (i + 1) * rows] = lower(pos_ref[0], n_tp, own_ref[i], 0, ref, every)


def in_blocks(total, refs):
    rows = refs[0].shape[0]
    for i, ref in enumerate(refs):
        ref[...] = total[i * rows : (i + 1) * rows].astype(jnp.bfloat16)


def mix_kernel(n_tp, count, begin, pos_ref, mix_ref, done_ref, part_ref, *refs):
    pieces, refs = refs[: n_tp - 1], refs[n_tp - 1 :]
    downs, (*partial_refs, out_ref) = refs[:count], refs[count:]
    columns = pl.ds(begin, out_ref.shape[1])
    at = done_ref.shape[0]
    rows = part_ref.shape[0] // count
    out_ref[:at] = done_ref[:, columns]
    for i, ref in enumerate(downs):
        total = part_ref[i * rows : (i + 1) * rows, columns]
        for s in range(1, n_tp):
            total = total + lower(pos_ref[0], n_tp, pieces[s - 1][i], s, ref, columns)
        out_ref[at + i * rows : at + (i + 1) * rows] = total.astype(jnp.bfloat16)
    out = out_ref[...]
    partial = jnp.dot(mix_ref[0], out, preferred_element_type=jnp.float32)
    partial = partial + jnp.dot(mix_ref[1], out, preferred_element_type=jnp.float32)
    in_blocks(partial, partial_refs)


def total_of(refs):
    return functools.reduce(lambda a, ref: a + ref[...].astype(jnp.float32), refs[1:], refs[0][...].astype(jnp.float32))


def sum_kernel(count, signs, blocks, *refs):
    out_refs = refs[count + signs :]
    in_blocks(total_of(refs[:count]), out_refs[:blocks])
    for ref in out_refs[blocks:]:
        ref[...] = jnp.zeros_like(ref)


def own_kernel(dims, pos_ref, first_ref, second_ref, _, out_ref, own_ref):
    n_mid, n_tp, slow_n, tok_dev, half = dims
    col_part = out_ref.shape[1]
    for s in range(n_tp):
        at = s * n_mid * slow_n * tok_dev
        own_ref[s * tok_dev : (s + 1) * tok_dev, half:] = first_ref[at : at + tok_dev, :half].astype(jnp.float32)
        at = s * slow_n * tok_dev
        own_ref[s * tok_dev : (s + 1) * tok_dev, :half] = second_ref[at : at + tok_dev].astype(jnp.float32)
    out_ref[...] = own_ref[:, pl.ds(pl.multiple_of(pos_ref[0] * col_part, col_part), col_part)]


def final_kernel(n_tp, count, pos_ref, own_ref, *refs):
    left, right, out_ref = refs[:count], refs[count:-1], refs[-1]
    begin, tok_dev = 0, own_ref.shape[0] // n_tp
    for side in (left, right):
        columns = pl.ds(begin, side[0].shape[1])
        total = total_of(side) + own_ref[:, columns]
        rows = []
        for j in range(n_tp):
            row = total[:tok_dev]
            for s in range(1, n_tp):
                here = lax.rem(pos_ref[0] - s + n_tp, n_tp) == j
                row = jnp.where(here, total[s * tok_dev : (s + 1) * tok_dev], row)
            rows.append(row)
        out_ref[:, columns] = jnp.concatenate(rows, axis=0).astype(jnp.bfloat16)
        begin += side[0].shape[1]


VMEM = pl.BlockSpec(memory_space=pltpu.VMEM)
SMEM = pl.BlockSpec(memory_space=pltpu.SMEM)
HBM = pl.BlockSpec(memory_space=pltpu.HBM)
KEPT = pltpu.VMEM
TOKEN = jax.ShapeDtypeStruct((8, LANES), jnp.float32)


def local_call(kernel, shapes, operands, far=(), scratch=(), limit=6 << 20, flops=0, moved=0):
    specs, given = [], []
    for i, a in enumerate(operands):
        if i in far:
            specs.append(HBM)
            given.append(pltpu.with_memory_space_constraint(a, pltpu.HBM))
        else:
            specs.append(SMEM if a.dtype == jnp.int32 else VMEM)
            given.append(a)
    return pl.pallas_call(
        kernel,
        out_shape=shapes,
        in_specs=specs,
        out_specs=[VMEM] * len(shapes),
        scratch_shapes=list(scratch),
        compiler_params=pltpu.CompilerParams(vmem_limit_bytes=limit),
        cost_estimate=pl.CostEstimate(flops=flops, bytes_accessed=moved, transcendentals=0),
    )(*given)


def kept(array, count):
    return [KEPT(array.shape[1:], array.dtype)] * count


def runs_of(array):
    return 4 if array.shape[1] % 64 == 0 else 1


def loaded(wanted, after):
    sign, *near = local_call(
        functools.partial(load_kernel, [expert for _, expert in wanted], len(after)),
        [TOKEN] + [KEPT(array.shape[1:], array.dtype) for array, _ in wanted],
        [array for array, _ in wanted] + after,
        far=range(len(wanted)),
        scratch=[pltpu.SemaphoreType.DMA((len(wanted), min(runs_of(array) for array, _ in wanted)))],
        limit=1 << 20,
        moved=2 * sum(array.size // array.shape[0] for array, _ in wanted),
    )
    return near, sign


def summed(pieces, blocks, after, signed):
    rows, columns = pieces[0].shape
    return local_call(
        functools.partial(sum_kernel, len(pieces), len(after), blocks),
        [jax.ShapeDtypeStruct((rows // blocks, columns), pieces[0].dtype)] * blocks + [TOKEN] * signed,
        list(pieces) + after,
        limit=4 << 20,
        moved=2 * (len(pieces) + 1) * rows * columns,
    )


def joined(pieces, after, signed):
    rows, columns = pieces[0].shape
    return local_call(
        functools.partial(join_kernel, len(pieces), len(after)),
        [jax.ShapeDtypeStruct((len(pieces) * rows, columns), pieces[0].dtype)] + [TOKEN] * signed,
        list(pieces) + after,
        limit=4 << 20,
        moved=4 * len(pieces) * rows * columns,
    )


def by_tokens(hidden_in, norm_gain, expert_ids, gate_weights, w_gate, w_up, w_down):
    n_ep = lax.axis_size("ep")
    n_tp = lax.axis_size("tp")
    ep_pos = lax.axis_index("ep")
    tp_pos = lax.axis_index("tp")
    tok_dev, width = hidden_in.shape
    group, top = expert_ids.shape
    exp_loc, _, hid_part = w_gate.shape
    col_part = w_down.shape[2]
    experts = exp_loc * n_ep
    cap = max(2, 2 * top * group // experts)
    rows = cap * n_ep
    tokens = group * n_ep
    digits = factors_of(n_ep)
    fast, mid, slow = digits[0], digits[1:2], digits[2:]
    half = width // 2
    slow_n = n_ep
    for _, radix in [fast] + mid:
        slow_n //= radix
    n_fast, n_mid = fast[1], mid[0][1] if mid else 1

    bf16 = functools.partial(jax.ShapeDtypeStruct, dtype=jnp.bfloat16)
    slots = exp_loc * rows
    lead = exp_loc - exp_loc // 2
    tail = exp_loc - lead
    gain = norm_gain.reshape(width // LANES, LANES)
    position = jnp.stack([tp_pos, ep_pos * exp_loc])
    (message,) = local_call(
        functools.partial(pack_kernel, top),
        [bf16((tok_dev, width + LANES))],
        [position, expert_ids.T, gate_weights.T, hidden_in],
        far=[1, 2, 3],
        scratch=[
            pltpu.VMEM((top, group), jnp.int32),
            pltpu.VMEM((top, group), jnp.float32),
            pltpu.SemaphoreType.DMA((3,)),
        ],
        limit=4 << 20,
    )
    around = [message]
    for digit in reversed(slow):
        around = [a for piece in around for a in arrivals(piece, "ep", n_ep, *digit)]
    loads, sign = loaded([(w_gate, e) for e in range(lead)] + [(w_up, 0)], [])
    gate_lead, up_lead = loads[:lead], loads[lead:]
    first, second, sign = local_call(
        functools.partial(split_kernel, half),
        [bf16((slow_n * tok_dev, width + LANES - half)), bf16((slow_n * tok_dev, half)), TOKEN],
        around + [sign],
        limit=4 << 20,
    )
    gate_tail, sign = loaded([(w_gate, e) for e in range(lead, exp_loc - 1)], [sign]) if tail > 1 else ([], sign)
    along_tp = lambda a: arrivals(a, "tp", n_tp, 1, n_tp)
    along_mid = lambda a: arrivals(a, "ep", n_ep, *mid[0]) if mid else [a]
    first, second = along_mid(first), along_tp(second)
    first, sign = joined(first, [sign], 1)
    (second,) = joined(second, [], 0)
    loads, sign = loaded([(w_up, e) for e in range(1, lead)] + [(w_down, e) for e in range(lead)], [sign])
    up_lead, down_lead = up_lead + loads[: lead - 1], loads[lead - 1 :]
    first, second = along_tp(first), along_mid(second)
    (first,) = joined(first, [sign], 0)
    (second,) = joined(second, [], 0)
    first = arrivals(first, "ep", n_ep, *fast)
    second = arrivals(second, "ep", n_ep, *fast)

    dims = (n_fast, n_mid, n_tp, slow_n, tok_dev, top, exp_loc, rows, half)
    sems = lambda array, count: pltpu.SemaphoreType.DMA((count, runs_of(array)))
    operands = [position, gain] + first + second + gate_lead + up_lead + [w_gate, w_up]
    hidden, normed, mix, turned, gate_last, *up_tail = local_call(
        functools.partial(select_kernel, dims, lead, tail),
        [
            bf16((lead, rows, hid_part)),
            bf16((exp_loc, rows, width)),
            bf16((2, tokens, slots)),
            bf16((2, tokens, slots)),
        ]
        + kept(w_gate, 1)
        + kept(w_up, tail),
        operands,
        far=[len(operands) - 2, len(operands) - 1],
        scratch=[sems(w_up, 1 + tail)],
        flops=2 * slots * tokens * width + 4 * lead * rows * width * hid_part,
        moved=4 * lead * width * hid_part,
    )
    pieces = along_tp(hidden)
    operands = [position, normed] + gate_tail + [gate_last] + up_tail + [w_down]
    hidden, *down_tail = local_call(
        functools.partial(up_kernel, lead, tail, range(lead, exp_loc)),
        [bf16((tail, rows, hid_part))] + kept(w_down, tail),
        operands,
        far=[len(operands) - 1],
        scratch=[sems(w_down, tail)],
        flops=4 * tail * rows * width * hid_part,
        moved=4 * tail * width * hid_part,
    )
    late = along_tp(hidden)
    done, part = local_call(
        functools.partial(down_kernel, n_tp, lead),
        [bf16((lead * rows, col_part)), jax.ShapeDtypeStruct((tail * rows, col_part), jnp.float32)],
        [position, late[0]] + pieces + down_lead + down_tail,
        flops=2 * lead * rows * n_tp * hid_part * col_part,
        moved=2 * lead * n_tp * hid_part * col_part,
    )
    left_cols = col_part * 5 // 8 // LANES * LANES
    right_cols = col_part - left_cols
    mixed_of = lambda table, begin, size: local_call(
        functools.partial(mix_kernel, n_tp, tail, begin),
        [bf16((tokens // n_fast, size))] * n_fast,
        [position, table, done, part] + late[1:] + down_tail,
        scratch=[pltpu.VMEM((slots, size), jnp.bfloat16)],
        flops=2 * slots * n_tp * hid_part * size,
        moved=2 * tail * n_tp * hid_part * size,
    )

    def swapped(blocks, digit):
        own, *others = trades(blocks, "ep", n_ep, *digit)
        return [own] + others

    slow = list(reversed(slow))
    right_way, left_way = slow + mid, mid + slow
    right = summed(swapped(mixed_of(turned, left_cols, right_cols), fast), right_way[0][1], [], 0)
    left = summed(swapped(mixed_of(mix, 0, left_cols), fast), left_way[0][1], [], 0)
    signs = []
    for digit, later in zip(left_way[:-1], left_way[1:]):
        *left, late_sign = summed(swapped(left, digit), later[1], [], 1)
        signs.append(late_sign)
    for digit, later in zip(right_way[:-1], right_way[1:]):
        right = summed(swapped(right, digit), later[1], signs, 0)
        signs = []
    left = swapped(left, left_way[-1])
    right = swapped(right, right_way[-1])
    (own,) = local_call(
        functools.partial(own_kernel, (n_mid, n_tp, slow_n, tok_dev, half)),
        [jax.ShapeDtypeStruct((group, col_part), jnp.float32)],
        [position, first[0], second[0], late_sign],
        scratch=[pltpu.VMEM((group, width), jnp.float32)],
        limit=4 << 20,
        moved=4 * group * width,
    )
    (mixed,) = local_call(
        functools.partial(final_kernel, n_tp, len(left)),
        [bf16((group, col_part))],
        [position, own] + left + right,
        limit=4 << 20,
        moved=2 * group * 8 * col_part,
    )
    return mixed


def by_slots(hidden_in, norm_gain, expert_ids, gate_weights, w_gate, w_up, w_down):
    n_ep = lax.axis_size("ep")
    tp_pos = lax.axis_index("tp")
    tok_dev, width = hidden_in.shape
    group, top = expert_ids.shape
    exp_loc, _, hid_part = w_gate.shape
    col_part = w_down.shape[2]
    experts = exp_loc * n_ep
    cap = max(2, 2 * top * group // experts)
    values = hidden_in.astype(jnp.float32)
    scale = lax.rsqrt(jnp.mean(values * values, axis=1, keepdims=True) + 1e-06)
    normed = (values * scale * norm_gain.astype(jnp.float32)).astype(jnp.bfloat16)
    flat_ids = expert_ids.reshape(-1)
    pairs = flat_ids.shape[0]
    hits = (flat_ids[:, None] == lax.broadcasted_iota(jnp.int32, (pairs, experts), 1)).astype(
        jnp.int32
    )
    before = jnp.cumsum(hits, axis=0) - hits
    position = jnp.sum(before * hits, axis=1)
    slot_index = flat_ids * cap + position
    places = lax.broadcasted_iota(jnp.int32, (experts * cap, group, top), 0)
    dispatch_map = jnp.any(places == slot_index.reshape(group, top)[None], axis=2).astype(
        jnp.bfloat16
    )
    whole_norm, whole_input = (
        lax.all_gather(normed, "tp", axis=0, tiled=True),
        lax.all_gather(hidden_in, "tp", axis=0, tiled=True),
    )
    residual = lax.dynamic_slice_in_dim(whole_input, tp_pos * col_part, col_part, 1)
    packed = jnp.dot(dispatch_map, whole_norm, preferred_element_type=jnp.float32).astype(
        jnp.bfloat16
    )
    packed = packed.reshape(n_ep, exp_loc, cap, width)
    arrived = lax.all_to_all(packed, "ep", split_axis=0, concat_axis=0, tiled=True)
    gate_act = jnp.einsum("secd,edh->sech", arrived, w_gate, preferred_element_type=jnp.float32)
    up_act = jnp.einsum("secd,edh->sech", arrived, w_up, preferred_element_type=jnp.float32)
    hidden = (jax.nn.silu(gate_act) * up_act).astype(jnp.bfloat16)
    outputs = jnp.einsum(
        "sech,ehf->secf",
        lax.all_gather(hidden, "tp", axis=3, tiled=True),
        w_down,
        preferred_element_type=jnp.float32,
    )
    returned = lax.all_to_all(
        outputs.astype(jnp.bfloat16), "ep", split_axis=0, concat_axis=0, tiled=True
    )
    flat_back = returned.reshape(experts * cap, col_part)
    picked = flat_back[slot_index].reshape(group, top, col_part).astype(jnp.float32)
    combined = jnp.sum(picked * gate_weights[:, :, None], axis=1)
    return (residual.astype(jnp.float32) + combined).astype(jnp.bfloat16)


def shards(hidden_in, norm_gain, expert_ids, gate_weights, w_gate, w_up, w_down):
    group, top = expert_ids.shape
    exp_loc = w_gate.shape[0]
    cap = max(2, 2 * top * group // (exp_loc * lax.axis_size("ep")))
    n_ep = lax.axis_size("ep")
    whole = exp_loc > 1 and exp_loc * cap >= group and n_ep > 4 and n_ep & (n_ep - 1) == 0
    plan = by_tokens if whole else by_slots
    return plan(hidden_in, norm_gain, expert_ids, gate_weights, w_gate, w_up, w_down)


def solution(mesh):
    in_specs = (
        P(("ep", "tp"), None),
        P(),
        P("ep", None),
        P("ep", None),
        P("ep", None, "tp"),
        P("ep", None, "tp"),
        P("ep", None, "tp"),
    )
    out_specs = P("ep", "tp")
    return jax.shard_map(shards, mesh=mesh, in_specs=in_specs, out_specs=out_specs, check_vma=False)
```
